512 devices in a mesh: batch: 128 (over y, x, z_hi), rep: 4 (over z_lo, core).
Axes of the slice: x: 4, y: 8, z: 8 (z_hi: 4, z_lo: 2; z = z_hi * 2 + z_lo), core: 2. Of those that a mesh axis runs over, the one named last changes fastest.
Arguments:
- img_feat: bfloat16 [16384, 1152], P('batch'), may hold values from -48 to 48
- head_weight: bfloat16 [1152, 1152], replicated, may hold values from -1 to 3
- text_embed: bfloat16 [16384, 1152], P(('batch', 'rep')), may hold values from -48 to 48
- log_temp: float32 [1], replicated, may hold values from 3.5 to 4.7
- logit_bias: float32 [1], replicated, may hold values from -14 to -6
Outputs:
- loss: float32 [1], replicated
- feat_grad: bfloat16 [16384, 1152], P('batch')
- head_grad: bfloat16 [1152, 1152], P(None, 'rep')
The draws below stay inside these ranges and needn't reach their ends.
All inputs are finite; a program needn't handle non-finite values.
Results may differ from the reference program's by a relative error of at most 0.0058.
Values may be sent and summed in bfloat16 or wider, within the bound.
No kernel may reach another device: no remote copies, remote signals or barrier semaphores. Data moves between devices by JAX's collectives and lax.ppermute only.
A program may use at most 64 MiB of HBM per device.

```python
import jax
import jax.numpy as jnp
from jax import lax

E = 1152
D = 1152
ROWS = 128
GROUP = 16384
N_BATCH = 128


def pair_common(key):
    label_key, centre_key, mixing_key, paired_key = jax.random.split(key, 4)
    groups = max(GROUP // 8, 1)
    labels = jax.random.randint(label_key, (GROUP,), 0, groups)
    centres = jax.random.normal(centre_key, (groups, E), jnp.float32)
    position = lax.broadcasted_iota(jnp.float32, (GROUP, 1), 0) / GROUP
    mixing = jax.random.uniform(mixing_key, (GROUP, 1), jnp.float32, 0.3, 1.0) * (0.5 + position)
    paired = jax.random.normal(paired_key, (GROUP, E), jnp.float32)
    return jnp.take(centres, labels, axis=0) * mixing + 0.9 * paired


def finish_rows(common, random_part):
    values = common + 0.6 * random_part
    return jnp.clip(values, -48.0, 48.0).astype(jnp.bfloat16)


def draw_img_feat(key, part):
    common = pair_common(key)
    key = jax.random.fold_in(key, 11)
    random_key = jax.random.fold_in(key, 0)
    random_part = jax.random.normal(random_key, (GROUP, D), jnp.float32)
    return finish_rows(common, random_part)


def draw_text_embed(key, part):
    common = pair_common(key)
    key = jax.random.fold_in(key, 13)
    random_key = jax.random.fold_in(key, 0)
    random_part = jax.random.normal(random_key, (GROUP, E), jnp.float32)
    return finish_rows(common, random_part)


def draw_head_weight(key, part):
    key = jax.random.fold_in(key, 17)
    rows_at = lax.broadcasted_iota(jnp.int32, (D, E), 0)
    cols_at = lax.broadcasted_iota(jnp.int32, (D, E), 1)
    diagonal_part = jnp.where(rows_at == cols_at, 2.0, 0.0).astype(jnp.float32)
    random_part = jax.random.normal(key, (D, E), jnp.float32)
    values = diagonal_part + random_part * D ** (-0.5)
    return jnp.clip(values, -1.0, 3.0).astype(jnp.bfloat16)


def setup_inputs(seed: int = 0) -> dict:
    streams_of = jax.random.split(jax.random.key(seed), 6)
    return {
        "img_feat": draw_img_feat(jax.random.fold_in(streams_of[5], 71), 0),
        "head_weight": draw_head_weight(jax.random.fold_in(streams_of[5], 71), 0),
        "text_embed": draw_text_embed(jax.random.fold_in(streams_of[5], 71), 0),
        "log_temp": jnp.clip(jax.random.uniform(streams_of[3], (1,), jnp.float32, 3.5, 4.7), 3.5, 4.7),
        "logit_bias": jnp.clip(jax.random.uniform(streams_of[4], (1,), jnp.float32, -14.0, -6.0), -14.0, -6.0),
    }


EPS = 1e-06

def normalize(values):
    inverse = lax.rsqrt(lax.optimization_barrier(jnp.sum(values * values, axis=-1, keepdims=True)) + EPS)
    return (values * inverse, inverse)

def back_norm(direction, unit, inverse):
    return (direction - unit * lax.optimization_barrier(jnp.sum(unit * direction, axis=-1, keepdims=True))) * inverse

def reference(img_feat, head_weight, text_embed, log_temp, logit_bias):
    scale = jnp.exp(log_temp[0])
    shift = logit_bias[0]
    image_head = jnp.dot(img_feat, head_weight, preferred_element_type=jnp.float32)
    image_unit, image_inv = normalize(image_head)
    image_low = image_unit.astype(jnp.bfloat16)
    text_unit, text_inv = normalize(text_embed.astype(jnp.float32))
    text_low = text_unit.astype(jnp.bfloat16)
    columns = jnp.arange(GROUP, dtype=jnp.int32)[None, :]

    def one_block(start):
        block_low = lax.dynamic_slice_in_dim(image_low, start, ROWS, 0)
        logits = scale * jnp.dot(block_low, text_low.T, preferred_element_type=jnp.float32) + shift
        rows_index = start + jnp.arange(ROWS, dtype=jnp.int32)[:, None]
        label = jnp.where(rows_index == columns, 1.0, -1.0).astype(jnp.float32)
        block_loss = jnp.sum(-jax.nn.log_sigmoid(label * logits))
        slope = (-label * jax.nn.sigmoid(-label * logits)).astype(jnp.bfloat16)
        direction = scale * jnp.dot(slope, text_low, preferred_element_type=jnp.float32)
        return (direction, block_loss)
    starts = jnp.arange(N_BATCH, dtype=jnp.int32) * ROWS
    blocks, losses = lax.map(one_block, starts)
    image_dir = blocks.reshape(GROUP, E)
    image_back = back_norm(image_dir, image_unit, image_inv).astype(jnp.bfloat16)
    feat_grad = jnp.dot(image_back, head_weight.T, preferred_element_type=jnp.float32).astype(jnp.bfloat16)
    head_grad = jnp.dot(img_feat.T, image_back, preferred_element_type=jnp.float32).astype(jnp.bfloat16)
    loss = (jnp.sum(losses) / (GROUP * GROUP)).reshape(1)
    return (loss, feat_grad, head_grad)
```

```python
import jax
import jax.numpy as jnp
from jax import lax
from jax.sharding import Mesh
from jax.sharding import PartitionSpec as P

EPS = 1e-06
BF16 = jnp.bfloat16
F32 = jnp.float32


def normalize(values):
    inverse = lax.rsqrt(jnp.sum(values * values, axis=-1, keepdims=True) + EPS)
    return (values * inverse, inverse)


def back_norm(direction, unit, inverse):
    return (direction - unit * jnp.sum(unit * direction, axis=-1, keepdims=True)) * inverse


def spread(block, axes):
    n = lax.axis_size(axes)
    copies = jnp.broadcast_to(block[None], (n,) + block.shape).reshape((n * block.shape[0],) + block.shape[1:])
    return lax.all_to_all(copies, axes, 0, 0, tiled=True)


def split3(value):
    hi = value.astype(BF16)
    rest = value - hi.astype(F32)
    mid = rest.astype(BF16)
    low = (rest - mid.astype(F32)).astype(BF16)
    return (hi, mid, low)


def local(img_feat, head_weight, text_embed, log_temp, logit_bias):
    rows, width = img_feat.shape
    quarter = text_embed.shape[0]
    ny, nx, nzh, nzl, nc = (lax.axis_size(a) for a in ("y", "x", "zh", "zl", "c"))
    nrep = nzl * nc
    y_at, x_at, zh_at, zl_at, c_at = (lax.axis_index(a) for a in ("y", "x", "zh", "zl", "c"))
    rep_at = zl_at * nc + c_at
    scale = jnp.exp(log_temp[0])
    shift = logit_bias[0]

    text_unit, _ = normalize(text_embed.astype(F32))
    text_low = text_unit.astype(BF16)

    image_head = jnp.dot(img_feat, head_weight, preferred_element_type=F32)
    image_unit, image_inv = normalize(image_head)
    image_low = image_unit.astype(BF16)
    images = lax.all_gather(image_low, "zh", axis=0)
    images = images.reshape(nzh, nzl, nc, quarter, width).transpose(2, 0, 1, 3, 4)
    images = images.reshape(nzh * rows, width)

    texts = spread(text_low, "y")
    texts = spread(texts, "x")

    logits = (
        scale * lax.dot_general(images, texts, (((1,), (1,)), ((), ())), preferred_element_type=F32)
        + shift
    )
    row = jnp.arange(nzh * rows, dtype=jnp.int32)[:, None]
    col = jnp.arange(nx * ny * quarter, dtype=jnp.int32)[None, :]
    own_row = c_at * (nzh * nzl * quarter) + (zh_at * nzl + zl_at) * quarter
    own_col = (x_at * ny + y_at) * quarter
    own = (row - own_row == col - own_col) & (row >= own_row) & (row < own_row + quarter)
    label = jnp.where(own, 1.0, -1.0).astype(F32)
    partial_loss = jnp.sum(-jax.nn.log_sigmoid(label * logits))
    slope = (-label * jax.nn.sigmoid(-label * logits)).astype(BF16)
    partial_dir = scale * jnp.dot(slope, texts, preferred_element_type=F32)

    half = nzh * nzl * quarter
    mine = lax.dynamic_slice_in_dim(partial_dir, c_at * half, half, 0)
    other = lax.dynamic_slice_in_dim(partial_dir, (1 - c_at) * half, half, 0).astype(BF16)
    other = lax.ppermute(other, "c", [(0, 1), (1, 0)])
    both = (mine + other.astype(F32)).astype(BF16)
    parts = lax.all_to_all(both, ("zh", "zl"), 0, 0, tiled=True)
    image_dir = jnp.sum(parts.reshape(nzh * nzl, quarter, width).astype(F32), axis=0)

    own_unit = lax.dynamic_slice_in_dim(image_unit, rep_at * quarter, quarter, 0)
    own_inv = lax.dynamic_slice_in_dim(image_inv, rep_at * quarter, quarter, 0)
    own_back = back_norm(image_dir, own_unit, own_inv).astype(BF16)
    loss_terms = jnp.concatenate([jnp.full((1, 1), t, BF16) for t in split3(partial_loss)], axis=1)
    sent = jnp.concatenate([own_back, jnp.pad(loss_terms, ((0, 15), (0, width - 3)))], axis=0)
    gathered = spread(sent, ("zl", "c")).reshape(nrep, quarter + 16, width)
    image_back = gathered[:, :quarter].reshape(rows, width)
    rep_loss = jnp.sum(gathered[:, quarter, :3].astype(F32))

    feat_grad = lax.dot_general(
        image_back, head_weight, (((1,), (1,)), ((), ())), preferred_element_type=F32
    ).astype(BF16)
    cols = width // nrep
    back_cols = lax.dynamic_slice_in_dim(image_back, rep_at * cols, cols, 1)
    head_t = lax.dot_general(
        back_cols, img_feat, (((0,), (0,)), ((), ())), preferred_element_type=F32
    ).astype(BF16)
    lanes = 128
    tiles = width // lanes
    flat = head_t.reshape(cols, tiles, lanes).transpose(1, 0, 2).reshape(tiles * cols, lanes)
    plane = nx * ny
    piece = -(-(tiles * cols + 16) // (plane * 16)) * 16
    tail = jnp.concatenate([jnp.full((1, 1), t, BF16) for t in split3(rep_loss)], axis=1)
    tail = jnp.pad(tail, ((0, plane * piece - tiles * cols - 1), (0, lanes - 3)))
    flat = jnp.concatenate([flat, tail], axis=0)
    parts = lax.all_to_all(flat, ("y", "x"), 0, 0, tiled=True)
    part = jnp.sum(parts.reshape(plane, piece, lanes).astype(F32), axis=0)
    part = jnp.sum(spread(part, "zh").reshape(nzh, piece, lanes), axis=0)
    at_loss = tiles * cols
    whole = lax.axis_index(("y", "x"))
    holds = whole == at_loss // piece
    line = at_loss % piece
    total = jnp.where(holds, jnp.sum(part[line, :3]), 0.0)
    terms = jnp.concatenate([jnp.full((1, 1), t, BF16) for t in split3(total)], axis=1)
    terms = jnp.pad(terms, ((0, 0), (0, lanes - 3)))
    low = part.astype(BF16)
    low = jnp.concatenate([low[:line], jnp.where(holds, terms, low[line : line + 1]), low[line + 1 :]], axis=0)
    full = spread(low, ("y", "x"))
    head_grad = full[:at_loss].reshape(tiles, cols, lanes).transpose(0, 2, 1).reshape(width, cols)
    group = rows * ny * nx * nzh
    loss = (jnp.sum(full[at_loss, :3].astype(F32)) / (group * group)).reshape(1)
    return (loss, feat_grad, head_grad)


def solution(mesh):
    devices = mesh.devices.reshape(8, 4, 4, 2, 2)
    fine = Mesh(devices, ("y", "x", "zh", "zl", "c"))
    batch, rep = (("y", "x", "zh"), ("zl", "c"))
    in_specs = (P(batch, None), P(), P(batch + rep, None), P(), P())
    out_specs = (P(), P(batch, None), P(None, rep))
    return jax.shard_map(local, mesh=fine, in_specs=in_specs, out_specs=out_specs, check_vma=False)
```

```python
import functools

import jax
import jax.numpy as jnp
from jax import lax
from jax.experimental import pallas as pl
from jax.experimental.pallas import tpu as pltpu
from jax.sharding import Mesh
from jax.sharding import PartitionSpec as P

EPS = 1e-06
BF16 = jnp.bfloat16
F32 = jnp.float32
LANES = 128
EXTRA = 16
VMEM = pl.BlockSpec(memory_space=pltpu.VMEM)
SMEM = pl.BlockSpec(memory_space=pltpu.SMEM)


def call(body, outs, *args, smem=0, flops=0, **kwargs):
    many = isinstance(outs, (tuple, list))
    specs = [SMEM] * smem + [VMEM] * (len(args) - smem)
    size = sum(a.size * a.dtype.itemsize for a in args)
    return pl.pallas_call(
        body,
        out_shape=outs,
        in_specs=specs,
        out_specs=[VMEM] * len(outs) if many else VMEM,
        cost_estimate=pl.CostEstimate(flops=flops, bytes_accessed=size, transcendentals=0),
        compiler_params=pltpu.CompilerParams(vmem_limit_bytes=40 * 2**20),
        **kwargs,
    )(*args)


def shape(dims, dtype):
    return jax.ShapeDtypeStruct(dims, dtype)


def split3(value):
    hi = value.astype(BF16)
    rest = value - hi.astype(F32)
    mid = rest.astype(BF16)
    low = (rest - mid.astype(F32)).astype(BF16)
    return [hi, mid, low]


def to_all(copies, axes):
    return lax.all_to_all(copies, axes, 0, 0, tiled=True)


def text_kernel(text_ref, out_ref):
    values = text_ref[...].astype(F32)
    inverse = lax.rsqrt(jnp.sum(values * values, axis=-1, keepdims=True) + EPS)
    low = (values * inverse).astype(BF16)
    n = text_ref.shape[0]
    for k in range(out_ref.shape[0] // n):
        out_ref[k * n : (k + 1) * n] = low


def repeat_kernel(x_ref, out_ref):
    out_ref[...] = x_ref[...]


def repeat(x, n):
    rows, width = x.shape
    return pl.pallas_call(
        repeat_kernel,
        grid=(n,),
        out_shape=shape((n * rows, width), x.dtype),
        in_specs=[pl.BlockSpec((rows, width), lambda k: (0, 0))],
        out_specs=pl.BlockSpec((rows, width), lambda k: (k, 0)),
    )(x)


def image_kernel(at_ref, wt_ref, feats_ref, unit_ref, low_ref, inv_ref, own_unit_ref, cols_ref):
    head = lax.dot_general(
        wt_ref[...], feats_ref[...], (((1,), (1,)), ((), ())), preferred_element_type=F32
    )
    inv = lax.rsqrt(jnp.sum(head * head, axis=0, keepdims=True) + EPS)
    unit = head * inv
    unit_ref[...] = unit
    low_ref[...] = unit.astype(BF16)
    inv_ref[...] = inv
    cols = cols_ref.shape[0]
    start = pl.multiple_of(at_ref[0] * cols, 16)
    cols_ref[...] = unit_ref[pl.ds(start, cols), :]
    rows = own_unit_ref.shape[1]
    lane = pl.multiple_of(at_ref[1] * rows, rows)
    own_unit_ref[...] = unit_ref[pl.ds(start, cols), pl.ds(lane, rows)]


def pair_kernel(at_ref, par_ref, texts_ref, low_ref, unit_ref, keep_ref, send_ref, acc_ref, loss_ref):
    step = pl.program_id(0)
    chunk = texts_ref.shape[0]
    images = low_ref.shape[1]
    scale = par_ref[0]
    shift = par_ref[1]

    @pl.when(step == 0)
    def _():
        acc_ref[...] = jnp.zeros_like(acc_ref)
        loss_ref[...] = jnp.zeros_like(loss_ref)

    texts = texts_ref[...]
    z = scale * jnp.dot(texts, low_ref[...], preferred_element_type=F32) + shift
    col = lax.broadcasted_iota(jnp.int32, (chunk, images), 0) + (step * chunk - at_ref[2])
    row = lax.broadcasted_iota(jnp.int32, (chunk, images), 1) - at_ref[3]
    own = (row == col) & (col >= 0) & (col < at_ref[4])
    v = jnp.where(own, -z, z)
    e = jnp.exp(-jnp.abs(v))
    one = 1.0 + e
    series = e * (1.0 - e * (0.5 - e * (1.0 / 3.0 - e * (0.25 - e * 0.2))))
    log1p = jnp.where(e < 0.03, series, jnp.log(one))
    soft = jnp.maximum(v, 0.0) + log1p
    s = jnp.where(v >= 0.0, 1.0, e) / one
    slope = jnp.where(own, -s, s).astype(BF16)
    loss_ref[...] += jnp.sum(soft, axis=0, keepdims=True)
    acc_ref[...] += lax.dot_general(
        texts, slope, (((0,), (0,)), ((), ())), preferred_element_type=F32
    )

    @pl.when(step == pl.num_programs(0) - 1)
    def _():
        cols = (keep_ref.shape[0] - EXTRA) // 2
        c = at_ref[5]
        loss = loss_ref[...]
        dots = scale * jnp.sum(unit_ref[...] * acc_ref[...], axis=0, keepdims=True)
        for k in range(2):
            mine = pl.multiple_of((2 * k + c) * cols, 16)
            other = pl.multiple_of((2 * k + 1 - c) * cols, 16)
            keep_ref[k * cols : (k + 1) * cols] = scale * acc_ref[pl.ds(mine, cols), :]
            send_ref[k * cols : (k + 1) * cols] = (scale * acc_ref[pl.ds(other, cols), :]).astype(BF16)
        pack(keep_ref, send_ref, 2 * cols, dots, loss)


def pack(keep_ref, send_ref, at, dots, loss):
    zeros = jnp.zeros((EXTRA - 2, dots.shape[1]), F32)
    keep_ref[at : at + EXTRA] = jnp.concatenate([dots, loss, zeros], axis=0)
    terms = [t.astype(F32) for t in split3(dots) + split3(loss)]
    zeros = jnp.zeros((EXTRA - 6, dots.shape[1]), F32)
    send_ref[at : at + EXTRA] = jnp.concatenate(terms + [zeros], axis=0).astype(BF16)


def unpack(keep_ref, got_ref, at):
    kept = keep_ref[at : at + EXTRA]
    got = got_ref[at : at + EXTRA].astype(F32)
    dots = kept[0:1] + (got[0:1] + got[1:2] + got[2:3])
    loss = kept[1:2] + (got[3:4] + got[4:5] + got[5:6])
    return dots, loss


def middle_kernel(at_ref, keep_ref, got_ref, keep2_ref, send2_ref):
    cols = keep2_ref.shape[0] - EXTRA
    dots, loss = unpack(keep_ref, got_ref, 2 * cols)
    zl = at_ref[6]
    mine = pl.multiple_of(zl * cols, 16)
    other = pl.multiple_of((1 - zl) * cols, 16)
    keep2_ref[:cols] = keep_ref[pl.ds(mine, cols), :] + got_ref[pl.ds(mine, cols), :].astype(F32)
    send2_ref[:cols] = (
        keep_ref[pl.ds(other, cols), :] + got_ref[pl.ds(other, cols), :].astype(F32)
    ).astype(BF16)
    pack(keep2_ref, send2_ref, cols, dots, loss)


def head_kernel(keep_ref, got_ref, unit_ref, inv_ref, feats_ref, flat_ref, dirs_ref):
    cols = keep_ref.shape[0] - EXTRA
    dots, loss = unpack(keep_ref, got_ref, cols)
    total = keep_ref[:cols] + got_ref[:cols].astype(F32)
    back = ((total - unit_ref[...] * dots) * inv_ref[...]).astype(BF16)
    head = jnp.dot(back, feats_ref[...], preferred_element_type=F32).astype(BF16)
    tiles = feats_ref.shape[1] // LANES
    for k in range(tiles):
        flat_ref[k * cols : (k + 1) * cols] = head[:, k * LANES : (k + 1) * LANES]
    blocks = dirs_ref.shape[0]
    part = loss[:, :LANES]
    for k in range(1, blocks):
        part = part + loss[:, k * LANES : (k + 1) * LANES]
    terms = [t.astype(F32) for t in split3(part)]
    tail = jnp.concatenate(terms + [jnp.zeros((EXTRA - 3, LANES), F32)], axis=0)
    at = tiles * cols
    flat_ref[at : at + EXTRA] = tail.astype(BF16)
    flat_ref[at + EXTRA :] = jnp.zeros((flat_ref.shape[0] - at - EXTRA, LANES), BF16)
    low = total.astype(BF16)
    terms = [t.astype(F32) for t in split3(dots)]
    rows = jnp.concatenate(terms + [jnp.zeros((EXTRA - 3, dots.shape[1]), F32)], axis=0).astype(BF16)
    for k in range(blocks):
        dirs_ref[k, :cols] = low[:, k * LANES : (k + 1) * LANES]
        dirs_ref[k, cols:] = rows[:, k * LANES : (k + 1) * LANES]


def back_kernel(at_ref, parts_ref, unit_ref, inv_ref, out_ref):
    cols, rows = unit_ref.shape
    parts = parts_ref[...].astype(F32)
    total = parts[0]
    for k in range(1, parts.shape[0]):
        total = total + parts[k]
    dots = total[cols : cols + 1] + total[cols + 1 : cols + 2] + total[cols + 2 : cols + 3]
    inv = inv_ref[:, pl.ds(pl.multiple_of(at_ref[1] * rows, rows), rows)]
    back = ((total[:cols] - unit_ref[...] * dots) * inv).astype(BF16)
    for k in range(out_ref.shape[0]):
        out_ref[k] = back


def sum_kernel(parts_ref, out_ref):
    total = jnp.sum(parts_ref[...].astype(F32), axis=0)
    for k in range(out_ref.shape[0]):
        out_ref[k] = total


def last_sum_kernel(at_ref, parts_ref, out_ref):
    total = jnp.sum(parts_ref[...], axis=0)
    low = total.astype(BF16)
    first = total[:EXTRA]
    terms = [t.astype(F32) for t in split3(first[0:1] + first[1:2] + first[2:3])]
    row = jnp.concatenate(terms + [jnp.zeros((EXTRA - 3, LANES), F32)], axis=0).astype(BF16)
    first = jnp.where(at_ref[7] > 0, row.astype(F32), first).astype(BF16)
    for k in range(out_ref.shape[0]):
        out_ref[k, :EXTRA] = first
        out_ref[k, EXTRA:] = low[EXTRA:]


def final_kernel(pairs, full_ref, head_ref, loss_ref):
    width, cols = head_ref.shape
    tiles = width // LANES
    for k in range(tiles):
        head_ref[k * LANES : (k + 1) * LANES] = full_ref[k * cols : (k + 1) * cols].astype(F32).T.astype(BF16)
    at = tiles * cols
    total = jnp.sum(full_ref[at : at + EXTRA].astype(F32), axis=0, keepdims=True)
    loss_ref[...] = jnp.sum(total, axis=1, keepdims=True) / pairs


def local(img_feat, head_weight, text_embed, log_temp, logit_bias):
    rows, width = img_feat.shape
    quarter = text_embed.shape[0]
    ny, nx, nzh, nzl, nc = (lax.axis_size(a) for a in ("y", "x", "zh", "zl", "c"))
    nrep = nzl * nc
    plane = nx * ny
    cols = width // nrep
    images = nzh * rows
    texts_n = plane * quarter
    tiles = width // LANES
    y_at, x_at, zh_at, zl_at, c_at = (lax.axis_index(a) for a in ("y", "x", "zh", "zl", "c"))
    rep_at = zl_at * nc + c_at
    at_loss = tiles * cols
    piece = -(-(at_loss + EXTRA) // (plane * 16)) * 16
    assert at_loss % piece == 0
    at = jnp.stack(
        [
            rep_at,
            zh_at,
            (x_at * ny + y_at) * quarter,
            zh_at * rows + rep_at * quarter,
            quarter + 0 * rep_at,
            c_at,
            zl_at,
            (y_at * nx + x_at == at_loss // piece).astype(jnp.int32),
        ]
    ).astype(jnp.int32)
    par = jnp.stack([jnp.exp(log_temp[0]), logit_bias[0]])

    feats = lax.all_gather(img_feat, "zh", axis=0, tiled=True)
    texts = call(text_kernel, shape((ny * quarter, width), BF16), text_embed)
    texts = to_all(texts, "y")
    texts = to_all(repeat(texts, nx), "x")

    unit, low, inv, own_unit, col_unit = call(
        image_kernel,
        [
            shape((width, images), F32),
            shape((width, images), BF16),
            shape((1, images), F32),
            shape((cols, rows), F32),
            shape((cols, images), F32),
        ],
        at,
        head_weight.T,
        feats,
        smem=1,
        flops=2 * width * width * images,
    )

    steps = 4
    chunk = texts_n // steps
    keep, send = pl.pallas_call(
        pair_kernel,
        grid=(steps,),
        out_shape=[shape((2 * cols + EXTRA, images), F32), shape((2 * cols + EXTRA, images), BF16)],
        in_specs=[
            SMEM,
            SMEM,
            pl.BlockSpec((chunk, width), lambda k: (k, 0)),
            pl.BlockSpec((width, images), lambda k: (0, 0)),
            pl.BlockSpec((width, images), lambda k: (0, 0)),
        ],
        out_specs=[
            pl.BlockSpec((2 * cols + EXTRA, images), lambda k: (0, 0)),
            pl.BlockSpec((2 * cols + EXTRA, images), lambda k: (0, 0)),
        ],
        scratch_shapes=[pltpu.VMEM((width, images), F32), pltpu.VMEM((1, images), F32)],
        cost_estimate=pl.CostEstimate(
            flops=4 * width * images * texts_n, bytes_accessed=8 * 2**20, transcendentals=3 * images * texts_n
        ),
        compiler_params=pltpu.CompilerParams(vmem_limit_bytes=48 * 2**20),
    )(at, par, texts, low, unit)
    got = lax.ppermute(send, "c", [(0, 1), (1, 0)])
    keep2, send2 = call(
        middle_kernel,
        [shape((cols + EXTRA, images), F32), shape((cols + EXTRA, images), BF16)],
        at,
        keep,
        got,
        smem=1,
    )
    got2 = lax.ppermute(send2, "zl", [(0, 1), (1, 0)])
    flat, dirs = call(
        head_kernel,
        [shape((plane * piece, LANES), BF16), shape((nzh, cols + EXTRA, rows), BF16)],
        keep2,
        got2,
        col_unit,
        inv,
        feats,
        flops=2 * cols * images * width,
    )

    parts = to_all(flat, ("y", "x")).reshape(plane, piece, LANES)
    part = call(sum_kernel, shape((nzh, piece, LANES), F32), parts)
    part = to_all(part, "zh")
    low_part = call(last_sum_kernel, shape((plane, piece, LANES), BF16), at, part, smem=1)
    full = to_all(low_part.reshape(plane * piece, LANES), ("y", "x"))
    group = rows * plane * nzh
    head_grad, loss = call(
        functools.partial(final_kernel, float(group) * float(group)),
        [shape((width, cols), BF16), shape((1, 1), F32)],
        full,
    )

    dirs = to_all(dirs, "zh")
    back = call(back_kernel, shape((nrep, cols, rows), BF16), at, dirs, own_unit, inv, smem=1)
    back = to_all(back, ("zl", "c")).reshape(width, rows)
    feat_grad = lax.dot_general(
        back, head_weight, (((0,), (1,)), ((), ())), preferred_element_type=F32
    ).astype(BF16)
    return (loss.reshape(1), feat_grad, head_grad)


def solution(mesh):
    devices = mesh.devices.reshape(8, 4, 4, 2, 2)
    fine = Mesh(devices, ("y", "x", "zh", "zl", "c"))
    batch, rep = (("y", "x", "zh"), ("zl", "c"))
    in_specs = (P(batch, None), P(), P(batch + rep, None), P(), P())
    out_specs = (P(), P(batch, None), P(None, rep))
    return jax.shard_map(local, mesh=fine, in_specs=in_specs, out_specs=out_specs, check_vma=False)
```

```python
import functools

import jax
import jax.numpy as jnp
from jax import lax
from jax.experimental import pallas as pl
from jax.experimental.pallas import tpu as pltpu
from jax.sharding import Mesh
from jax.sharding import PartitionSpec as P

EPS = 1e-06
BF16 = jnp.bfloat16
F32 = jnp.float32
LANES = 128
EXTRA = 16
VMEM = pl.BlockSpec(memory_space=pltpu.VMEM)
SMEM = pl.BlockSpec(memory_space=pltpu.SMEM)


def call(body, outs, *args, smem=0, flops=0, **kwargs):
    many = isinstance(outs, (tuple, list))
    specs = [SMEM] * smem + [VMEM] * (len(args) - smem)
    size = sum(a.size * a.dtype.itemsize for a in args)
    return pl.pallas_call(
        body,
        out_shape=outs,
        in_specs=specs,
        out_specs=[VMEM] * len(outs) if many else VMEM,
        cost_estimate=pl.CostEstimate(flops=flops, bytes_accessed=size, transcendentals=0),
        compiler_params=pltpu.CompilerParams(vmem_limit_bytes=40 * 2**20),
        **kwargs,
    )(*args)


def shape(dims, dtype):
    return jax.ShapeDtypeStruct(dims, dtype)


def split3(value):
    hi = value.astype(BF16)
    rest = value - hi.astype(F32)
    mid = rest.astype(BF16)
    low = (rest - mid.astype(F32)).astype(BF16)
    return [hi, mid, low]


def to_all(copies, axes):
    return lax.all_to_all(copies, axes, 0, 0, tiled=True)


def text_kernel(text_ref, out_ref):
    values = text_ref[...].astype(F32)
    inverse = lax.rsqrt(jnp.sum(values * values, axis=-1, keepdims=True) + EPS)
    low = (values * inverse).astype(BF16)
    n = text_ref.shape[0]
    for k in range(out_ref.shape[0] // n):
        out_ref[k * n : (k + 1) * n] = low


def image_kernel(at_ref, wt_ref, *refs):
    feat_refs = refs[:-6]
    unit_ref, low_ref, inv_ref, own_unit_ref, cols_ref, feats_ref = refs[-6:]
    n = len(feat_refs)
    rows = feat_refs[0].shape[0]
    for k in range(n):
        feats_ref[k * rows : (k + 1) * rows] = feat_refs[k][...]
    head = lax.dot_general(
        wt_ref[...], feats_ref[...], (((1,), (1,)), ((), ())), preferred_element_type=F32
    )
    inv = lax.rsqrt(jnp.sum(head * head, axis=0, keepdims=True) + EPS)
    unit = head * inv
    unit_ref[...] = unit
    low_ref[...] = unit.astype(BF16)
    inv_ref[...] = inv
    cols = cols_ref.shape[0]
    start = pl.multiple_of(at_ref[0] * cols, 16)
    cols_ref[...] = unit_ref[pl.ds(start, cols), :]
    own_unit_ref[...] = unit_ref[pl.ds(start, cols), :rows]


def pairs(par_ref, texts, low_ref, own=None):
    z = par_ref[0] * jnp.dot(texts, low_ref[...], preferred_element_type=F32) + par_ref[1]
    v = z if own is None else jnp.where(own, -z, z)
    e = jnp.exp(-jnp.abs(v))
    one = 1.0 + e
    series = e * (1.0 - e * (0.5 - e * (1.0 / 3.0 - e * (0.25 - e * 0.2))))
    log1p = jnp.where(e < 0.03, series, jnp.log(one))
    soft = jnp.maximum(v, 0.0) + log1p
    s = jnp.where(v >= 0.0, 1.0, e) / one
    slope = (s if own is None else jnp.where(own, -s, s)).astype(BF16)
    return slope, jnp.sum(soft, axis=0, keepdims=True)


def turn(texts, slope):
    return lax.dot_general(texts, slope, (((0,), (0,)), ((), ())), preferred_element_type=F32)


def first_kernel(at_ref, par_ref, own_ref, left_ref, right_ref, low_ref, acc_ref, loss_ref):
    size = (own_ref.shape[0], low_ref.shape[1])
    col = lax.broadcasted_iota(jnp.int32, size, 0) - at_ref[2]
    row = lax.broadcasted_iota(jnp.int32, size, 1) - at_ref[3]
    own = (row == col) & (col >= 0) & (col < at_ref[4])
    slope, loss = pairs(par_ref, own_ref[...], low_ref, own)
    acc_ref[...] = turn(own_ref[...], slope)
    for ref in (left_ref, right_ref):
        slope, more = pairs(par_ref, ref[...], low_ref)
        acc_ref[...] += turn(ref[...], slope)
        loss = loss + more
    loss_ref[...] = loss


def second_kernel(at_ref, par_ref, a_ref, b_ref, low_ref, unit_ref, acc_ref, loss_ref, keep_ref, send_ref, sum_ref):
    scale = par_ref[0]
    texts = jnp.concatenate([a_ref[...], b_ref[...]], axis=0)
    slope, loss = pairs(par_ref, texts, low_ref)
    loss = loss_ref[...] + loss
    total = scale * (acc_ref[...] + turn(texts, slope))
    sum_ref[...] = total
    dots = jnp.sum(unit_ref[...] * total, axis=0, keepdims=True)
    cols = (keep_ref.shape[0] - EXTRA) // 2
    c = at_ref[5]
    for k in range(2):
        mine = pl.multiple_of((2 * k + c) * cols, 16)
        other = pl.multiple_of((2 * k + 1 - c) * cols, 16)
        keep_ref[k * cols : (k + 1) * cols] = sum_ref[pl.ds(mine, cols), :]
        send_ref[k * cols : (k + 1) * cols] = sum_ref[pl.ds(other, cols), :].astype(BF16)
    pack(keep_ref, send_ref, 2 * cols, dots, loss)


def pack(keep_ref, send_ref, at, dots, loss):
    zeros = jnp.zeros((EXTRA - 2, dots.shape[1]), F32)
    keep_ref[at : at + EXTRA] = jnp.concatenate([dots, loss, zeros], axis=0)
    terms = [t.astype(F32) for t in split3(dots) + split3(loss)]
    zeros = jnp.zeros((EXTRA - 6, dots.shape[1]), F32)
    send_ref[at : at + EXTRA] = jnp.concatenate(terms + [zeros], axis=0).astype(BF16)


def unpack(keep_ref, got_ref, at):
    kept = keep_ref[at : at + EXTRA]
    got = got_ref[at : at + EXTRA].astype(F32)
    dots = kept[0:1] + (got[0:1] + got[1:2] + got[2:3])
    loss = kept[1:2] + (got[3:4] + got[4:5] + got[5:6])
    return dots, loss


def middle_kernel(at_ref, keep_ref, got_ref, keep2_ref, send2_ref):
    cols = keep2_ref.shape[0] - EXTRA
    dots, loss = unpack(keep_ref, got_ref, 2 * cols)
    zl = at_ref[6]
    mine = pl.multiple_of(zl * cols, 16)
    other = pl.multiple_of((1 - zl) * cols, 16)
    keep2_ref[:cols] = keep_ref[pl.ds(mine, cols), :] + got_ref[pl.ds(mine, cols), :].astype(F32)
    send2_ref[:cols] = (
        keep_ref[pl.ds(other, cols), :] + got_ref[pl.ds(other, cols), :].astype(F32)
    ).astype(BF16)
    pack(keep2_ref, send2_ref, cols, dots, loss)


def head_kernel(keep_ref, got_ref, unit_ref, inv_ref, feats_ref, flat_ref, *dir_refs):
    cols = keep_ref.shape[0] - EXTRA
    dots, loss = unpack(keep_ref, got_ref, cols)
    total = keep_ref[:cols] + got_ref[:cols].astype(F32)
    back = ((total - unit_ref[...] * dots) * inv_ref[...]).astype(BF16)
    head = jnp.dot(back, feats_ref[...], preferred_element_type=F32).astype(BF16)
    tiles = feats_ref.shape[1] // LANES
    for k in range(tiles):
        flat_ref[k * cols : (k + 1) * cols] = head[:, k * LANES : (k + 1) * LANES]
    part = loss[:, :LANES]
    for k in range(1, loss.shape[1] // LANES):
        part = part + loss[:, k * LANES : (k + 1) * LANES]
    terms = [t.astype(F32) for t in split3(part)]
    tail = jnp.concatenate(terms + [jnp.zeros((EXTRA - 3, LANES), F32)], axis=0)
    at = tiles * cols
    flat_ref[at : at + EXTRA] = tail.astype(BF16)
    flat_ref[at + EXTRA :] = jnp.zeros((flat_ref.shape[0] - at - EXTRA, LANES), BF16)
    low = total.astype(BF16)
    terms = [t.astype(F32) for t in split3(dots)]
    lines = jnp.concatenate(terms + [jnp.zeros((EXTRA - 3, dots.shape[1]), F32)], axis=0).astype(BF16)
    rows = dir_refs[0].shape[1]
    for k, ref in enumerate(dir_refs):
        ref[:cols] = low[:, k * rows : (k + 1) * rows]
        ref[cols:] = lines[:, k * rows : (k + 1) * rows]


def back_kernel(unit_ref, inv_ref, *refs):
    out_ref = refs[-1]
    cols, rows = unit_ref.shape
    total = refs[0][...].astype(F32)
    for ref in refs[1:-1]:
        total = total + ref[...].astype(F32)
    dots = total[cols : cols + 1] + total[cols + 1 : cols + 2] + total[cols + 2 : cols + 3]
    out_ref[...] = ((total[:cols] - unit_ref[...] * dots) * inv_ref[:, :rows]).astype(BF16)


def sum_kernel(parts_ref, after_ref, out_ref):
    total = jnp.sum(parts_ref[...].astype(F32), axis=0)
    for k in range(out_ref.shape[0]):
        out_ref[k] = total


def feat_kernel(at_ref, weight_ref, *refs):
    out_ref, back_ref = refs[-2:]
    cols = refs[0].shape[0]
    for d, ref in enumerate(refs[:-2]):
        back_ref[pl.ds(pl.multiple_of(at_ref[8 + d] * cols, 16), cols), :] = ref[...]
    out_ref[...] = lax.dot_general(
        back_ref[...], weight_ref[...], (((0,), (1,)), ((), ())), preferred_element_type=F32
    ).astype(BF16)


def last_sum_kernel(at_ref, parts_ref, out_ref):
    total = jnp.sum(parts_ref[...], axis=0)
    low = total.astype(BF16)
    first = total[:EXTRA]
    terms = [t.astype(F32) for t in split3(first[0:1] + first[1:2] + first[2:3])]
    row = jnp.concatenate(terms + [jnp.zeros((EXTRA - 3, LANES), F32)], axis=0).astype(BF16)
    first = jnp.where(at_ref[7] > 0, row.astype(F32), first).astype(BF16)
    for k in range(out_ref.shape[0]):
        out_ref[k, :EXTRA] = first
        out_ref[k, EXTRA:] = low[EXTRA:]


def final_kernel(pairs, full_ref, head_ref, loss_ref):
    width, cols = head_ref.shape
    tiles = width // LANES
    for k in range(tiles):
        head_ref[k * LANES : (k + 1) * LANES] = full_ref[k * cols : (k + 1) * cols].astype(F32).T.astype(BF16)
    at = tiles * cols
    total = jnp.sum(full_ref[at : at + EXTRA].astype(F32), axis=0, keepdims=True)
    loss_ref[...] = jnp.sum(total, axis=1, keepdims=True) / pairs


def shift_by(x, axis, step):
    n = lax.axis_size(axis)
    return lax.ppermute(x, axis, [(k, (k + step) % n) for k in range(n)])


def local(img_feat, head_weight, text_embed, log_temp, logit_bias):
    rows, width = img_feat.shape
    quarter = text_embed.shape[0]
    ny, nx, nzh, nzl, nc = (lax.axis_size(a) for a in ("y", "x", "zh", "zl", "c"))
    nrep = nzl * nc
    plane = nx * ny
    cols = width // nrep
    images = nzh * rows
    tiles = width // LANES
    y_at, x_at, zl_at, c_at = (lax.axis_index(a) for a in ("y", "x", "zl", "c"))
    rep_at = zl_at * nc + c_at
    at_loss = tiles * cols
    piece = -(-(at_loss + EXTRA) // (plane * 16)) * 16
    assert at_loss % piece == 0
    at = jnp.stack(
        [
            rep_at,
            0 * rep_at,
            y_at * quarter,
            rep_at * quarter,
            quarter + 0 * rep_at,
            c_at,
            zl_at,
            (y_at * nx + x_at == at_loss // piece).astype(jnp.int32),
        ]
        + [rep_at ^ d for d in range(nrep)]
    ).astype(jnp.int32)
    par = jnp.stack([jnp.exp(log_temp[0]), logit_bias[0]])

    copies = call(text_kernel, shape((ny * quarter, width), BF16), text_embed)
    feats = [img_feat] + [shift_by(img_feat, "zh", s) for s in range(1, nzh)]
    own = to_all(copies, "y")
    left = shift_by(own, "x", 1)
    right = shift_by(own, "x", -1)
    half = own.shape[0] // 2
    far_a = shift_by(left[:half], "x", 1)
    far_b = shift_by(right[half:], "x", -1)

    unit, low, inv, own_unit, col_unit, feats = call(
        image_kernel,
        [
            shape((width, images), F32),
            shape((width, images), BF16),
            shape((1, images), F32),
            shape((cols, rows), F32),
            shape((cols, images), F32),
            shape((images, width), BF16),
        ],
        at,
        head_weight.T,
        *feats,
        smem=1,
        flops=2 * width * width * images,
    )
    acc, loss_row = call(
        first_kernel,
        [shape((width, images), F32), shape((1, images), F32)],
        at,
        par,
        own,
        left,
        right,
        low,
        smem=2,
        flops=4 * width * images * 3 * own.shape[0],
    )
    keep, send = call(
        second_kernel,
        [shape((2 * cols + EXTRA, images), F32), shape((2 * cols + EXTRA, images), BF16)],
        at,
        par,
        far_a,
        far_b,
        low,
        unit,
        acc,
        loss_row,
        smem=2,
        flops=4 * width * images * own.shape[0],
        scratch_shapes=[pltpu.VMEM((width, images), F32)],
    )
    got = lax.ppermute(send, "c", [(0, 1), (1, 0)])
    keep2, send2 = call(
        middle_kernel,
        [shape((cols + EXTRA, images), F32), shape((cols + EXTRA, images), BF16)],
        at,
        keep,
        got,
        smem=1,
    )
    got2 = lax.ppermute(send2, "zl", [(0, 1), (1, 0)])
    flat, *dirs = call(
        head_kernel,
        [shape((plane * piece, LANES), BF16)] + [shape((cols + EXTRA, rows), BF16)] * nzh,
        keep2,
        got2,
        col_unit,
        inv,
        feats,
        flops=2 * cols * images * width,
    )

    dirs = [dirs[0]] + [shift_by(dirs[s], "zh", -s) for s in range(1, nzh)]
    back = call(back_kernel, shape((cols, rows), BF16), own_unit, inv, *dirs)

    parts = to_all(flat, ("y", "x")).reshape(plane, piece, LANES)
    part = pl.pallas_call(
        sum_kernel,
        out_shape=shape((nzh, piece, LANES), F32),
        in_specs=[VMEM, pl.BlockSpec(memory_space=pl.ANY)],
        out_specs=VMEM,
    )(parts, back)
    part = to_all(part, "zh")
    low_part = call(last_sum_kernel, shape((plane, piece, LANES), BF16), at, part, smem=1)
    full = to_all(low_part.reshape(plane * piece, LANES), ("y", "x"))
    group = rows * plane * nzh
    head_grad, loss = call(
        functools.partial(final_kernel, float(group) * float(group)),
        [shape((width, cols), BF16), shape((1, 1), F32)],
        full,
    )

    backs = [back]
    for d in range(1, nrep):
        backs.append(lax.ppermute(back, ("zl", "c"), [(k, k ^ d) for k in range(nrep)]))
    feat_grad = call(
        feat_kernel,
        shape((rows, width), BF16),
        at,
        head_weight,
        *backs,
        smem=1,
        flops=2 * rows * width * width,
        scratch_shapes=[pltpu.VMEM((width, rows), BF16)],
    )
    return (loss.reshape(1), feat_grad, head_grad)


def solution(mesh):
    devices = mesh.devices.reshape(8, 4, 4, 2, 2)
    fine = Mesh(devices, ("y", "x", "zh", "zl", "c"))
    batch, rep = (("y", "x", "zh"), ("zl", "c"))
    in_specs = (P(batch, None), P(), P(batch + rep, None), P(), P())
    out_specs = (P(), P(batch, None), P(None, rep))
    return jax.shard_map(local, mesh=fine, in_specs=in_specs, out_specs=out_specs, check_vma=False)
```

```python
import functools

import jax
import jax.numpy as jnp
from jax import lax
from jax.experimental import pallas as pl
from jax.experimental.pallas import tpu as pltpu
from jax.sharding import Mesh
from jax.sharding import PartitionSpec as P

EPS = 1e-06
BF16 = jnp.bfloat16
F32 = jnp.float32
LANES = 128
EXTRA = 16
VMEM = pl.BlockSpec(memory_space=pltpu.VMEM)
SMEM = pl.BlockSpec(memory_space=pltpu.SMEM)


def call(body, outs, *args, smem=0, flops=0, **kwargs):
    many = isinstance(outs, (tuple, list))
    specs = [SMEM] * smem + [VMEM] * (len(args) - smem)
    size = sum(a.size * a.dtype.itemsize for a in args)
    return pl.pallas_call(
        body,
        out_shape=outs,
        in_specs=specs,
        out_specs=[VMEM] * len(outs) if many else VMEM,
        cost_estimate=pl.CostEstimate(flops=flops, bytes_accessed=size, transcendentals=0),
        compiler_params=pltpu.CompilerParams(vmem_limit_bytes=40 * 2**20),
        **kwargs,
    )(*args)


def shape(dims, dtype):
    return jax.ShapeDtypeStruct(dims, dtype)


def split3(value):
    hi = value.astype(BF16)
    rest = value - hi.astype(F32)
    mid = rest.astype(BF16)
    low = (rest - mid.astype(F32)).astype(BF16)
    return [hi, mid, low]


def to_all(copies, axes):
    return lax.all_to_all(copies, axes, 0, 0, tiled=True)


def text_kernel(text_ref, out_ref):
    values = text_ref[...].astype(F32)
    inverse = lax.rsqrt(jnp.sum(values * values, axis=-1, keepdims=True) + EPS)
    low = (values * inverse).astype(BF16)
    n = text_ref.shape[0]
    for k in range(out_ref.shape[0] // n):
        out_ref[k * n : (k + 1) * n] = low


def image_kernel(at_ref, wt_ref, own_ref, fetched_ref, swapped_ref, *refs):
    unit_ref, low_ref, inv_ref, own_unit_ref, cols_ref, feats_ref = refs
    rows = own_ref.shape[0]
    part = rows // 2
    c = at_ref[5]
    feats_ref[:rows] = own_ref[...]
    for k in range(fetched_ref.shape[0] // part):
        base = (k + 1) * rows
        block = pl.ds(k * part, part)
        feats_ref[pl.ds(pl.multiple_of(base + c * part, 16), part), :] = fetched_ref[block, :]
        feats_ref[pl.ds(pl.multiple_of(base + (1 - c) * part, 16), part), :] = swapped_ref[block, :]
    head = lax.dot_general(
        wt_ref[...], feats_ref[...], (((1,), (1,)), ((), ())), preferred_element_type=F32
    )
    inv = lax.rsqrt(jnp.sum(head * head, axis=0, keepdims=True) + EPS)
    unit = head * inv
    unit_ref[...] = unit
    low_ref[...] = unit.astype(BF16)
    inv_ref[...] = inv
    cols = cols_ref.shape[0]
    start = pl.multiple_of(at_ref[0] * cols, 16)
    cols_ref[...] = unit_ref[pl.ds(start, cols), :]
    own_unit_ref[...] = unit_ref[pl.ds(start, cols), :rows]


def pairs(par_ref, texts, low_ref, own=None):
    z = par_ref[0] * jnp.dot(texts, low_ref[...], preferred_element_type=F32) + par_ref[1]
    v = z if own is None else jnp.where(own, -z, z)
    e = jnp.exp(-jnp.abs(v))
    one = 1.0 + e
    series = e * (1.0 - e * (0.5 - e * (1.0 / 3.0 - e * (0.25 - e * 0.2))))
    log1p = jnp.where(e < 0.03, series, jnp.log(one))
    soft = jnp.maximum(v, 0.0) + log1p
    s = jnp.where(v >= 0.0, 1.0, e) / one
    slope = (s if own is None else jnp.where(own, -s, s)).astype(BF16)
    return slope, jnp.sum(soft, axis=0, keepdims=True)


def turn(texts, slope):
    return lax.dot_general(texts, slope, (((0,), (0,)), ((), ())), preferred_element_type=F32)


def first_kernel(at_ref, par_ref, own_ref, left_ref, right_ref, low_ref, acc_ref, loss_ref):
    size = (own_ref.shape[0], low_ref.shape[1])
    col = lax.broadcasted_iota(jnp.int32, size, 0) - at_ref[2]
    row = lax.broadcasted_iota(jnp.int32, size, 1) - at_ref[3]
    own = (row == col) & (col >= 0) & (col < at_ref[4])
    slope, loss = pairs(par_ref, own_ref[...], low_ref, own)
    acc_ref[...] = turn(own_ref[...], slope)
    for ref in (left_ref, right_ref):
        slope, more = pairs(par_ref, ref[...], low_ref)
        acc_ref[...] += turn(ref[...], slope)
        loss = loss + more
    loss_ref[...] = loss


def second_kernel(at_ref, par_ref, a_ref, b_ref, low_ref, unit_ref, acc_ref, loss_ref, keep_ref, send_ref, sum_ref):
    scale = par_ref[0]
    texts = jnp.concatenate([a_ref[...], b_ref[...]], axis=0)
    slope, loss = pairs(par_ref, texts, low_ref)
    loss = loss_ref[...] + loss
    total = scale * (acc_ref[...] + turn(texts, slope))
    sum_ref[...] = total
    dots = jnp.sum(unit_ref[...] * total, axis=0, keepdims=True)
    cols = (keep_ref.shape[0] - EXTRA) // 2
    c = at_ref[5]
    for k in range(2):
        mine = pl.multiple_of((2 * k + c) * cols, 16)
        other = pl.multiple_of((2 * k + 1 - c) * cols, 16)
        keep_ref[k * cols : (k + 1) * cols] = sum_ref[pl.ds(mine, cols), :]
        send_ref[k * cols : (k + 1) * cols] = sum_ref[pl.ds(other, cols), :].astype(BF16)
    pack(keep_ref, send_ref, 2 * cols, dots, loss)


def pack(keep_ref, send_ref, at, dots, loss):
    zeros = jnp.zeros((EXTRA - 2, dots.shape[1]), F32)
    keep_ref[at : at + EXTRA] = jnp.concatenate([dots, loss, zeros], axis=0)
    terms = [t.astype(F32) for t in split3(dots) + split3(loss)]
    zeros = jnp.zeros((EXTRA - 6, dots.shape[1]), F32)
    send_ref[at : at + EXTRA] = jnp.concatenate(terms + [zeros], axis=0).astype(BF16)


def unpack(keep_ref, got_ref, at):
    kept = keep_ref[at : at + EXTRA]
    got = got_ref[at : at + EXTRA].astype(F32)
    dots = kept[0:1] + (got[0:1] + got[1:2] + got[2:3])
    loss = kept[1:2] + (got[3:4] + got[4:5] + got[5:6])
    return dots, loss


def middle_kernel(at_ref, keep_ref, got_ref, keep2_ref, send2_ref):
    cols = keep2_ref.shape[0] - EXTRA
    dots, loss = unpack(keep_ref, got_ref, 2 * cols)
    zl = at_ref[6]
    mine = pl.multiple_of(zl * cols, 16)
    other = pl.multiple_of((1 - zl) * cols, 16)
    keep2_ref[:cols] = keep_ref[pl.ds(mine, cols), :] + got_ref[pl.ds(mine, cols), :].astype(F32)
    send2_ref[:cols] = (
        keep_ref[pl.ds(other, cols), :] + got_ref[pl.ds(other, cols), :].astype(F32)
    ).astype(BF16)
    pack(keep2_ref, send2_ref, cols, dots, loss)


def head_kernel(keep_ref, got_ref, unit_ref, inv_ref, feats_ref, flat_ref, *dir_refs):
    cols = keep_ref.shape[0] - EXTRA
    dots, loss = unpack(keep_ref, got_ref, cols)
    total = keep_ref[:cols] + got_ref[:cols].astype(F32)
    back = ((total - unit_ref[...] * dots) * inv_ref[...]).astype(BF16)
    head = jnp.dot(back, feats_ref[...], preferred_element_type=F32).astype(BF16)
    tiles = feats_ref.shape[1] // LANES
    for k in range(tiles):
        flat_ref[k * cols : (k + 1) * cols] = head[:, k * LANES : (k + 1) * LANES]
    part = loss[:, :LANES]
    for k in range(1, loss.shape[1] // LANES):
        part = part + loss[:, k * LANES : (k + 1) * LANES]
    terms = [t.astype(F32) for t in split3(part)]
    tail = jnp.concatenate(terms + [jnp.zeros((EXTRA - 3, LANES), F32)], axis=0)
    at = tiles * cols
    flat_ref[at : at + EXTRA] = tail.astype(BF16)
    flat_ref[at + EXTRA :] = jnp.zeros((flat_ref.shape[0] - at - EXTRA, LANES), BF16)
    low = total.astype(BF16)
    terms = [t.astype(F32) for t in split3(dots)]
    lines = jnp.concatenate(terms + [jnp.zeros((EXTRA - 3, dots.shape[1]), F32)], axis=0).astype(BF16)
    rows = dir_refs[0].shape[1]
    for k, ref in enumerate(dir_refs):
        ref[:cols] = low[:, k * rows : (k + 1) * rows]
        ref[cols:] = lines[:, k * rows : (k + 1) * rows]


def back_kernel(unit_ref, inv_ref, *refs):
    out_ref = refs[-1]
    cols, rows = unit_ref.shape
    total = refs[0][...].astype(F32)
    for ref in refs[1:-1]:
        total = total + ref[...].astype(F32)
    dots = total[cols : cols + 1] + total[cols + 1 : cols + 2] + total[cols + 2 : cols + 3]
    out_ref[...] = ((total[:cols] - unit_ref[...] * dots) * inv_ref[:, :rows]).astype(BF16)


def sum_kernel(parts_ref, after_ref, out_ref):
    total = jnp.sum(parts_ref[...].astype(F32), axis=0)
    for k in range(out_ref.shape[0]):
        out_ref[k] = total


def feat_kernel(at_ref, weight_ref, *refs):
    out_ref, back_ref = refs[-2:]
    cols = refs[0].shape[0]
    for d, ref in enumerate(refs[:-2]):
        back_ref[pl.ds(pl.multiple_of(at_ref[8 + d] * cols, 16), cols), :] = ref[...]
    out_ref[...] = lax.dot_general(
        back_ref[...], weight_ref[...], (((0,), (1,)), ((), ())), preferred_element_type=F32
    ).astype(BF16)


def last_sum_kernel(at_ref, parts_ref, out_ref):
    total = jnp.sum(parts_ref[...], axis=0)
    low = total.astype(BF16)
    first = total[:EXTRA]
    terms = [t.astype(F32) for t in split3(first[0:1] + first[1:2] + first[2:3])]
    row = jnp.concatenate(terms + [jnp.zeros((EXTRA - 3, LANES), F32)], axis=0).astype(BF16)
    first = jnp.where(at_ref[7] > 0, row.astype(F32), first).astype(BF16)
    for k in range(out_ref.shape[0]):
        out_ref[k, :EXTRA] = first
        out_ref[k, EXTRA:] = low[EXTRA:]


def final_kernel(pairs, full_ref, head_ref, loss_ref):
    width, cols = head_ref.shape
    tiles = width // LANES
    for k in range(tiles):
        head_ref[k * LANES : (k + 1) * LANES] = full_ref[k * cols : (k + 1) * cols].astype(F32).T.astype(BF16)
    at = tiles * cols
    total = jnp.sum(full_ref[at : at + EXTRA].astype(F32), axis=0, keepdims=True)
    loss_ref[...] = jnp.sum(total, axis=1, keepdims=True) / pairs


def shift_by(x, axis, step):
    n = lax.axis_size(axis)
    return lax.ppermute(x, axis, [(k, (k + step) % n) for k in range(n)])


def local(img_feat, head_weight, text_embed, log_temp, logit_bias):
    rows, width = img_feat.shape
    quarter = text_embed.shape[0]
    ny, nx, nzh, nzl, nc = (lax.axis_size(a) for a in ("y", "x", "zh", "zl", "c"))
    nrep = nzl * nc
    plane = nx * ny
    cols = width // nrep
    images = nzh * rows
    tiles = width // LANES
    y_at, x_at, zl_at, c_at = (lax.axis_index(a) for a in ("y", "x", "zl", "c"))
    rep_at = zl_at * nc + c_at
    at_loss = tiles * cols
    piece = -(-(at_loss + EXTRA) // (plane * 16)) * 16
    assert at_loss % piece == 0
    at = jnp.stack(
        [
            rep_at,
            0 * rep_at,
            y_at * quarter,
            rep_at * quarter,
            quarter + 0 * rep_at,
            c_at,
            zl_at,
            (y_at * nx + x_at == at_loss // piece).astype(jnp.int32),
        ]
        + [rep_at ^ d for d in range(nrep)]
    ).astype(jnp.int32)
    par = jnp.stack([jnp.exp(log_temp[0]), logit_bias[0]])

    copies = call(text_kernel, shape((ny * quarter, width), BF16), text_embed)
    part = rows // nc
    half_rows = lax.dynamic_slice_in_dim(img_feat, c_at * part, part, 0)
    fetched = jnp.concatenate([shift_by(half_rows, "zh", s) for s in range(1, nzh)], axis=0)
    own = to_all(copies, "y")
    own, fetched = lax.optimization_barrier((own, fetched))
    swapped = lax.ppermute(fetched, "c", [(0, 1), (1, 0)])
    left = shift_by(own, "x", 1)
    right = shift_by(own, "x", -1)
    unit, low, inv, own_unit, col_unit, feats = call(
        image_kernel,
        [
            shape((width, images), F32),
            shape((width, images), BF16),
            shape((1, images), F32),
            shape((cols, rows), F32),
            shape((cols, images), F32),
            shape((images, width), BF16),
        ],
        at,
        head_weight.T,
        img_feat,
        fetched,
        swapped,
        smem=1,
        flops=2 * width * width * images,
    )
    left, right, low = lax.optimization_barrier((left, right, low))
    half = own.shape[0] // 2
    far_a = shift_by(left[:half], "x", 1)
    far_b = shift_by(right[half:], "x", -1)
    acc, loss_row = call(
        first_kernel,
        [shape((width, images), F32), shape((1, images), F32)],
        at,
        par,
        own,
        left,
        right,
        low,
        smem=2,
        flops=4 * width * images * 3 * own.shape[0],
    )
    keep, send = call(
        second_kernel,
        [shape((2 * cols + EXTRA, images), F32), shape((2 * cols + EXTRA, images), BF16)],
        at,
        par,
        far_a,
        far_b,
        low,
        unit,
        acc,
        loss_row,
        smem=2,
        flops=4 * width * images * own.shape[0],
        scratch_shapes=[pltpu.VMEM((width, images), F32)],
    )
    got = lax.ppermute(send, "c", [(0, 1), (1, 0)])
    keep2, send2 = call(
        middle_kernel,
        [shape((cols + EXTRA, images), F32), shape((cols + EXTRA, images), BF16)],
        at,
        keep,
        got,
        smem=1,
    )
    got2 = lax.ppermute(send2, "zl", [(0, 1), (1, 0)])
    flat, *dirs = call(
        head_kernel,
        [shape((plane * piece, LANES), BF16)] + [shape((cols + EXTRA, rows), BF16)] * nzh,
        keep2,
        got2,
        col_unit,
        inv,
        feats,
        flops=2 * cols * images * width,
    )

    dirs = [dirs[0]] + [shift_by(dirs[s], "zh", -s) for s in range(1, nzh)]
    back = call(back_kernel, shape((cols, rows), BF16), own_unit, inv, *dirs)

    parts = to_all(flat, ("y", "x")).reshape(plane, piece, LANES)
    part = pl.pallas_call(
        sum_kernel,
        out_shape=shape((nzh, piece, LANES), F32),
        in_specs=[VMEM, pl.BlockSpec(memory_space=pl.ANY)],
        out_specs=VMEM,
    )(parts, back)
    part = to_all(part, "zh")
    low_part = call(last_sum_kernel, shape((plane, piece, LANES), BF16), at, part, smem=1)
    full = to_all(low_part.reshape(plane * piece, LANES), ("y", "x"))
    group = rows * plane * nzh
    head_grad, loss = call(
        functools.partial(final_kernel, float(group) * float(group)),
        [shape((width, cols), BF16), shape((1, 1), F32)],
        full,
    )

    backs = [back]
    for d in range(1, nrep):
        backs.append(lax.ppermute(back, ("zl", "c"), [(k, k ^ d) for k in range(nrep)]))
    feat_grad = call(
        feat_kernel,
        shape((rows, width), BF16),
        at,
        head_weight,
        *backs,
        smem=1,
        flops=2 * rows * width * width,
        scratch_shapes=[pltpu.VMEM((width, rows), BF16)],
    )
    return (loss.reshape(1), feat_grad, head_grad)


def solution(mesh):
    devices = mesh.devices.reshape(8, 4, 4, 2, 2)
    fine = Mesh(devices, ("y", "x", "zh", "zl", "c"))
    batch, rep = (("y", "x", "zh"), ("zl", "c"))
    in_specs = (P(batch, None), P(), P(batch + rep, None), P(), P())
    out_specs = (P(), P(batch, None), P(None, rep))
    return jax.shard_map(local, mesh=fine, in_specs=in_specs, out_specs=out_specs, check_vma=False)
```

```python
import functools

import jax
import jax.numpy as jnp
from jax import lax
from jax.experimental import pallas as pl
from jax.experimental.pallas import tpu as pltpu
from jax.sharding import Mesh
from jax.sharding import PartitionSpec as P

EPS = 1e-06
BF16 = jnp.bfloat16
F32 = jnp.float32
LANES = 128
EXTRA = 16
VMEM = pl.BlockSpec(memory_space=pltpu.VMEM)
SMEM = pl.BlockSpec(memory_space=pltpu.SMEM)


def call(body, outs, *args, smem=0, flops=0, **kwargs):
    many = isinstance(outs, (tuple, list))
    specs = [SMEM] * smem + [VMEM] * (len(args) - smem)
    size = sum(a.size * a.dtype.itemsize for a in args)
    return pl.pallas_call(
        body,
        out_shape=outs,
        in_specs=specs,
        out_specs=[VMEM] * len(outs) if many else VMEM,
        cost_estimate=pl.CostEstimate(flops=flops, bytes_accessed=size, transcendentals=0),
        compiler_params=pltpu.CompilerParams(vmem_limit_bytes=40 * 2**20),
        **kwargs,
    )(*args)


def shape(dims, dtype):
    return jax.ShapeDtypeStruct(dims, dtype)


def split3(value):
    hi = value.astype(BF16)
    rest = value - hi.astype(F32)
    mid = rest.astype(BF16)
    low = (rest - mid.astype(F32)).astype(BF16)
    return [hi, mid, low]


def to_all(copies, axes):
    return lax.all_to_all(copies, axes, 0, 0, tiled=True)


def text_kernel(text_ref, out_ref):
    values = text_ref[...].astype(F32)
    inverse = lax.rsqrt(jnp.sum(values * values, axis=-1, keepdims=True) + EPS)
    low = (values * inverse).astype(BF16)
    n = text_ref.shape[0]
    for k in range(out_ref.shape[0] // n):
        out_ref[k * n : (k + 1) * n] = low


def image_kernel(at_ref, wt_ref, own_ref, fetched_ref, swapped_ref, *refs):
    unit_ref, low_ref, inv_ref, own_unit_ref, cols_ref, feats_ref = refs
    rows = own_ref.shape[0]
    part = rows // 2
    c = at_ref[5]
    feats_ref[:rows] = own_ref[...]
    for k, ref in ((c, fetched_ref), (1 - c, swapped_ref)):
        feats_ref[pl.ds(pl.multiple_of((1 + 2 * k) * rows, 16), rows), :] = ref[:rows]
        feats_ref[pl.ds(pl.multiple_of(2 * rows + k * part, 16), part), :] = ref[rows:]
    head = lax.dot_general(
        wt_ref[...], feats_ref[...], (((1,), (1,)), ((), ())), preferred_element_type=F32
    )
    inv = lax.rsqrt(jnp.sum(head * head, axis=0, keepdims=True) + EPS)
    unit = head * inv
    unit_ref[...] = unit
    low_ref[...] = unit.astype(BF16)
    inv_ref[...] = inv
    cols = cols_ref.shape[0]
    start = pl.multiple_of(at_ref[0] * cols, 16)
    cols_ref[...] = unit_ref[pl.ds(start, cols), :]
    own_unit_ref[...] = unit_ref[pl.ds(start, cols), :rows]


def pairs(par_ref, texts, low_ref, own=None):
    z = par_ref[0] * jnp.dot(texts, low_ref[...], preferred_element_type=F32) + par_ref[1]
    v = z if own is None else jnp.where(own, -z, z)
    e = jnp.exp(-jnp.abs(v))
    one = 1.0 + e
    series = e * (1.0 - e * (0.5 - e * (1.0 / 3.0 - e * (0.25 - e * 0.2))))
    log1p = jnp.where(e < 0.03, series, jnp.log(one))
    soft = jnp.maximum(v, 0.0) + log1p
    s = jnp.where(v >= 0.0, 1.0, e) / one
    slope = (s if own is None else jnp.where(own, -s, s)).astype(BF16)
    return slope, jnp.sum(soft, axis=0, keepdims=True)


def turn(texts, slope):
    return lax.dot_general(texts, slope, (((0,), (0,)), ((), ())), preferred_element_type=F32)


def first_kernel(at_ref, par_ref, own_ref, left_ref, right_ref, low_ref, acc_ref, loss_ref):
    size = (own_ref.shape[0], low_ref.shape[1])
    col = lax.broadcasted_iota(jnp.int32, size, 0) - at_ref[2]
    row = lax.broadcasted_iota(jnp.int32, size, 1) - at_ref[3]
    own = (row == col) & (col >= 0) & (col < at_ref[4])
    slope, loss = pairs(par_ref, own_ref[...], low_ref, own)
    acc_ref[...] = turn(own_ref[...], slope)
    for ref in (left_ref, right_ref):
        slope, more = pairs(par_ref, ref[...], low_ref)
        acc_ref[...] += turn(ref[...], slope)
        loss = loss + more
    loss_ref[...] = loss


def second_kernel(at_ref, par_ref, far_ref, low_ref, unit_ref, acc_ref, loss_ref, keep_ref, send_ref, sum_ref):
    scale = par_ref[0]
    texts = far_ref[...]
    slope, loss = pairs(par_ref, texts, low_ref)
    loss = loss_ref[...] + loss
    total = scale * (acc_ref[...] + turn(texts, slope))
    sum_ref[...] = total
    dots = jnp.sum(unit_ref[...] * total, axis=0, keepdims=True)
    cols = (keep_ref.shape[0] - EXTRA) // 2
    c = at_ref[5]
    for k in range(2):
        mine = pl.multiple_of((2 * k + c) * cols, 16)
        other = pl.multiple_of((2 * k + 1 - c) * cols, 16)
        keep_ref[k * cols : (k + 1) * cols] = sum_ref[pl.ds(mine, cols), :]
        send_ref[k * cols : (k + 1) * cols] = sum_ref[pl.ds(other, cols), :].astype(BF16)
    pack(keep_ref, send_ref, 2 * cols, dots, loss)


def pack(keep_ref, send_ref, at, dots, loss):
    zeros = jnp.zeros((EXTRA - 2, dots.shape[1]), F32)
    keep_ref[at : at + EXTRA] = jnp.concatenate([dots, loss, zeros], axis=0)
    terms = [t.astype(F32) for t in split3(dots) + split3(loss)]
    zeros = jnp.zeros((EXTRA - 6, dots.shape[1]), F32)
    send_ref[at : at + EXTRA] = jnp.concatenate(terms + [zeros], axis=0).astype(BF16)


def unpack(keep_ref, got_ref, at):
    kept = keep_ref[at : at + EXTRA]
    got = got_ref[at : at + EXTRA].astype(F32)
    dots = kept[0:1] + (got[0:1] + got[1:2] + got[2:3])
    loss = kept[1:2] + (got[3:4] + got[4:5] + got[5:6])
    return dots, loss


def middle_kernel(at_ref, keep_ref, got_ref, keep2_ref, send2_ref):
    cols = keep2_ref.shape[0] - EXTRA
    dots, loss = unpack(keep_ref, got_ref, 2 * cols)
    zl = at_ref[6]
    mine = pl.multiple_of(zl * cols, 16)
    other = pl.multiple_of((1 - zl) * cols, 16)
    keep2_ref[:cols] = keep_ref[pl.ds(mine, cols), :] + got_ref[pl.ds(mine, cols), :].astype(F32)
    send2_ref[:cols] = (
        keep_ref[pl.ds(other, cols), :] + got_ref[pl.ds(other, cols), :].astype(F32)
    ).astype(BF16)
    pack(keep2_ref, send2_ref, cols, dots, loss)


def head_kernel(keep_ref, got_ref, unit_ref, inv_ref, feats_ref, flat_ref, *dir_refs):
    cols = keep_ref.shape[0] - EXTRA
    dots, loss = unpack(keep_ref, got_ref, cols)
    total = keep_ref[:cols] + got_ref[:cols].astype(F32)
    back = ((total - unit_ref[...] * dots) * inv_ref[...]).astype(BF16)
    head = jnp.dot(back, feats_ref[...], preferred_element_type=F32).astype(BF16)
    tiles = feats_ref.shape[1] // LANES
    for k in range(tiles):
        flat_ref[k * cols : (k + 1) * cols] = head[:, k * LANES : (k + 1) * LANES]
    part = loss[:, :LANES]
    for k in range(1, loss.shape[1] // LANES):
        part = part + loss[:, k * LANES : (k + 1) * LANES]
    terms = [t.astype(F32) for t in split3(part)]
    tail = jnp.concatenate(terms + [jnp.zeros((EXTRA - 3, LANES), F32)], axis=0)
    at = tiles * cols
    flat_ref[at : at + EXTRA] = tail.astype(BF16)
    flat_ref[at + EXTRA :] = jnp.zeros((flat_ref.shape[0] - at - EXTRA, LANES), BF16)
    low = total.astype(BF16)
    terms = [t.astype(F32) for t in split3(dots)]
    lines = jnp.concatenate(terms + [jnp.zeros((EXTRA - 3, dots.shape[1]), F32)], axis=0).astype(BF16)
    rows = dir_refs[0].shape[1]
    for k, ref in enumerate(dir_refs):
        ref[:cols] = low[:, k * rows : (k + 1) * rows]
        ref[cols:] = lines[:, k * rows : (k + 1) * rows]


def back_kernel(unit_ref, inv_ref, *refs):
    out_ref = refs[-1]
    cols, rows = unit_ref.shape
    total = refs[0][...].astype(F32)
    for ref in refs[1:-1]:
        total = total + ref[...].astype(F32)
    dots = total[cols : cols + 1] + total[cols + 1 : cols + 2] + total[cols + 2 : cols + 3]
    out_ref[...] = ((total[:cols] - unit_ref[...] * dots) * inv_ref[:, :rows]).astype(BF16)


def sum_kernel(parts_ref, after_ref, out_ref):
    total = jnp.sum(parts_ref[...].astype(F32), axis=0)
    for k in range(out_ref.shape[0]):
        out_ref[k] = total


def feat_kernel(at_ref, weight_ref, *refs):
    out_ref, back_ref = refs[-2:]
    cols = refs[0].shape[0]
    for d, ref in enumerate(refs[:-2]):
        back_ref[pl.ds(pl.multiple_of(at_ref[8 + d] * cols, 16), cols), :] = ref[...]
    out_ref[...] = lax.dot_general(
        back_ref[...], weight_ref[...], (((0,), (1,)), ((), ())), preferred_element_type=F32
    ).astype(BF16)


def last_sum_kernel(at_ref, parts_ref, out_ref):
    total = jnp.sum(parts_ref[...], axis=0)
    low = total.astype(BF16)
    first = total[:EXTRA]
    terms = [t.astype(F32) for t in split3(first[0:1] + first[1:2] + first[2:3])]
    row = jnp.concatenate(terms + [jnp.zeros((EXTRA - 3, LANES), F32)], axis=0).astype(BF16)
    first = jnp.where(at_ref[7] > 0, row.astype(F32), first).astype(BF16)
    for k in range(out_ref.shape[0]):
        out_ref[k, :EXTRA] = first
        out_ref[k, EXTRA:] = low[EXTRA:]


def final_kernel(pairs, full_ref, head_ref, loss_ref):
    width, cols = head_ref.shape
    tiles = width // LANES
    for k in range(tiles):
        head_ref[k * LANES : (k + 1) * LANES] = full_ref[k * cols : (k + 1) * cols].astype(F32).T.astype(BF16)
    at = tiles * cols
    total = jnp.sum(full_ref[at : at + EXTRA].astype(F32), axis=0, keepdims=True)
    loss_ref[...] = jnp.sum(total, axis=1, keepdims=True) / pairs


def shift_by(x, axis, step):
    n = lax.axis_size(axis)
    return lax.ppermute(x, axis, [(k, (k + step) % n) for k in range(n)])


def local(img_feat, head_weight, text_embed, log_temp, logit_bias):
    rows, width = img_feat.shape
    quarter = text_embed.shape[0]
    ny, nx, nzh, nzl, nc = (lax.axis_size(a) for a in ("y", "x", "zh", "zl", "c"))
    nrep = nzl * nc
    plane = nx * ny
    cols = width // nrep
    images = nzh * rows
    tiles = width // LANES
    y_at, x_at, zl_at, c_at = (lax.axis_index(a) for a in ("y", "x", "zl", "c"))
    rep_at = zl_at * nc + c_at
    at_loss = tiles * cols
    piece = -(-(at_loss + EXTRA) // (plane * 16)) * 16
    assert at_loss % piece == 0
    at = jnp.stack(
        [
            rep_at,
            0 * rep_at,
            y_at * quarter,
            rep_at * quarter,
            quarter + 0 * rep_at,
            c_at,
            zl_at,
            (y_at * nx + x_at == at_loss // piece).astype(jnp.int32),
        ]
        + [rep_at ^ d for d in range(nrep)]
    ).astype(jnp.int32)
    par = jnp.stack([jnp.exp(log_temp[0]), logit_bias[0]])

    copies = call(text_kernel, shape((ny * quarter, width), BF16), text_embed)
    part = rows // nc
    near = [(z * nc + c, (z + 1 - 2 * c) % nzh * nc + c) for z in range(nzh) for c in range(nc)]
    half_rows = lax.dynamic_slice_in_dim(img_feat, c_at * part, part, 0)
    fetched = jnp.concatenate(
        [lax.ppermute(img_feat, ("zh", "c"), near), shift_by(half_rows, "zh", 2)], axis=0
    )
    own = to_all(copies, "y")
    own, fetched = lax.optimization_barrier((own, fetched))
    far = shift_by(own, "x", 2)
    left = shift_by(own, "x", 1)
    right = shift_by(own, "x", -1)
    swapped = lax.ppermute(fetched, "c", [(0, 1), (1, 0)])

    unit, low, inv, own_unit, col_unit, feats = call(
        image_kernel,
        [
            shape((width, images), F32),
            shape((width, images), BF16),
            shape((1, images), F32),
            shape((cols, rows), F32),
            shape((cols, images), F32),
            shape((images, width), BF16),
        ],
        at,
        head_weight.T,
        img_feat,
        fetched,
        swapped,
        smem=1,
        flops=2 * width * width * images,
    )
    acc, loss_row = call(
        first_kernel,
        [shape((width, images), F32), shape((1, images), F32)],
        at,
        par,
        own,
        left,
        right,
        low,
        smem=2,
        flops=4 * width * images * 3 * own.shape[0],
    )
    keep, send = call(
        second_kernel,
        [shape((2 * cols + EXTRA, images), F32), shape((2 * cols + EXTRA, images), BF16)],
        at,
        par,
        far,
        low,
        unit,
        acc,
        loss_row,
        smem=2,
        flops=4 * width * images * own.shape[0],
        scratch_shapes=[pltpu.VMEM((width, images), F32)],
    )
    got = lax.ppermute(send, "c", [(0, 1), (1, 0)])
    keep2, send2 = call(
        middle_kernel,
        [shape((cols + EXTRA, images), F32), shape((cols + EXTRA, images), BF16)],
        at,
        keep,
        got,
        smem=1,
    )
    got2 = lax.ppermute(send2, "zl", [(0, 1), (1, 0)])
    flat, *dirs = call(
        head_kernel,
        [shape((plane * piece, LANES), BF16)] + [shape((cols + EXTRA, rows), BF16)] * nzh,
        keep2,
        got2,
        col_unit,
        inv,
        feats,
        flops=2 * cols * images * width,
    )

    dirs = [dirs[0]] + [shift_by(dirs[s], "zh", -s) for s in range(1, nzh)]
    back = call(back_kernel, shape((cols, rows), BF16), own_unit, inv, *dirs)

    parts = to_all(flat, ("y", "x")).reshape(plane, piece, LANES)
    part = pl.pallas_call(
        sum_kernel,
        out_shape=shape((nzh, piece, LANES), F32),
        in_specs=[VMEM, pl.BlockSpec(memory_space=pl.ANY)],
        out_specs=VMEM,
    )(parts, back)
    part = to_all(part, "zh")
    low_part = call(last_sum_kernel, shape((plane, piece, LANES), BF16), at, part, smem=1)
    full = to_all(low_part.reshape(plane * piece, LANES), ("y", "x"))
    group = rows * plane * nzh
    head_grad, loss = call(
        functools.partial(final_kernel, float(group) * float(group)),
        [shape((width, cols), BF16), shape((1, 1), F32)],
        full,
    )

    backs = [back]
    for d in range(1, nrep):
        backs.append(lax.ppermute(back, ("zl", "c"), [(k, k ^ d) for k in range(nrep)]))
    feat_grad = call(
        feat_kernel,
        shape((rows, width), BF16),
        at,
        head_weight,
        *backs,
        smem=1,
        flops=2 * rows * width * width,
        scratch_shapes=[pltpu.VMEM((width, rows), BF16)],
    )
    return (loss.reshape(1), feat_grad, head_grad)


def solution(mesh):
    devices = mesh.devices.reshape(8, 4, 4, 2, 2)
    fine = Mesh(devices, ("y", "x", "zh", "zl", "c"))
    batch, rep = (("y", "x", "zh"), ("zl", "c"))
    in_specs = (P(batch, None), P(), P(batch + rep, None), P(), P())
    out_specs = (P(), P(batch, None), P(None, rep))
    return jax.shard_map(local, mesh=fine, in_specs=in_specs, out_specs=out_specs, check_vma=False)
```

```python
import functools

import jax
import jax.numpy as jnp
from jax import lax
from jax.experimental import pallas as pl
from jax.experimental.pallas import tpu as pltpu
from jax.sharding import Mesh
from jax.sharding import PartitionSpec as P

EPS = 1e-06
BF16 = jnp.bfloat16
F32 = jnp.float32
LANES = 128
EXTRA = 16
VMEM = pl.BlockSpec(memory_space=pltpu.VMEM)
SMEM = pl.BlockSpec(memory_space=pltpu.SMEM)


def call(body, outs, *args, smem=0, flops=0, limit=12, **kwargs):
    many = isinstance(outs, (tuple, list))
    specs = [SMEM] * smem + [VMEM] * (len(args) - smem)
    size = sum(a.size * a.dtype.itemsize for a in args)
    return pl.pallas_call(
        body,
        out_shape=outs,
        in_specs=specs,
        out_specs=[VMEM] * len(outs) if many else VMEM,
        cost_estimate=pl.CostEstimate(flops=flops, bytes_accessed=size, transcendentals=0),
        compiler_params=pltpu.CompilerParams(vmem_limit_bytes=limit * 2**20),
        **kwargs,
    )(*args)


def shape(dims, dtype):
    return jax.ShapeDtypeStruct(dims, dtype)


def split3(value):
    hi = value.astype(BF16)
    rest = value - hi.astype(F32)
    mid = rest.astype(BF16)
    low = (rest - mid.astype(F32)).astype(BF16)
    return [hi, mid, low]


def to_all(copies, axes):
    return lax.all_to_all(copies, axes, 0, 0, tiled=True)


def spread(block, axes):
    n = lax.axis_size(axes)
    return to_all(jnp.broadcast_to(block[None], (n,) + block.shape), axes).reshape(n * block.shape[0], block.shape[1])


def text_kernel(text_ref, out_ref):
    values = text_ref[...].astype(F32)
    inverse = lax.rsqrt(jnp.sum(values * values, axis=-1, keepdims=True) + EPS)
    low = (values * inverse).astype(BF16)
    n = text_ref.shape[0]
    for k in range(out_ref.shape[0] // n):
        out_ref[k * n : (k + 1) * n] = low


def image_kernel(at_ref, wt_ref, own_ref, fetched_ref, swapped_ref, *refs):
    unit_ref, low_ref, inv_ref, own_unit_ref, cols_ref, feats_ref = refs
    rows = own_ref.shape[0]
    part = rows // 2
    c = at_ref[5]
    feats_ref[:rows] = own_ref[...]
    for k, ref in ((c, fetched_ref), (1 - c, swapped_ref)):
        feats_ref[pl.ds(pl.multiple_of((1 + 2 * k) * rows, 16), rows), :] = ref[:rows]
        feats_ref[pl.ds(pl.multiple_of(2 * rows + k * part, 16), part), :] = ref[rows:]
    head = lax.dot_general(
        wt_ref[...], feats_ref[...], (((1,), (1,)), ((), ())), preferred_element_type=F32
    )
    inv = lax.rsqrt(jnp.sum(head * head, axis=0, keepdims=True) + EPS)
    unit = head * inv
    unit_ref[...] = unit
    low_ref[...] = unit.astype(BF16)
    inv_ref[...] = inv
    cols = cols_ref.shape[0]
    start = pl.multiple_of(at_ref[0] * cols, 16)
    cols_ref[...] = unit_ref[pl.ds(start, cols), :]
    own_unit_ref[...] = unit_ref[pl.ds(start, cols), :rows]


def pairs(z, own):
    v = jnp.where(own, -z, z)
    e = jnp.exp(-jnp.abs(v))
    one = 1.0 + e
    series = e * (1.0 - e * (0.5 - e * (1.0 / 3.0 - e * (0.25 - e * 0.2))))
    log1p = jnp.where(e < 0.03, series, jnp.log(one))
    soft = jnp.maximum(v, 0.0) + log1p
    s = jnp.where(v >= 0.0, 1.0, e) / one
    slope = jnp.where(own, -s, s).astype(BF16)
    return slope, jnp.sum(soft, axis=0, keepdims=True)


def turn(texts, slope):
    return lax.dot_general(texts, slope, (((0,), (0,)), ((), ())), preferred_element_type=F32)


def pair_kernel(
    steps, at_ref, par_ref, texts_ref, low_in, unit_in, keep_ref, send_ref, held_ref, acc_ref, low_ref, unit_ref, sems
):
    chunk = texts_ref.shape[0] // steps
    low_copy = pltpu.make_async_copy(low_in, low_ref, sems.at[steps])
    unit_copy = pltpu.make_async_copy(unit_in, unit_ref, sems.at[steps + 1])
    low_copy.start()
    copies = []
    for k in range(steps):
        block = pl.ds(k * chunk, chunk)
        copies.append(pltpu.make_async_copy(texts_ref.at[block], held_ref.at[block], sems.at[k]))
        copies[-1].start()
    unit_copy.start()
    low_copy.wait()
    size = (chunk, low_ref.shape[1])
    row = lax.broadcasted_iota(jnp.int32, size, 1) - at_ref[3]

    def logits(k):
        copies[k].wait()
        texts = held_ref[k * chunk : (k + 1) * chunk]
        return par_ref[0] * jnp.dot(texts, low_ref[...], preferred_element_type=F32) + par_ref[1]

    z = logits(0)
    total_loss = None
    for k in range(steps):
        after = logits(k + 1) if k + 1 < steps else None
        col = lax.broadcasted_iota(jnp.int32, size, 0) + (k * chunk - at_ref[2])
        own = (row == col) & (col >= 0) & (col < at_ref[4])
        slope, loss = pairs(z, own)
        term = turn(held_ref[k * chunk : (k + 1) * chunk], slope)
        acc_ref[...] = term if k == 0 else acc_ref[...] + term
        total_loss = loss if k == 0 else total_loss + loss
        z = after
    unit_copy.wait()
    scale = par_ref[0]
    dots = scale * jnp.sum(unit_ref[...] * acc_ref[...], axis=0, keepdims=True)
    cols = (keep_ref.shape[0] - EXTRA) // 2
    c = at_ref[5]
    for k in range(2):
        mine = pl.multiple_of((2 * k + c) * cols, 16)
        other = pl.multiple_of((2 * k + 1 - c) * cols, 16)
        keep_ref[k * cols : (k + 1) * cols] = scale * acc_ref[pl.ds(mine, cols), :]
        send_ref[k * cols : (k + 1) * cols] = (scale * acc_ref[pl.ds(other, cols), :]).astype(BF16)
    pack(keep_ref, send_ref, 2 * cols, dots, total_loss)


def pack(keep_ref, send_ref, at, dots, loss):
    zeros = jnp.zeros((EXTRA - 2, dots.shape[1]), F32)
    keep_ref[at : at + EXTRA] = jnp.concatenate([dots, loss, zeros], axis=0)
    terms = [t.astype(F32) for t in split3(dots) + split3(loss)]
    zeros = jnp.zeros((EXTRA - 6, dots.shape[1]), F32)
    send_ref[at : at + EXTRA] = jnp.concatenate(terms + [zeros], axis=0).astype(BF16)


def unpack(keep_ref, got_ref, at):
    kept = keep_ref[at : at + EXTRA]
    got = got_ref[at : at + EXTRA].astype(F32)
    dots = kept[0:1] + (got[0:1] + got[1:2] + got[2:3])
    loss = kept[1:2] + (got[3:4] + got[4:5] + got[5:6])
    return dots, loss


def middle_kernel(at_ref, keep_ref, got_ref, keep2_ref, send2_ref):
    cols = keep2_ref.shape[0] - EXTRA
    dots, loss = unpack(keep_ref, got_ref, 2 * cols)
    zl = at_ref[6]
    mine = pl.multiple_of(zl * cols, 16)
    other = pl.multiple_of((1 - zl) * cols, 16)
    keep2_ref[:cols] = keep_ref[pl.ds(mine, cols), :] + got_ref[pl.ds(mine, cols), :].astype(F32)
    send2_ref[:cols] = (
        keep_ref[pl.ds(other, cols), :] + got_ref[pl.ds(other, cols), :].astype(F32)
    ).astype(BF16)
    pack(keep2_ref, send2_ref, cols, dots, loss)


def head_kernel(keep_ref, got_ref, unit_ref, inv_ref, feats_ref, flat_ref, *dir_refs):
    cols = keep_ref.shape[0] - EXTRA
    dots, loss = unpack(keep_ref, got_ref, cols)
    total = keep_ref[:cols] + got_ref[:cols].astype(F32)
    back = ((total - unit_ref[...] * dots) * inv_ref[...]).astype(BF16)
    head = jnp.dot(back, feats_ref[...], preferred_element_type=F32).astype(BF16)
    tiles = feats_ref.shape[1] // LANES
    for k in range(tiles):
        flat_ref[k * cols : (k + 1) * cols] = head[:, k * LANES : (k + 1) * LANES]
    part = loss[:, :LANES]
    for k in range(1, loss.shape[1] // LANES):
        part = part + loss[:, k * LANES : (k + 1) * LANES]
    terms = [t.astype(F32) for t in split3(part)]
    tail = jnp.concatenate(terms + [jnp.zeros((EXTRA - 3, LANES), F32)], axis=0)
    at = tiles * cols
    flat_ref[at : at + EXTRA] = tail.astype(BF16)
    flat_ref[at + EXTRA :] = jnp.zeros((flat_ref.shape[0] - at - EXTRA, LANES), BF16)
    low = total.astype(BF16)
    terms = [t.astype(F32) for t in split3(dots)]
    lines = jnp.concatenate(terms + [jnp.zeros((EXTRA - 3, dots.shape[1]), F32)], axis=0).astype(BF16)
    rows = dir_refs[0].shape[1]
    for k, ref in enumerate(dir_refs):
        ref[:cols] = low[:, k * rows : (k + 1) * rows]
        ref[cols:] = lines[:, k * rows : (k + 1) * rows]


def back_kernel(unit_ref, inv_ref, *refs):
    out_ref = refs[-1]
    cols, rows = unit_ref.shape
    total = refs[0][...].astype(F32)
    for ref in refs[1:-1]:
        total = total + ref[...].astype(F32)
    dots = total[cols : cols + 1] + total[cols + 1 : cols + 2] + total[cols + 2 : cols + 3]
    out_ref[...] = ((total[:cols] - unit_ref[...] * dots) * inv_ref[:, :rows]).astype(BF16)


def sum_kernel(parts_ref, after_ref, out_ref):
    total = jnp.sum(parts_ref[...].astype(F32), axis=0)
    for k in range(out_ref.shape[0]):
        out_ref[k] = total


def feat_kernel(at_ref, weight_ref, *refs):
    out_ref, back_ref = refs[-2:]
    cols = refs[0].shape[0]
    for d, ref in enumerate(refs[:-2]):
        back_ref[pl.ds(pl.multiple_of(at_ref[8 + d] * cols, 16), cols), :] = ref[...]
    out_ref[...] = lax.dot_general(
        back_ref[...], weight_ref[...], (((0,), (1,)), ((), ())), preferred_element_type=F32
    ).astype(BF16)


def last_sum_kernel(at_ref, parts_ref, out_ref):
    total = jnp.sum(parts_ref[...], axis=0)
    low = total.astype(BF16)
    first = total[:EXTRA]
    terms = [t.astype(F32) for t in split3(first[0:1] + first[1:2] + first[2:3])]
    row = jnp.concatenate(terms + [jnp.zeros((EXTRA - 3, LANES), F32)], axis=0).astype(BF16)
    first = jnp.where(at_ref[7] > 0, row.astype(F32), first).astype(BF16)
    for k in range(out_ref.shape[0]):
        out_ref[k, :EXTRA] = first
        out_ref[k, EXTRA:] = low[EXTRA:]


def final_kernel(pairs, full_ref, head_ref, loss_ref):
    cols, width = head_ref.shape
    tiles = width // LANES
    for k in range(tiles):
        head_ref[:, k * LANES : (k + 1) * LANES] = full_ref[k * cols : (k + 1) * cols]
    at = tiles * cols
    total = jnp.sum(full_ref[at : at + EXTRA].astype(F32), axis=0, keepdims=True)
    loss_ref[...] = jnp.sum(total, axis=1, keepdims=True) / pairs


def shift_by(x, axis, step):
    n = lax.axis_size(axis)
    return lax.ppermute(x, axis, [(k, (k + step) % n) for k in range(n)])


def local(img_feat, head_weight, text_embed, log_temp, logit_bias):
    rows, width = img_feat.shape
    quarter = text_embed.shape[0]
    ny, nx, nzh, nzl, nc = (lax.axis_size(a) for a in ("y", "x", "zh", "zl", "c"))
    nrep = nzl * nc
    plane = nx * ny
    cols = width // nrep
    images = nzh * rows
    tiles = width // LANES
    y_at, x_at, zl_at, c_at = (lax.axis_index(a) for a in ("y", "x", "zl", "c"))
    rep_at = zl_at * nc + c_at
    at_loss = tiles * cols
    piece = -(-(at_loss + EXTRA) // (plane * 16)) * 16
    assert at_loss % piece == 0
    at = jnp.stack(
        [
            rep_at,
            0 * rep_at,
            (x_at * ny + y_at) * quarter,
            rep_at * quarter,
            quarter + 0 * rep_at,
            c_at,
            zl_at,
            (y_at * nx + x_at == at_loss // piece).astype(jnp.int32),
        ]
        + [rep_at ^ d for d in range(nrep)]
    ).astype(jnp.int32)
    par = jnp.stack([jnp.exp(log_temp[0]), logit_bias[0]])

    copies = call(text_kernel, shape((ny * quarter, width), BF16), text_embed)
    part = rows // nc
    near = [(z * nc + c, (z + 1 - 2 * c) % nzh * nc + c) for z in range(nzh) for c in range(nc)]
    half_rows = lax.dynamic_slice_in_dim(img_feat, c_at * part, part, 0)
    beside = lax.ppermute(img_feat, ("zh", "c"), near)
    own = to_all(copies, "y")
    own, beside = lax.optimization_barrier((own, beside))
    texts = spread(own, "x")
    fetched = jnp.concatenate([beside, shift_by(half_rows, "zh", 2)], axis=0)
    swapped = lax.ppermute(fetched, "c", [(0, 1), (1, 0)])

    unit, low, inv, own_unit, col_unit, feats = call(
        image_kernel,
        [
            shape((width, images), F32),
            shape((width, images), BF16),
            shape((1, images), F32),
            shape((cols, rows), F32),
            shape((cols, images), F32),
            shape((images, width), BF16),
        ],
        at,
        head_weight.T,
        img_feat,
        fetched,
        swapped,
        smem=1,
        flops=2 * width * width * images,
    )
    steps = 4
    keep, send = pl.pallas_call(
        functools.partial(pair_kernel, steps),
        out_shape=[shape((2 * cols + EXTRA, images), F32), shape((2 * cols + EXTRA, images), BF16)],
        in_specs=[SMEM, SMEM] + [pl.BlockSpec(memory_space=pl.ANY)] * 3,
        out_specs=[VMEM, VMEM],
        scratch_shapes=[
            pltpu.VMEM(texts.shape, BF16),
            pltpu.VMEM((width, images), F32),
            pltpu.VMEM((width, images), BF16),
            pltpu.VMEM((width, images), F32),
            pltpu.SemaphoreType.DMA((steps + 2,)),
        ],
        cost_estimate=pl.CostEstimate(
            flops=4 * width * images * texts.shape[0], bytes_accessed=texts.size * 2, transcendentals=0
        ),
        compiler_params=pltpu.CompilerParams(vmem_limit_bytes=20 * 2**20),
    )(at, par, texts, low, unit)
    got = lax.ppermute(send, "c", [(0, 1), (1, 0)])
    keep2, send2 = call(
        middle_kernel,
        [shape((cols + EXTRA, images), F32), shape((cols + EXTRA, images), BF16)],
        at,
        keep,
        got,
        smem=1,
    )
    got2 = lax.ppermute(send2, "zl", [(0, 1), (1, 0)])
    flat, *dirs = call(
        head_kernel,
        [shape((plane * piece, LANES), BF16)] + [shape((cols + EXTRA, rows), BF16)] * nzh,
        keep2,
        got2,
        col_unit,
        inv,
        feats,
        flops=2 * cols * images * width,
    )

    dirs = [dirs[0]] + [shift_by(dirs[s], "zh", -s) for s in range(1, nzh)]
    back = call(back_kernel, shape((cols, rows), BF16), own_unit, inv, *dirs)

    parts = to_all(flat, ("y", "x")).reshape(plane, piece, LANES)
    part = pl.pallas_call(
        sum_kernel,
        out_shape=shape((nzh, piece, LANES), F32),
        in_specs=[VMEM, pl.BlockSpec(memory_space=pl.ANY)],
        out_specs=VMEM,
    )(parts, back)
    part = to_all(part, "zh")
    low_part = call(last_sum_kernel, shape((plane, piece, LANES), BF16), at, part, smem=1)
    full = to_all(low_part.reshape(plane * piece, LANES), ("y", "x"))
    group = rows * plane * nzh
    head_grad, loss = call(
        functools.partial(final_kernel, float(group) * float(group)),
        [shape((cols, width), BF16), shape((1, 1), F32)],
        full,
    )

    backs = [back]
    for d in range(1, nrep):
        backs.append(lax.ppermute(back, ("zl", "c"), [(k, k ^ d) for k in range(nrep)]))
    feat_grad = call(
        feat_kernel,
        shape((rows, width), BF16),
        at,
        head_weight,
        *backs,
        smem=1,
        flops=2 * rows * width * width,
        scratch_shapes=[pltpu.VMEM((width, rows), BF16)],
    )
    return (loss.reshape(1), feat_grad, head_grad.T)


def solution(mesh):
    devices = mesh.devices.reshape(8, 4, 4, 2, 2)
    fine = Mesh(devices, ("y", "x", "zh", "zl", "c"))
    batch, rep = (("y", "x", "zh"), ("zl", "c"))
    in_specs = (P(batch, None), P(), P(batch + rep, None), P(), P())
    out_specs = (P(), P(batch, None), P(None, rep))
    return jax.shard_map(local, mesh=fine, in_specs=in_specs, out_specs=out_specs, check_vma=False)
```

```python
import functools

import jax
import jax.numpy as jnp
from jax import lax
from jax.experimental import pallas as pl
from jax.experimental.pallas import tpu as pltpu
from jax.sharding import Mesh
from jax.sharding import PartitionSpec as P

EPS = 1e-06
BF16 = jnp.bfloat16
F32 = jnp.float32
LANES = 128
EXTRA = 16
VMEM = pl.BlockSpec(memory_space=pltpu.VMEM)
SMEM = pl.BlockSpec(memory_space=pltpu.SMEM)


def call(body, outs, *args, smem=0, flops=0, limit=16, **kwargs):
    many = isinstance(outs, (tuple, list))
    specs = [SMEM] * smem + [VMEM] * (len(args) - smem)
    size = sum(a.size * a.dtype.itemsize for a in args)
    return pl.pallas_call(
        body,
        out_shape=outs,
        in_specs=specs,
        out_specs=[VMEM] * len(outs) if many else VMEM,
        cost_estimate=pl.CostEstimate(flops=flops, bytes_accessed=size, transcendentals=0),
        compiler_params=pltpu.CompilerParams(vmem_limit_bytes=limit * 2**20),
        **kwargs,
    )(*args)


def shape(dims, dtype):
    return jax.ShapeDtypeStruct(dims, dtype)


def split3(value):
    hi = value.astype(BF16)
    rest = value - hi.astype(F32)
    mid = rest.astype(BF16)
    low = (rest - mid.astype(F32)).astype(BF16)
    return [hi, mid, low]


def to_all(copies, axes):
    return lax.all_to_all(copies, axes, 0, 0, tiled=True)


def text_kernel(text_ref, out_ref):
    values = text_ref[...].astype(F32)
    inverse = lax.rsqrt(jnp.sum(values * values, axis=-1, keepdims=True) + EPS)
    low = (values * inverse).astype(BF16)
    n = text_ref.shape[0]
    for k in range(out_ref.shape[0] // n):
        out_ref[k * n : (k + 1) * n] = low


def image_kernel(at_ref, wt_ref, own_ref, fetched_ref, swapped_ref, *refs):
    unit_ref, low_ref, inv_ref, own_unit_ref, cols_ref, feats_ref = refs
    rows = own_ref.shape[0]
    part = rows // 2
    c = at_ref[5]
    feats_ref[:rows] = own_ref[...]
    for k, ref in ((c, fetched_ref), (1 - c, swapped_ref)):
        feats_ref[pl.ds(pl.multiple_of((1 + 2 * k) * rows, 16), rows), :] = ref[:rows]
        feats_ref[pl.ds(pl.multiple_of(2 * rows + k * part, 16), part), :] = ref[rows:]
    head = lax.dot_general(
        wt_ref[...], feats_ref[...], (((1,), (1,)), ((), ())), preferred_element_type=F32
    )
    inv = lax.rsqrt(jnp.sum(head * head, axis=0, keepdims=True) + EPS)
    unit = head * inv
    unit_ref[...] = unit
    low_ref[...] = unit.astype(BF16)
    inv_ref[...] = inv
    cols = cols_ref.shape[0]
    start = pl.multiple_of(at_ref[0] * cols, 16)
    cols_ref[...] = unit_ref[pl.ds(start, cols), :]
    own_unit_ref[...] = unit_ref[pl.ds(start, cols), :rows]


def pairs(par_ref, texts, low_ref, own=None):
    z = par_ref[0] * jnp.dot(texts, low_ref[...], preferred_element_type=F32) + par_ref[1]
    v = z if own is None else jnp.where(own, -z, z)
    e = jnp.exp(-jnp.abs(v))
    one = 1.0 + e
    series = e * (1.0 - e * (0.5 - e * (1.0 / 3.0 - e * (0.25 - e * 0.2))))
    log1p = jnp.where(e < 0.03, series, jnp.log(one))
    soft = jnp.maximum(v, 0.0) + log1p
    s = jnp.where(v >= 0.0, 1.0, e) / one
    slope = (s if own is None else jnp.where(own, -s, s)).astype(BF16)
    return slope, jnp.sum(soft, axis=0, keepdims=True)


def turn(texts, slope):
    return lax.dot_general(texts, slope, (((0,), (0,)), ((), ())), preferred_element_type=F32)


def first_kernel(at_ref, par_ref, own_ref, left_ref, low_ref, acc_ref, loss_ref):
    size = (own_ref.shape[0], low_ref.shape[1])
    col = lax.broadcasted_iota(jnp.int32, size, 0) - at_ref[2]
    row = lax.broadcasted_iota(jnp.int32, size, 1) - at_ref[3]
    own = (row == col) & (col >= 0) & (col < at_ref[4])
    slope, loss = pairs(par_ref, own_ref[...], low_ref, own)
    more_slope, more = pairs(par_ref, left_ref[...], low_ref)
    acc_ref[...] = turn(own_ref[...], slope) + turn(left_ref[...], more_slope)
    loss_ref[...] = loss + more


def second_kernel(at_ref, par_ref, right_ref, far_ref, low_ref, unit_ref, acc_ref, loss_ref, keep_ref, send_ref, sum_ref):
    scale = par_ref[0]
    slope, loss = pairs(par_ref, right_ref[...], low_ref)
    more_slope, more = pairs(par_ref, far_ref[...], low_ref)
    loss = loss_ref[...] + loss + more
    total = scale * (acc_ref[...] + turn(right_ref[...], slope) + turn(far_ref[...], more_slope))
    sum_ref[...] = total
    dots = jnp.sum(unit_ref[...] * total, axis=0, keepdims=True)
    cols = (keep_ref.shape[0] - EXTRA) // 2
    c = at_ref[5]
    for k in range(2):
        mine = pl.multiple_of((2 * k + c) * cols, 16)
        other = pl.multiple_of((2 * k + 1 - c) * cols, 16)
        keep_ref[k * cols : (k + 1) * cols] = sum_ref[pl.ds(mine, cols), :]
        send_ref[k * cols : (k + 1) * cols] = sum_ref[pl.ds(other, cols), :].astype(BF16)
    pack(keep_ref, send_ref, 2 * cols, dots, loss)


def pack(keep_ref, send_ref, at, dots, loss):
    zeros = jnp.zeros((EXTRA - 2, dots.shape[1]), F32)
    keep_ref[at : at + EXTRA] = jnp.concatenate([dots, loss, zeros], axis=0)
    terms = [t.astype(F32) for t in split3(dots) + split3(loss)]
    zeros = jnp.zeros((EXTRA - 6, dots.shape[1]), F32)
    send_ref[at : at + EXTRA] = jnp.concatenate(terms + [zeros], axis=0).astype(BF16)


def unpack(keep_ref, got_ref, at):
    kept = keep_ref[at : at + EXTRA]
    got = got_ref[at : at + EXTRA].astype(F32)
    dots = kept[0:1] + (got[0:1] + got[1:2] + got[2:3])
    loss = kept[1:2] + (got[3:4] + got[4:5] + got[5:6])
    return dots, loss


def middle_kernel(at_ref, keep_ref, got_ref, keep2_ref, send2_ref):
    cols = keep2_ref.shape[0] - EXTRA
    dots, loss = unpack(keep_ref, got_ref, 2 * cols)
    zl = at_ref[6]
    mine = pl.multiple_of(zl * cols, 16)
    other = pl.multiple_of((1 - zl) * cols, 16)
    keep2_ref[:cols] = keep_ref[pl.ds(mine, cols), :] + got_ref[pl.ds(mine, cols), :].astype(F32)
    send2_ref[:cols] = (
        keep_ref[pl.ds(other, cols), :] + got_ref[pl.ds(other, cols), :].astype(F32)
    ).astype(BF16)
    pack(keep2_ref, send2_ref, cols, dots, loss)


def head_kernel(at_loss, keep_ref, got_ref, unit_ref, inv_ref, feats_ref, flat_ref, *dir_refs):
    cols = keep_ref.shape[0] - EXTRA
    dots, loss = unpack(keep_ref, got_ref, cols)
    total = keep_ref[:cols] + got_ref[:cols].astype(F32)
    back = ((total - unit_ref[...] * dots) * inv_ref[...]).astype(BF16)
    head = jnp.dot(back, feats_ref[...], preferred_element_type=F32).astype(BF16)
    tiles = feats_ref.shape[1] // LANES
    for k in range(tiles):
        flat_ref[k * cols : (k + 1) * cols] = head[:, k * LANES : (k + 1) * LANES]
    part = loss[:, :LANES]
    for k in range(1, loss.shape[1] // LANES):
        part = part + loss[:, k * LANES : (k + 1) * LANES]
    terms = [t.astype(F32) for t in split3(part)]
    tail = jnp.concatenate(terms + [jnp.zeros((EXTRA - 3, LANES), F32)], axis=0)
    end = tiles * cols
    flat_ref[end:at_loss] = jnp.zeros((at_loss - end, LANES), BF16)
    flat_ref[at_loss : at_loss + EXTRA] = tail.astype(BF16)
    flat_ref[at_loss + EXTRA :] = jnp.zeros((flat_ref.shape[0] - at_loss - EXTRA, LANES), BF16)
    low = total.astype(BF16)
    terms = [t.astype(F32) for t in split3(dots)]
    lines = jnp.concatenate(terms + [jnp.zeros((EXTRA - 3, dots.shape[1]), F32)], axis=0).astype(BF16)
    rows = dir_refs[0].shape[1]
    for k, ref in enumerate(dir_refs):
        ref[:cols] = low[:, k * rows : (k + 1) * rows]
        ref[cols:] = lines[:, k * rows : (k + 1) * rows]


def back_kernel(unit_ref, inv_ref, *refs):
    out_ref = refs[-1]
    cols, rows = unit_ref.shape
    total = refs[0][...].astype(F32)
    for ref in refs[1:-1]:
        total = total + ref[...].astype(F32)
    dots = total[cols : cols + 1] + total[cols + 1 : cols + 2] + total[cols + 2 : cols + 3]
    out_ref[...] = ((total[:cols] - unit_ref[...] * dots) * inv_ref[:, :rows]).astype(BF16)


def sum_kernel(parts_ref, after_ref, out_ref):
    total = jnp.sum(parts_ref[...].astype(F32), axis=0)
    for k in range(out_ref.shape[0]):
        out_ref[k] = total


def feat_kernel(at_ref, weight_ref, *refs):
    out_ref, back_ref = refs[-2:]
    cols = refs[0].shape[0]
    for d, ref in enumerate(refs[:-2]):
        back_ref[pl.ds(pl.multiple_of(at_ref[8 + d] * cols, 16), cols), :] = ref[...]
    out_ref[...] = lax.dot_general(
        back_ref[...], weight_ref[...], (((0,), (1,)), ((), ())), preferred_element_type=F32
    ).astype(BF16)


def last_sum_kernel(at_ref, parts_ref, out_ref):
    total = jnp.sum(parts_ref[...], axis=0)
    low = total.astype(BF16)
    first = total[:EXTRA]
    terms = [t.astype(F32) for t in split3(first[0:1] + first[1:2] + first[2:3])]
    row = jnp.concatenate(terms + [jnp.zeros((EXTRA - 3, LANES), F32)], axis=0).astype(BF16)
    first = jnp.where(at_ref[7] > 0, row.astype(F32), first).astype(BF16)
    for k in range(out_ref.shape[0]):
        out_ref[k, :EXTRA] = first
        out_ref[k, EXTRA:] = low[EXTRA:]


def final_kernel(at_loss, pairs, full_ref, head_ref, loss_ref):
    cols, width = head_ref.shape
    tiles = width // LANES
    for k in range(tiles):
        head_ref[:, k * LANES : (k + 1) * LANES] = full_ref[k * cols : (k + 1) * cols]
    total = jnp.sum(full_ref[at_loss : at_loss + EXTRA].astype(F32), axis=0, keepdims=True)
    loss_ref[...] = jnp.sum(total, axis=1, keepdims=True) / pairs


def shift_by(x, axis, step):
    n = lax.axis_size(axis)
    return lax.ppermute(x, axis, [(k, (k + step) % n) for k in range(n)])


def local(img_feat, head_weight, text_embed, log_temp, logit_bias):
    rows, width = img_feat.shape
    quarter = text_embed.shape[0]
    ny, nx, nzh, nzl, nc = (lax.axis_size(a) for a in ("y", "x", "zh", "zl", "c"))
    nrep = nzl * nc
    plane = nx * ny
    cols = width // nrep
    images = nzh * rows
    tiles = width // LANES
    y_at, x_at, zl_at, c_at = (lax.axis_index(a) for a in ("y", "x", "zl", "c"))
    rep_at = zl_at * nc + c_at
    piece = -(-(tiles * cols) // (plane * 8)) * 8
    at_loss = -(-(tiles * cols) // piece) * piece
    assert at_loss < plane * piece
    at = jnp.stack(
        [
            rep_at,
            0 * rep_at,
            y_at * quarter,
            rep_at * quarter,
            quarter + 0 * rep_at,
            c_at,
            zl_at,
            (y_at * nx + x_at == at_loss // piece).astype(jnp.int32),
        ]
        + [rep_at ^ d for d in range(nrep)]
    ).astype(jnp.int32)
    par = jnp.stack([jnp.exp(log_temp[0]), logit_bias[0]])

    copies = call(text_kernel, shape((ny * quarter, width), BF16), text_embed)
    part = rows // nc
    def place(z, low, core):
        return (z % nzh * nzl + low) * nc + core

    near = []
    cross = []
    for z in range(nzh):
        near += [(place(z, 1, k), place(z + 1, k, 0)) for k in range(nc)]
        near += [(place(z, 0, k), place(z - 1, k, 1)) for k in range(nc)]
        cross += [(place(z, 1, k), place(z + 2, 0, k)) for k in range(nc)]
        cross += [(place(z, 0, k), place(z - 2, 1, k)) for k in range(nc)]
    half_rows = lax.dynamic_slice_in_dim(img_feat, c_at * part, part, 0)
    line = ("zh", "zl", "c")
    across = lax.ppermute(half_rows, line, cross)
    beside = lax.ppermute(img_feat, line, near)
    fetched = jnp.concatenate([beside, across], axis=0)
    own = to_all(copies, "y")
    own, fetched = lax.optimization_barrier((own, fetched))
    far = shift_by(own, "x", 2)
    left = shift_by(own, "x", 1)
    right = shift_by(own, "x", -1)
    swapped = lax.ppermute(fetched, "c", [(0, 1), (1, 0)])

    unit, low, inv, own_unit, col_unit, feats = call(
        image_kernel,
        [
            shape((width, images), F32),
            shape((width, images), BF16),
            shape((1, images), F32),
            shape((cols, rows), F32),
            shape((cols, images), F32),
            shape((images, width), BF16),
        ],
        at,
        head_weight.T,
        img_feat,
        fetched,
        swapped,
        smem=1,
        flops=2 * width * width * images,
    )
    acc, loss_row = call(
        first_kernel,
        [shape((width, images), F32), shape((1, images), F32)],
        at,
        par,
        own,
        left,
        low,
        smem=2,
        flops=8 * width * images * own.shape[0],
    )
    keep, send = call(
        second_kernel,
        [shape((2 * cols + EXTRA, images), F32), shape((2 * cols + EXTRA, images), BF16)],
        at,
        par,
        right,
        far,
        low,
        unit,
        acc,
        loss_row,
        smem=2,
        flops=8 * width * images * own.shape[0],
        scratch_shapes=[pltpu.VMEM((width, images), F32)],
    )
    got = lax.ppermute(send, "c", [(0, 1), (1, 0)])
    keep2, send2 = call(
        middle_kernel,
        [shape((cols + EXTRA, images), F32), shape((cols + EXTRA, images), BF16)],
        at,
        keep,
        got,
        smem=1,
    )
    got2 = lax.ppermute(send2, "zl", [(0, 1), (1, 0)])
    flat, *dirs = call(
        functools.partial(head_kernel, at_loss),
        [shape((plane * piece, LANES), BF16)] + [shape((cols + EXTRA, rows), BF16)] * nzh,
        keep2,
        got2,
        col_unit,
        inv,
        feats,
        flops=2 * cols * images * width,
    )

    dirs = [dirs[0]] + [shift_by(dirs[s], "zh", -s) for s in range(1, nzh)]
    back = call(back_kernel, shape((cols, rows), BF16), own_unit, inv, *dirs)

    parts = to_all(flat, ("y", "x")).reshape(plane, piece, LANES)
    part = pl.pallas_call(
        sum_kernel,
        out_shape=shape((nzh, piece, LANES), F32),
        in_specs=[VMEM, pl.BlockSpec(memory_space=pl.ANY)],
        out_specs=VMEM,
    )(parts, back)
    part = to_all(part, "zh")
    low_part = call(last_sum_kernel, shape((plane, piece, LANES), BF16), at, part, smem=1)
    full = to_all(low_part.reshape(plane * piece, LANES), ("y", "x"))
    group = rows * plane * nzh
    head_grad, loss = call(
        functools.partial(final_kernel, at_loss, float(group) * float(group)),
        [shape((cols, width), BF16), shape((1, 1), F32)],
        full,
    )

    backs = [back]
    for d in range(1, nrep):
        backs.append(lax.ppermute(back, ("zl", "c"), [(k, k ^ d) for k in range(nrep)]))
    feat_grad = call(
        feat_kernel,
        shape((rows, width), BF16),
        at,
        head_weight,
        *backs,
        smem=1,
        flops=2 * rows * width * width,
        scratch_shapes=[pltpu.VMEM((width, rows), BF16)],
    )
    return (loss.reshape(1), feat_grad, head_grad.T)


def solution(mesh):
    devices = mesh.devices.reshape(8, 4, 4, 2, 2)
    fine = Mesh(devices, ("y", "x", "zh", "zl", "c"))
    batch, rep = (("y", "x", "zh"), ("zl", "c"))
    in_specs = (P(batch, None), P(), P(batch + rep, None), P(), P())
    out_specs = (P(), P(batch, None), P(None, rep))
    return jax.shard_map(local, mesh=fine, in_specs=in_specs, out_specs=out_specs, check_vma=False)
```

```python
import functools

import jax
import jax.numpy as jnp
from jax import lax
from jax.experimental import pallas as pl
from jax.experimental.pallas import tpu as pltpu
from jax.sharding import Mesh
from jax.sharding import PartitionSpec as P

EPS = 1e-06
BF16 = jnp.bfloat16
F32 = jnp.float32
LANES = 128
EXTRA = 16
VMEM = pl.BlockSpec(memory_space=pltpu.VMEM)
SMEM = pl.BlockSpec(memory_space=pltpu.SMEM)


def call(body, outs, *args, smem=0, flops=0, limit=16, **kwargs):
    many = isinstance(outs, (tuple, list))
    specs = [SMEM] * smem + [VMEM] * (len(args) - smem)
    size = sum(a.size * a.dtype.itemsize for a in args)
    return pl.pallas_call(
        body,
        out_shape=outs,
        in_specs=specs,
        out_specs=[VMEM] * len(outs) if many else VMEM,
        cost_estimate=pl.CostEstimate(flops=flops, bytes_accessed=size, transcendentals=0),
        compiler_params=pltpu.CompilerParams(vmem_limit_bytes=limit * 2**20),
        **kwargs,
    )(*args)


def shape(dims, dtype):
    return jax.ShapeDtypeStruct(dims, dtype)


def split3(value):
    hi = value.astype(BF16)
    rest = value - hi.astype(F32)
    mid = rest.astype(BF16)
    low = (rest - mid.astype(F32)).astype(BF16)
    return [hi, mid, low]


def to_all(copies, axes):
    return lax.all_to_all(copies, axes, 0, 0, tiled=True)


def text_kernel(text_ref, out_ref):
    values = text_ref[...].astype(F32)
    inverse = lax.rsqrt(jnp.sum(values * values, axis=-1, keepdims=True) + EPS)
    low = (values * inverse).astype(BF16)
    n = text_ref.shape[0]
    for k in range(out_ref.shape[0] // n):
        out_ref[k * n : (k + 1) * n] = low


def image_kernel(at_ref, wt_ref, own_ref, fetched_ref, swapped_ref, *refs):
    unit_ref, low_ref, inv_ref, own_unit_ref, cols_ref, feats_ref = refs
    rows = own_ref.shape[0]
    low = at_ref[6]
    beside = pl.multiple_of((1 + 2 * low) * rows, 16)
    beyond = pl.multiple_of((3 - 2 * low) * rows, 16)
    feats_ref[:rows] = own_ref[...]

    def place(ends_ref, middle_ref):
        feats_ref[pl.ds(beside, rows), :] = ends_ref[:rows]
        feats_ref[pl.ds(beyond, rows), :] = ends_ref[rows:]
        feats_ref[2 * rows : 3 * rows] = middle_ref[:rows]

    @pl.when(at_ref[5] == 0)
    def _():
        place(fetched_ref, swapped_ref)

    @pl.when(at_ref[5] != 0)
    def _():
        place(swapped_ref, fetched_ref)

    head = lax.dot_general(
        wt_ref[...], feats_ref[...], (((1,), (1,)), ((), ())), preferred_element_type=F32
    )
    inv = lax.rsqrt(jnp.sum(head * head, axis=0, keepdims=True) + EPS)
    unit = head * inv
    unit_ref[...] = unit
    low_ref[...] = unit.astype(BF16)
    inv_ref[...] = inv
    cols = cols_ref.shape[0]
    start = pl.multiple_of(at_ref[0] * cols, 16)
    cols_ref[...] = unit_ref[pl.ds(start, cols), :]
    own_unit_ref[...] = unit_ref[pl.ds(start, cols), :rows]


def pairs(par_ref, texts, low_ref, own=None):
    z = par_ref[0] * jnp.dot(texts, low_ref[...], preferred_element_type=F32) + par_ref[1]
    v = z if own is None else jnp.where(own, -z, z)
    e = jnp.exp(-jnp.abs(v))
    one = 1.0 + e
    series = e * (1.0 - e * (0.5 - e * (1.0 / 3.0 - e * (0.25 - e * 0.2))))
    log1p = jnp.where(e < 0.03, series, jnp.log(one))
    soft = jnp.maximum(v, 0.0) + log1p
    s = jnp.where(v >= 0.0, 1.0, e) / one
    slope = (s if own is None else jnp.where(own, -s, s)).astype(BF16)
    return slope, jnp.sum(soft, axis=0, keepdims=True)


def turn(texts, slope):
    return lax.dot_general(texts, slope, (((0,), (0,)), ((), ())), preferred_element_type=F32)


def first_kernel(at_ref, par_ref, own_ref, left_ref, low_ref, acc_ref, loss_ref):
    size = (own_ref.shape[0], low_ref.shape[1])
    col = lax.broadcasted_iota(jnp.int32, size, 0) - at_ref[2]
    row = lax.broadcasted_iota(jnp.int32, size, 1) - at_ref[3]
    own = (row == col) & (col >= 0) & (col < at_ref[4])
    slope, loss = pairs(par_ref, own_ref[...], low_ref, own)
    more_slope, more = pairs(par_ref, left_ref[...], low_ref)
    acc_ref[...] = turn(own_ref[...], slope) + turn(left_ref[...], more_slope)
    loss_ref[...] = loss + more


def second_kernel(at_ref, par_ref, right_ref, far_ref, low_ref, unit_ref, acc_ref, loss_ref, keep_ref, send_ref, sum_ref):
    scale = par_ref[0]
    slope, loss = pairs(par_ref, right_ref[...], low_ref)
    more_slope, more = pairs(par_ref, far_ref[...], low_ref)
    loss = loss_ref[...] + loss + more
    total = scale * (acc_ref[...] + turn(right_ref[...], slope) + turn(far_ref[...], more_slope))
    sum_ref[...] = total
    dots = jnp.sum(unit_ref[...] * total, axis=0, keepdims=True)
    cols = (keep_ref.shape[0] - EXTRA) // 2
    c = at_ref[5]
    for k in range(2):
        mine = pl.multiple_of((2 * k + c) * cols, 16)
        other = pl.multiple_of((2 * k + 1 - c) * cols, 16)
        keep_ref[k * cols : (k + 1) * cols] = sum_ref[pl.ds(mine, cols), :]
        send_ref[k * cols : (k + 1) * cols] = sum_ref[pl.ds(other, cols), :].astype(BF16)
    pack(keep_ref, send_ref, 2 * cols, dots, loss)


def pack(keep_ref, send_ref, at, dots, loss):
    zeros = jnp.zeros((EXTRA - 2, dots.shape[1]), F32)
    keep_ref[at : at + EXTRA] = jnp.concatenate([dots, loss, zeros], axis=0)
    terms = [t.astype(F32) for t in split3(dots) + split3(loss)]
    zeros = jnp.zeros((EXTRA - 6, dots.shape[1]), F32)
    send_ref[at : at + EXTRA] = jnp.concatenate(terms + [zeros], axis=0).astype(BF16)


def unpack(keep_ref, got_ref, at):
    kept = keep_ref[at : at + EXTRA]
    got = got_ref[at : at + EXTRA].astype(F32)
    dots = kept[0:1] + (got[0:1] + got[1:2] + got[2:3])
    loss = kept[1:2] + (got[3:4] + got[4:5] + got[5:6])
    return dots, loss


def middle_kernel(at_ref, keep_ref, got_ref, keep2_ref, send2_ref):
    cols = keep2_ref.shape[0] - EXTRA
    dots, loss = unpack(keep_ref, got_ref, 2 * cols)
    zl = at_ref[6]
    mine = pl.multiple_of(zl * cols, 16)
    other = pl.multiple_of((1 - zl) * cols, 16)
    keep2_ref[:cols] = keep_ref[pl.ds(mine, cols), :] + got_ref[pl.ds(mine, cols), :].astype(F32)
    send2_ref[:cols] = (
        keep_ref[pl.ds(other, cols), :] + got_ref[pl.ds(other, cols), :].astype(F32)
    ).astype(BF16)
    pack(keep2_ref, send2_ref, cols, dots, loss)


def head_kernel(at_loss, keep_ref, got_ref, unit_ref, inv_ref, feats_ref, flat_ref, *dir_refs):
    cols = keep_ref.shape[0] - EXTRA
    dots, loss = unpack(keep_ref, got_ref, cols)
    total = keep_ref[:cols] + got_ref[:cols].astype(F32)
    back = ((total - unit_ref[...] * dots) * inv_ref[...]).astype(BF16)
    head = jnp.dot(back, feats_ref[...], preferred_element_type=F32).astype(BF16)
    tiles = feats_ref.shape[1] // LANES
    for k in range(tiles):
        flat_ref[k * cols : (k + 1) * cols] = head[:, k * LANES : (k + 1) * LANES]
    part = loss[:, :LANES]
    for k in range(1, loss.shape[1] // LANES):
        part = part + loss[:, k * LANES : (k + 1) * LANES]
    terms = [t.astype(F32) for t in split3(part)]
    tail = jnp.concatenate(terms + [jnp.zeros((EXTRA - 3, LANES), F32)], axis=0)
    end = tiles * cols
    flat_ref[end:at_loss] = jnp.zeros((at_loss - end, LANES), BF16)
    flat_ref[at_loss : at_loss + EXTRA] = tail.astype(BF16)
    flat_ref[at_loss + EXTRA :] = jnp.zeros((flat_ref.shape[0] - at_loss - EXTRA, LANES), BF16)
    low = total.astype(BF16)
    terms = [t.astype(F32) for t in split3(dots)]
    lines = jnp.concatenate(terms + [jnp.zeros((EXTRA - 3, dots.shape[1]), F32)], axis=0).astype(BF16)
    rows = dir_refs[0].shape[1]
    for k, ref in enumerate(dir_refs):
        ref[:cols] = low[:, k * rows : (k + 1) * rows]
        ref[cols:] = lines[:, k * rows : (k + 1) * rows]


def back_kernel(unit_ref, inv_ref, *refs):
    out_ref = refs[-1]
    cols, rows = unit_ref.shape
    total = refs[0][...].astype(F32)
    for ref in refs[1:-1]:
        total = total + ref[...].astype(F32)
    dots = total[cols : cols + 1] + total[cols + 1 : cols + 2] + total[cols + 2 : cols + 3]
    out_ref[...] = ((total[:cols] - unit_ref[...] * dots) * inv_ref[:, :rows]).astype(BF16)


def sum_kernel(parts_ref, after_ref, out_ref):
    total = jnp.sum(parts_ref[...].astype(F32), axis=0)
    for k in range(out_ref.shape[0]):
        out_ref[k] = total


def feat_kernel(at_ref, weight_ref, *refs):
    out_ref, back_ref = refs[-2:]
    cols = refs[0].shape[0]
    for d, ref in enumerate(refs[:-2]):
        back_ref[pl.ds(pl.multiple_of(at_ref[8 + d] * cols, 16), cols), :] = ref[...]
    out_ref[...] = lax.dot_general(
        back_ref[...], weight_ref[...], (((0,), (1,)), ((), ())), preferred_element_type=F32
    ).astype(BF16)


def last_sum_kernel(at_ref, parts_ref, out_ref):
    total = jnp.sum(parts_ref[...], axis=0)
    low = total.astype(BF16)
    first = total[:EXTRA]
    terms = [t.astype(F32) for t in split3(first[0:1] + first[1:2] + first[2:3])]
    row = jnp.concatenate(terms + [jnp.zeros((EXTRA - 3, LANES), F32)], axis=0).astype(BF16)
    first = jnp.where(at_ref[7] > 0, row.astype(F32), first).astype(BF16)
    for k in range(out_ref.shape[0]):
        out_ref[k, :EXTRA] = first
        out_ref[k, EXTRA:] = low[EXTRA:]


def final_kernel(at_loss, pairs, full_ref, head_ref, loss_ref):
    cols, width = head_ref.shape
    tiles = width // LANES
    for k in range(tiles):
        head_ref[:, k * LANES : (k + 1) * LANES] = full_ref[k * cols : (k + 1) * cols]
    total = jnp.sum(full_ref[at_loss : at_loss + EXTRA].astype(F32), axis=0, keepdims=True)
    loss_ref[...] = jnp.sum(total, axis=1, keepdims=True) / pairs


def shift_by(x, axis, step):
    n = lax.axis_size(axis)
    return lax.ppermute(x, axis, [(k, (k + step) % n) for k in range(n)])


def local(img_feat, head_weight, text_embed, log_temp, logit_bias):
    rows, width = img_feat.shape
    quarter = text_embed.shape[0]
    ny, nx, nzh, nzl, nc = (lax.axis_size(a) for a in ("y", "x", "zh", "zl", "c"))
    nrep = nzl * nc
    plane = nx * ny
    cols = width // nrep
    images = nzh * rows
    tiles = width // LANES
    y_at, x_at, zl_at, c_at = (lax.axis_index(a) for a in ("y", "x", "zl", "c"))
    rep_at = zl_at * nc + c_at
    piece = -(-(tiles * cols) // (plane * 8)) * 8
    at_loss = -(-(tiles * cols) // piece) * piece
    assert at_loss < plane * piece
    at = jnp.stack(
        [
            rep_at,
            0 * rep_at,
            y_at * quarter,
            rep_at * quarter,
            quarter + 0 * rep_at,
            c_at,
            zl_at,
            (y_at * nx + x_at == at_loss // piece).astype(jnp.int32),
        ]
        + [rep_at ^ d for d in range(nrep)]
    ).astype(jnp.int32)
    par = jnp.stack([jnp.exp(log_temp[0]), logit_bias[0]])

    copies = call(text_kernel, shape((ny * quarter, width), BF16), text_embed)
    def place(z, low, core):
        return (z % nzh * nzl + low) * nc + core

    line = ("zh", "zl", "c")
    fetch = []
    for z in range(nzh):
        fetch += [(place(z - 1, 1, 0), place(z, 0, 0)), (place(z + 1, 0, 0), place(z, 1, 0))]
        fetch += [(place(z - 2, 1, 1), place(z, 0, 1)), (place(z + 2, 0, 1), place(z, 1, 1))]
    fetched = lax.ppermute(img_feat, line, fetch)
    across = lax.ppermute(fetched, ("zl", "c"), [(0, 2), (2, 0)])
    own = to_all(copies, "y")
    own, fetched, across = lax.optimization_barrier((own, fetched, across))
    fetched = jnp.concatenate([fetched, across], axis=0)
    swapped = lax.ppermute(fetched, "c", [(0, 1), (1, 0)])
    far = shift_by(own, "x", 2)
    left = shift_by(own, "x", 1)
    right = shift_by(own, "x", -1)

    unit, low, inv, own_unit, col_unit, feats = call(
        image_kernel,
        [
            shape((width, images), F32),
            shape((width, images), BF16),
            shape((1, images), F32),
            shape((cols, rows), F32),
            shape((cols, images), F32),
            shape((images, width), BF16),
        ],
        at,
        head_weight.T,
        img_feat,
        fetched,
        swapped,
        smem=1,
        flops=2 * width * width * images,
    )
    acc, loss_row = call(
        first_kernel,
        [shape((width, images), F32), shape((1, images), F32)],
        at,
        par,
        own,
        left,
        low,
        smem=2,
        flops=8 * width * images * own.shape[0],
    )
    keep, send = call(
        second_kernel,
        [shape((2 * cols + EXTRA, images), F32), shape((2 * cols + EXTRA, images), BF16)],
        at,
        par,
        right,
        far,
        low,
        unit,
        acc,
        loss_row,
        smem=2,
        flops=8 * width * images * own.shape[0],
        scratch_shapes=[pltpu.VMEM((width, images), F32)],
    )
    got = lax.ppermute(send, "c", [(0, 1), (1, 0)])
    keep2, send2 = call(
        middle_kernel,
        [shape((cols + EXTRA, images), F32), shape((cols + EXTRA, images), BF16)],
        at,
        keep,
        got,
        smem=1,
    )
    got2 = lax.ppermute(send2, "zl", [(0, 1), (1, 0)])
    flat, *dirs = call(
        functools.partial(head_kernel, at_loss),
        [shape((plane * piece, LANES), BF16)] + [shape((cols + EXTRA, rows), BF16)] * nzh,
        keep2,
        got2,
        col_unit,
        inv,
        feats,
        flops=2 * cols * images * width,
    )

    dirs = [dirs[0]] + [shift_by(dirs[s], "zh", -s) for s in range(1, nzh)]
    back = call(back_kernel, shape((cols, rows), BF16), own_unit, inv, *dirs)

    parts = to_all(flat, ("y", "x")).reshape(plane, piece, LANES)
    part = pl.pallas_call(
        sum_kernel,
        out_shape=shape((nzh, piece, LANES), F32),
        in_specs=[VMEM, pl.BlockSpec(memory_space=pl.ANY)],
        out_specs=VMEM,
    )(parts, back)
    part = to_all(part, "zh")
    low_part = call(last_sum_kernel, shape((plane, piece, LANES), BF16), at, part, smem=1)
    full = to_all(low_part.reshape(plane * piece, LANES), ("y", "x"))
    group = rows * plane * nzh
    head_grad, loss = call(
        functools.partial(final_kernel, at_loss, float(group) * float(group)),
        [shape((cols, width), BF16), shape((1, 1), F32)],
        full,
    )

    backs = [back]
    for d in range(1, nrep):
        backs.append(lax.ppermute(back, ("zl", "c"), [(k, k ^ d) for k in range(nrep)]))
    feat_grad = call(
        feat_kernel,
        shape((rows, width), BF16),
        at,
        head_weight,
        *backs,
        smem=1,
        flops=2 * rows * width * width,
        scratch_shapes=[pltpu.VMEM((width, rows), BF16)],
    )
    return (loss.reshape(1), feat_grad, head_grad.T)


def solution(mesh):
    devices = mesh.devices.reshape(8, 4, 4, 2, 2)
    fine = Mesh(devices, ("y", "x", "zh", "zl", "c"))
    batch, rep = (("y", "x", "zh"), ("zl", "c"))
    in_specs = (P(batch, None), P(), P(batch + rep, None), P(), P())
    out_specs = (P(), P(batch, None), P(None, rep))
    return jax.shard_map(local, mesh=fine, in_specs=in_specs, out_specs=out_specs, check_vma=False)
```

```python
import functools

import jax
import jax.numpy as jnp
from jax import lax
from jax.experimental import pallas as pl
from jax.experimental.pallas import tpu as pltpu
from jax.sharding import Mesh
from jax.sharding import PartitionSpec as P

EPS = 1e-06
BF16 = jnp.bfloat16
F32 = jnp.float32
LANES = 128
EXTRA = 16
VMEM = pl.BlockSpec(memory_space=pltpu.VMEM)
SMEM = pl.BlockSpec(memory_space=pltpu.SMEM)


def call(body, outs, *args, smem=0, flops=0, limit=16, **kwargs):
    many = isinstance(outs, (tuple, list))
    specs = [SMEM] * smem + [VMEM] * (len(args) - smem)
    size = sum(a.size * a.dtype.itemsize for a in args)
    return pl.pallas_call(
        body,
        out_shape=outs,
        in_specs=specs,
        out_specs=[VMEM] * len(outs) if many else VMEM,
        cost_estimate=pl.CostEstimate(flops=flops, bytes_accessed=size, transcendentals=0),
        compiler_params=pltpu.CompilerParams(vmem_limit_bytes=limit * 2**20),
        **kwargs,
    )(*args)


def shape(dims, dtype):
    return jax.ShapeDtypeStruct(dims, dtype)


def split3(value):
    hi = value.astype(BF16)
    rest = value - hi.astype(F32)
    mid = rest.astype(BF16)
    low = (rest - mid.astype(F32)).astype(BF16)
    return [hi, mid, low]


def to_all(copies, axes):
    return lax.all_to_all(copies, axes, 0, 0, tiled=True)


def text_kernel(text_ref, out_ref):
    values = text_ref[...].astype(F32)
    inverse = lax.rsqrt(jnp.sum(values * values, axis=-1, keepdims=True) + EPS)
    low = (values * inverse).astype(BF16)
    n = text_ref.shape[0]
    for k in range(out_ref.shape[0] // n):
        out_ref[k * n : (k + 1) * n] = low


def image_kernel(at_ref, wt_ref, own_ref, fetched_ref, swapped_ref, *refs):
    unit_ref, low_ref, inv_ref, own_unit_ref, cols_ref, feats_ref = refs
    rows = own_ref.shape[0]
    part = rows // 2
    c = at_ref[5]
    feats_ref[:rows] = own_ref[...]
    for k, ref in ((c, fetched_ref), (1 - c, swapped_ref)):
        feats_ref[pl.ds(pl.multiple_of((1 + 2 * k) * rows, 16), rows), :] = ref[:rows]
        feats_ref[pl.ds(pl.multiple_of(2 * rows + k * part, 16), part), :] = ref[rows:]
    head = lax.dot_general(
        wt_ref[...], feats_ref[...], (((1,), (1,)), ((), ())), preferred_element_type=F32
    )
    inv = lax.rsqrt(jnp.sum(head * head, axis=0, keepdims=True) + EPS)
    unit = head * inv
    unit_ref[...] = unit
    low_ref[...] = unit.astype(BF16)
    inv_ref[...] = inv
    cols = cols_ref.shape[0]
    start = pl.multiple_of(at_ref[0] * cols, 16)
    cols_ref[...] = unit_ref[pl.ds(start, cols), :]
    own_unit_ref[...] = unit_ref[pl.ds(start, cols), :rows]


def pairs(par_ref, texts, low_ref, own=None):
    z = par_ref[0] * jnp.dot(texts, low_ref[...], preferred_element_type=F32) + par_ref[1]
    v = z if own is None else jnp.where(own, -z, z)
    e = jnp.exp(-jnp.abs(v))
    one = 1.0 + e
    series = e * (1.0 - e * (0.5 - e * (1.0 / 3.0 - e * (0.25 - e * 0.2))))
    log1p = jnp.where(e < 0.03, series, jnp.log(one))
    soft = jnp.maximum(v, 0.0) + log1p
    s = jnp.where(v >= 0.0, 1.0, e) / one
    slope = (s if own is None else jnp.where(own, -s, s)).astype(BF16)
    return slope, jnp.sum(soft, axis=0, keepdims=True)


def turn(texts, slope):
    return lax.dot_general(texts, slope, (((0,), (0,)), ((), ())), preferred_element_type=F32)


def first_kernel(at_ref, par_ref, own_ref, left_ref, low_ref, acc_ref, loss_ref):
    size = (own_ref.shape[0], low_ref.shape[1])
    col = lax.broadcasted_iota(jnp.int32, size, 0) - at_ref[2]
    row = lax.broadcasted_iota(jnp.int32, size, 1) - at_ref[3]
    own = (row == col) & (col >= 0) & (col < at_ref[4])
    slope, loss = pairs(par_ref, own_ref[...], low_ref, own)
    more_slope, more = pairs(par_ref, left_ref[...], low_ref)
    acc_ref[...] = turn(own_ref[...], slope) + turn(left_ref[...], more_slope)
    loss_ref[...] = loss + more


def second_kernel(at_ref, par_ref, right_ref, far_ref, low_ref, unit_ref, acc_ref, loss_ref, keep_ref, send_ref, sum_ref):
    scale = par_ref[0]
    slope, loss = pairs(par_ref, right_ref[...], low_ref)
    more_slope, more = pairs(par_ref, far_ref[...], low_ref)
    loss = loss_ref[...] + loss + more
    total = scale * (acc_ref[...] + turn(right_ref[...], slope) + turn(far_ref[...], more_slope))
    sum_ref[...] = total
    dots = jnp.sum(unit_ref[...] * total, axis=0, keepdims=True)
    cols = (keep_ref.shape[0] - EXTRA) // 2
    c = at_ref[5]
    for k in range(2):
        mine = pl.multiple_of((2 * k + c) * cols, 16)
        other = pl.multiple_of((2 * k + 1 - c) * cols, 16)
        keep_ref[k * cols : (k + 1) * cols] = sum_ref[pl.ds(mine, cols), :]
        send_ref[k * cols : (k + 1) * cols] = sum_ref[pl.ds(other, cols), :].astype(BF16)
    pack(keep_ref, send_ref, 2 * cols, dots, loss)


def pack(keep_ref, send_ref, at, dots, loss):
    zeros = jnp.zeros((EXTRA - 2, dots.shape[1]), F32)
    keep_ref[at : at + EXTRA] = jnp.concatenate([dots, loss, zeros], axis=0)
    terms = [t.astype(F32) for t in split3(dots) + split3(loss)]
    zeros = jnp.zeros((EXTRA - 6, dots.shape[1]), F32)
    send_ref[at : at + EXTRA] = jnp.concatenate(terms + [zeros], axis=0).astype(BF16)


def unpack(keep_ref, got_ref, at):
    kept = keep_ref[at : at + EXTRA]
    got = got_ref[at : at + EXTRA].astype(F32)
    dots = kept[0:1] + (got[0:1] + got[1:2] + got[2:3])
    loss = kept[1:2] + (got[3:4] + got[4:5] + got[5:6])
    return dots, loss


def middle_kernel(at_ref, keep_ref, got_ref, keep2_ref, send2_ref):
    cols = keep2_ref.shape[0] - EXTRA
    dots, loss = unpack(keep_ref, got_ref, 2 * cols)
    zl = at_ref[6]
    mine = pl.multiple_of(zl * cols, 16)
    other = pl.multiple_of((1 - zl) * cols, 16)
    keep2_ref[:cols] = keep_ref[pl.ds(mine, cols), :] + got_ref[pl.ds(mine, cols), :].astype(F32)
    send2_ref[:cols] = (
        keep_ref[pl.ds(other, cols), :] + got_ref[pl.ds(other, cols), :].astype(F32)
    ).astype(BF16)
    pack(keep2_ref, send2_ref, cols, dots, loss)


def head_kernel(at_loss, keep_ref, got_ref, unit_ref, inv_ref, feats_ref, flat_ref, *dir_refs):
    cols = keep_ref.shape[0] - EXTRA
    dots, loss = unpack(keep_ref, got_ref, cols)
    total = keep_ref[:cols] + got_ref[:cols].astype(F32)
    back = ((total - unit_ref[...] * dots) * inv_ref[...]).astype(BF16)
    head = jnp.dot(back, feats_ref[...], preferred_element_type=F32).astype(BF16)
    tiles = feats_ref.shape[1] // LANES
    for k in range(tiles):
        flat_ref[k * cols : (k + 1) * cols] = head[:, k * LANES : (k + 1) * LANES]
    part = loss[:, :LANES]
    for k in range(1, loss.shape[1] // LANES):
        part = part + loss[:, k * LANES : (k + 1) * LANES]
    terms = [t.astype(F32) for t in split3(part)]
    tail = jnp.concatenate(terms + [jnp.zeros((EXTRA - 3, LANES), F32)], axis=0)
    end = tiles * cols
    flat_ref[end:at_loss] = jnp.zeros((at_loss - end, LANES), BF16)
    flat_ref[at_loss : at_loss + EXTRA] = tail.astype(BF16)
    flat_ref[at_loss + EXTRA :] = jnp.zeros((flat_ref.shape[0] - at_loss - EXTRA, LANES), BF16)
    low = total.astype(BF16)
    terms = [t.astype(F32) for t in split3(dots)]
    lines = jnp.concatenate(terms + [jnp.zeros((EXTRA - 3, dots.shape[1]), F32)], axis=0).astype(BF16)
    rows = dir_refs[0].shape[1]
    for k, ref in enumerate(dir_refs):
        ref[:cols] = low[:, k * rows : (k + 1) * rows]
        ref[cols:] = lines[:, k * rows : (k + 1) * rows]


def back_kernel(unit_ref, inv_ref, *refs):
    out_ref = refs[-1]
    cols, rows = unit_ref.shape
    total = refs[0][...].astype(F32)
    for ref in refs[1:-1]:
        total = total + ref[...].astype(F32)
    dots = total[cols : cols + 1] + total[cols + 1 : cols + 2] + total[cols + 2 : cols + 3]
    out_ref[...] = ((total[:cols] - unit_ref[...] * dots) * inv_ref[:, :rows]).astype(BF16)


def sum_kernel(parts_ref, after_ref, out_ref):
    total = jnp.sum(parts_ref[...].astype(F32), axis=0)
    for k in range(out_ref.shape[0]):
        out_ref[k] = total


def feat_kernel(at_ref, weight_ref, *refs):
    out_ref, back_ref = refs[-2:]
    cols = refs[0].shape[0]
    for d, ref in enumerate(refs[:-2]):
        back_ref[pl.ds(pl.multiple_of(at_ref[8 + d] * cols, 16), cols), :] = ref[...]
    out_ref[...] = lax.dot_general(
        back_ref[...], weight_ref[...], (((0,), (1,)), ((), ())), preferred_element_type=F32
    ).astype(BF16)


def last_sum_kernel(at_ref, parts_ref, out_ref):
    total = jnp.sum(parts_ref[...], axis=0)
    low = total.astype(BF16)
    first = total[:EXTRA]
    terms = [t.astype(F32) for t in split3(first[0:1] + first[1:2] + first[2:3])]
    row = jnp.concatenate(terms + [jnp.zeros((EXTRA - 3, LANES), F32)], axis=0).astype(BF16)
    first = jnp.where(at_ref[7] > 0, row.astype(F32), first).astype(BF16)
    for k in range(out_ref.shape[0]):
        out_ref[k, :EXTRA] = first
        out_ref[k, EXTRA:] = low[EXTRA:]


def final_kernel(at_loss, pairs, full_ref, head_ref, loss_ref):
    cols, width = head_ref.shape
    tiles = width // LANES
    for k in range(tiles):
        head_ref[:, k * LANES : (k + 1) * LANES] = full_ref[k * cols : (k + 1) * cols]
    total = jnp.sum(full_ref[at_loss : at_loss + EXTRA].astype(F32), axis=0, keepdims=True)
    loss_ref[...] = jnp.sum(total, axis=1, keepdims=True) / pairs


def shift_by(x, axis, step):
    n = lax.axis_size(axis)
    return lax.ppermute(x, axis, [(k, (k + step) % n) for k in range(n)])


def local(img_feat, head_weight, text_embed, log_temp, logit_bias):
    rows, width = img_feat.shape
    quarter = text_embed.shape[0]
    ny, nx, nzh, nzl, nc = (lax.axis_size(a) for a in ("y", "x", "zh", "zl", "c"))
    nrep = nzl * nc
    plane = nx * ny
    cols = width // nrep
    images = nzh * rows
    tiles = width // LANES
    y_at, x_at, zl_at, c_at = (lax.axis_index(a) for a in ("y", "x", "zl", "c"))
    rep_at = zl_at * nc + c_at
    piece = -(-(tiles * cols) // (plane * 8)) * 8
    at_loss = -(-(tiles * cols) // piece) * piece
    assert at_loss < plane * piece
    at = jnp.stack(
        [
            rep_at,
            0 * rep_at,
            y_at * quarter,
            rep_at * quarter,
            quarter + 0 * rep_at,
            c_at,
            zl_at,
            (y_at * nx + x_at == at_loss // piece).astype(jnp.int32),
        ]
        + [rep_at ^ d for d in range(nrep)]
    ).astype(jnp.int32)
    par = jnp.stack([jnp.exp(log_temp[0]), logit_bias[0]])

    copies = call(text_kernel, shape((ny * quarter, width), BF16), text_embed)
    part = rows // nc
    def place(z, low, core):
        return (z % nzh * nzl + low) * nc + core

    near = []
    cross = []
    for z in range(nzh):
        near += [(place(z, 1, k), place(z + 1, k, 0)) for k in range(nc)]
        near += [(place(z, 0, k), place(z - 1, k, 1)) for k in range(nc)]
        cross += [(place(z, 1, k), place(z + 2, 0, k)) for k in range(nc)]
        cross += [(place(z, 0, k), place(z - 2, 1, k)) for k in range(nc)]
    half_rows = lax.dynamic_slice_in_dim(img_feat, c_at * part, part, 0)
    line = ("zh", "zl", "c")
    across = lax.ppermute(half_rows, line, cross)
    beside = lax.ppermute(img_feat, line, near)
    fetched = jnp.concatenate([beside, across], axis=0)
    own = to_all(copies, "y")
    far = shift_by(own, "x", 2)
    left = shift_by(own, "x", 1)
    right = shift_by(own, "x", -1)
    swapped = lax.ppermute(fetched, "c", [(0, 1), (1, 0)])

    unit, low, inv, own_unit, col_unit, feats = call(
        image_kernel,
        [
            shape((width, images), F32),
            shape((width, images), BF16),
            shape((1, images), F32),
            shape((cols, rows), F32),
            shape((cols, images), F32),
            shape((images, width), BF16),
        ],
        at,
        head_weight.T,
        img_feat,
        fetched,
        swapped,
        smem=1,
        flops=2 * width,
    )
    acc, loss_row = call(
        first_kernel,
        [shape((width, images), F32), shape((1, images), F32)],
        at,
        par,
        own,
        left,
        low,
        smem=2,
        flops=8 * width * images * own.shape[0],
    )
    keep, send = call(
        second_kernel,
        [shape((2 * cols + EXTRA, images), F32), shape((2 * cols + EXTRA, images), BF16)],
        at,
        par,
        right,
        far,
        low,
        unit,
        acc,
        loss_row,
        smem=2,
        flops=8 * width * images * own.shape[0],
        scratch_shapes=[pltpu.VMEM((width, images), F32)],
    )
    got = lax.ppermute(send, "c", [(0, 1), (1, 0)])
    keep2, send2 = call(
        middle_kernel,
        [shape((cols + EXTRA, images), F32), shape((cols + EXTRA, images), BF16)],
        at,
        keep,
        got,
        smem=1,
    )
    got2 = lax.ppermute(send2, "zl", [(0, 1), (1, 0)])
    flat, *dirs = call(
        functools.partial(head_kernel, at_loss),
        [shape((plane * piece, LANES), BF16)] + [shape((cols + EXTRA, rows), BF16)] * nzh,
        keep2,
        got2,
        col_unit,
        inv,
        feats,
        flops=2 * cols * images * width,
    )

    dirs = [dirs[0]] + [shift_by(dirs[s], "zh", -s) for s in range(1, nzh)]
    back = call(back_kernel, shape((cols, rows), BF16), own_unit, inv, *dirs)

    parts = to_all(flat, ("y", "x")).reshape(plane, piece, LANES)
    part = pl.pallas_call(
        sum_kernel,
        out_shape=shape((nzh, piece, LANES), F32),
        in_specs=[VMEM, pl.BlockSpec(memory_space=pl.ANY)],
        out_specs=VMEM,
    )(parts, back)
    part = to_all(part, "zh")
    low_part = call(last_sum_kernel, shape((plane, piece, LANES), BF16), at, part, smem=1)
    full = to_all(low_part.reshape(plane * piece, LANES), ("y", "x"))
    group = rows * plane * nzh
    head_grad, loss = call(
        functools.partial(final_kernel, at_loss, float(group) * float(group)),
        [shape((cols, width), BF16), shape((1, 1), F32)],
        full,
    )

    backs = [back]
    for d in range(1, nrep):
        backs.append(lax.ppermute(back, ("zl", "c"), [(k, k ^ d) for k in range(nrep)]))
    feat_grad = call(
        feat_kernel,
        shape((rows, width), BF16),
        at,
        head_weight,
        *backs,
        smem=1,
        flops=2 * rows * width * width,
        scratch_shapes=[pltpu.VMEM((width, rows), BF16)],
    )
    return (loss.reshape(1), feat_grad, head_grad.T)


def solution(mesh):
    devices = mesh.devices.reshape(8, 4, 4, 2, 2)
    fine = Mesh(devices, ("y", "x", "zh", "zl", "c"))
    batch, rep = (("y", "x", "zh"), ("zl", "c"))
    in_specs = (P(batch, None), P(), P(batch + rep, None), P(), P())
    out_specs = (P(), P(batch, None), P(None, rep))
    return jax.shard_map(local, mesh=fine, in_specs=in_specs, out_specs=out_specs, check_vma=False)
```

```python
import functools

import jax
import jax.numpy as jnp
from jax import lax
from jax.experimental import pallas as pl
from jax.experimental.pallas import tpu as pltpu
from jax.sharding import Mesh
from jax.sharding import PartitionSpec as P

EPS = 1e-06
BF16 = jnp.bfloat16
F32 = jnp.float32
LANES = 128
EXTRA = 16
VMEM = pl.BlockSpec(memory_space=pltpu.VMEM)
SMEM = pl.BlockSpec(memory_space=pltpu.SMEM)


def call(body, outs, *args, smem=0, flops=0, limit=16, **kwargs):
    many = isinstance(outs, (tuple, list))
    specs = [SMEM] * smem + [VMEM] * (len(args) - smem)
    size = sum(a.size * a.dtype.itemsize for a in args)
    return pl.pallas_call(
        body,
        out_shape=outs,
        in_specs=specs,
        out_specs=[VMEM] * len(outs) if many else VMEM,
        cost_estimate=pl.CostEstimate(flops=flops, bytes_accessed=size, transcendentals=0),
        compiler_params=pltpu.CompilerParams(vmem_limit_bytes=limit * 2**20),
        **kwargs,
    )(*args)


def shape(dims, dtype):
    return jax.ShapeDtypeStruct(dims, dtype)


def split3(value):
    hi = value.astype(BF16)
    rest = value - hi.astype(F32)
    mid = rest.astype(BF16)
    low = (rest - mid.astype(F32)).astype(BF16)
    return [hi, mid, low]


def to_all(copies, axes):
    return lax.all_to_all(copies, axes, 0, 0, tiled=True)


def text_kernel(text_ref, out_ref):
    values = text_ref[...].astype(F32)
    inverse = lax.rsqrt(jnp.sum(values * values, axis=-1, keepdims=True) + EPS)
    low = (values * inverse).astype(BF16)
    n = text_ref.shape[0]
    for k in range(out_ref.shape[0] // n):
        out_ref[k * n : (k + 1) * n] = low


def image_kernel(at_ref, wt_ref, own_ref, fetched_ref, swapped_ref, *refs):
    unit_ref, low_ref, inv_ref, own_unit_ref, cols_ref, feats_ref = refs
    rows = own_ref.shape[0]
    part = rows // 2
    c = at_ref[5]
    feats_ref[:rows] = own_ref[...]
    for k, ref in ((c, fetched_ref), (1 - c, swapped_ref)):
        feats_ref[pl.ds(pl.multiple_of((1 + 2 * k) * rows, 16), rows), :] = ref[:rows]
        feats_ref[pl.ds(pl.multiple_of(2 * rows + k * part, 16), part), :] = ref[rows:]
    head = lax.dot_general(
        wt_ref[...], feats_ref[...], (((1,), (1,)), ((), ())), preferred_element_type=F32
    )
    inv = lax.rsqrt(jnp.sum(head * head, axis=0, keepdims=True) + EPS)
    unit = head * inv
    unit_ref[...] = unit
    low_ref[...] = unit.astype(BF16)
    inv_ref[...] = inv
    cols = cols_ref.shape[0]
    start = pl.multiple_of(at_ref[0] * cols, 16)
    cols_ref[...] = unit_ref[pl.ds(start, cols), :]
    own_unit_ref[...] = unit_ref[pl.ds(start, cols), :rows]


def pairs(par_ref, texts, low_ref, own=None):
    z = par_ref[0] * jnp.dot(texts, low_ref[...], preferred_element_type=F32) + par_ref[1]
    v = z if own is None else jnp.where(own, -z, z)
    e = jnp.exp(-jnp.abs(v))
    one = 1.0 + e
    series = e * (1.0 - e * (0.5 - e * (1.0 / 3.0 - e * (0.25 - e * 0.2))))
    log1p = jnp.where(e < 0.03, series, jnp.log(one))
    soft = jnp.maximum(v, 0.0) + log1p
    s = jnp.where(v >= 0.0, 1.0, e) / one
    slope = (s if own is None else jnp.where(own, -s, s)).astype(BF16)
    return slope, jnp.sum(soft, axis=0, keepdims=True)


def turn(texts, slope):
    return lax.dot_general(texts, slope, (((0,), (0,)), ((), ())), preferred_element_type=F32)


def first_kernel(at_ref, par_ref, own_ref, left_ref, low_ref, acc_ref, loss_ref):
    size = (own_ref.shape[0], low_ref.shape[1])
    col = lax.broadcasted_iota(jnp.int32, size, 0) - at_ref[2]
    row = lax.broadcasted_iota(jnp.int32, size, 1) - at_ref[3]
    own = (row == col) & (col >= 0) & (col < at_ref[4])
    slope, loss = pairs(par_ref, own_ref[...], low_ref, own)
    more_slope, more = pairs(par_ref, left_ref[...], low_ref)
    acc_ref[...] = turn(own_ref[...], slope) + turn(left_ref[...], more_slope)
    loss_ref[...] = loss + more


def next_kernel(par_ref, texts_ref, low_ref, acc_in_ref, loss_in_ref, acc_ref, loss_ref):
    slope, loss = pairs(par_ref, texts_ref[...], low_ref)
    acc_ref[...] = acc_in_ref[...] + turn(texts_ref[...], slope)
    loss_ref[...] = loss_in_ref[...] + loss


def last_kernel(at_ref, par_ref, texts_ref, low_ref, unit_ref, acc_ref, loss_ref, keep_ref, send_ref, sum_ref):
    scale = par_ref[0]
    slope, loss = pairs(par_ref, texts_ref[...], low_ref)
    loss = loss_ref[...] + loss
    total = scale * (acc_ref[...] + turn(texts_ref[...], slope))
    sum_ref[...] = total
    dots = jnp.sum(unit_ref[...] * total, axis=0, keepdims=True)
    cols = (keep_ref.shape[0] - EXTRA) // 2
    c = at_ref[5]
    for k in range(2):
        mine = pl.multiple_of((2 * k + c) * cols, 16)
        other = pl.multiple_of((2 * k + 1 - c) * cols, 16)
        keep_ref[k * cols : (k + 1) * cols] = sum_ref[pl.ds(mine, cols), :]
        send_ref[k * cols : (k + 1) * cols] = sum_ref[pl.ds(other, cols), :].astype(BF16)
    pack(keep_ref, send_ref, 2 * cols, dots, loss)


def pack(keep_ref, send_ref, at, dots, loss):
    zeros = jnp.zeros((EXTRA - 2, dots.shape[1]), F32)
    keep_ref[at : at + EXTRA] = jnp.concatenate([dots, loss, zeros], axis=0)
    terms = [t.astype(F32) for t in split3(dots) + split3(loss)]
    zeros = jnp.zeros((EXTRA - 6, dots.shape[1]), F32)
    send_ref[at : at + EXTRA] = jnp.concatenate(terms + [zeros], axis=0).astype(BF16)


def unpack(keep_ref, got_ref, at):
    kept = keep_ref[at : at + EXTRA]
    got = got_ref[at : at + EXTRA].astype(F32)
    dots = kept[0:1] + (got[0:1] + got[1:2] + got[2:3])
    loss = kept[1:2] + (got[3:4] + got[4:5] + got[5:6])
    return dots, loss


def middle_kernel(at_ref, keep_ref, got_ref, keep2_ref, send2_ref):
    cols = keep2_ref.shape[0] - EXTRA
    dots, loss = unpack(keep_ref, got_ref, 2 * cols)
    zl = at_ref[6]
    mine = pl.multiple_of(zl * cols, 16)
    other = pl.multiple_of((1 - zl) * cols, 16)
    keep2_ref[:cols] = keep_ref[pl.ds(mine, cols), :] + got_ref[pl.ds(mine, cols), :].astype(F32)
    send2_ref[:cols] = (
        keep_ref[pl.ds(other, cols), :] + got_ref[pl.ds(other, cols), :].astype(F32)
    ).astype(BF16)
    pack(keep2_ref, send2_ref, cols, dots, loss)


def head_kernel(at_loss, keep_ref, got_ref, unit_ref, inv_ref, feats_ref, flat_ref, *dir_refs):
    cols = keep_ref.shape[0] - EXTRA
    dots, loss = unpack(keep_ref, got_ref, cols)
    total = keep_ref[:cols] + got_ref[:cols].astype(F32)
    back = ((total - unit_ref[...] * dots) * inv_ref[...]).astype(BF16)
    head = jnp.dot(back, feats_ref[...], preferred_element_type=F32).astype(BF16)
    tiles = feats_ref.shape[1] // LANES
    for k in range(tiles):
        flat_ref[k * cols : (k + 1) * cols] = head[:, k * LANES : (k + 1) * LANES]
    part = loss[:, :LANES]
    for k in range(1, loss.shape[1] // LANES):
        part = part + loss[:, k * LANES : (k + 1) * LANES]
    terms = [t.astype(F32) for t in split3(part)]
    tail = jnp.concatenate(terms + [jnp.zeros((EXTRA - 3, LANES), F32)], axis=0)
    end = tiles * cols
    flat_ref[end:at_loss] = jnp.zeros((at_loss - end, LANES), BF16)
    flat_ref[at_loss : at_loss + EXTRA] = tail.astype(BF16)
    flat_ref[at_loss + EXTRA :] = jnp.zeros((flat_ref.shape[0] - at_loss - EXTRA, LANES), BF16)
    low = total.astype(BF16)
    terms = [t.astype(F32) for t in split3(dots)]
    lines = jnp.concatenate(terms + [jnp.zeros((EXTRA - 3, dots.shape[1]), F32)], axis=0).astype(BF16)
    rows = dir_refs[0].shape[1]
    for k, ref in enumerate(dir_refs):
        ref[:cols] = low[:, k * rows : (k + 1) * rows]
        ref[cols:] = lines[:, k * rows : (k + 1) * rows]


def back_kernel(unit_ref, inv_ref, *refs):
    out_ref = refs[-1]
    cols, rows = unit_ref.shape
    total = refs[0][...].astype(F32)
    for ref in refs[1:-1]:
        total = total + ref[...].astype(F32)
    dots = total[cols : cols + 1] + total[cols + 1 : cols + 2] + total[cols + 2 : cols + 3]
    out_ref[...] = ((total[:cols] - unit_ref[...] * dots) * inv_ref[:, :rows]).astype(BF16)


def to_low(at_ref, total):
    first = total[:EXTRA]
    terms = [t.astype(F32) for t in split3(first[0:1] + first[1:2] + first[2:3])]
    row = jnp.concatenate(terms + [jnp.zeros((EXTRA - 3, LANES), F32)], axis=0)
    return jnp.where(at_ref[7] > 0, row, first).astype(BF16), total[EXTRA:].astype(BF16)


def sum_kernel(at_ref, parts_ref, after_ref, out_ref):
    first, rest = to_low(at_ref, jnp.sum(parts_ref[...].astype(F32), axis=0))
    for k in range(out_ref.shape[0]):
        out_ref[k, :EXTRA] = first
        out_ref[k, EXTRA:] = rest


def feat_kernel(at_ref, weight_ref, *refs):
    out_ref, back_ref = refs[-2:]
    cols = refs[0].shape[0]
    for d, ref in enumerate(refs[:-2]):
        back_ref[pl.ds(pl.multiple_of(at_ref[8 + d] * cols, 16), cols), :] = ref[...]
    out_ref[...] = lax.dot_general(
        back_ref[...], weight_ref[...], (((0,), (1,)), ((), ())), preferred_element_type=F32
    ).astype(BF16)


def final_kernel(at_loss, pairs, full_ref, head_ref, loss_ref):
    cols, width = head_ref.shape
    tiles = width // LANES
    for k in range(tiles):
        head_ref[:, k * LANES : (k + 1) * LANES] = full_ref[k * cols : (k + 1) * cols]
    total = jnp.sum(full_ref[at_loss : at_loss + EXTRA].astype(F32), axis=0, keepdims=True)
    loss_ref[...] = jnp.sum(total, axis=1, keepdims=True) / pairs


def shift_by(x, axis, step):
    n = lax.axis_size(axis)
    return lax.ppermute(x, axis, [(k, (k + step) % n) for k in range(n)])


def local(img_feat, head_weight, text_embed, log_temp, logit_bias):
    rows, width = img_feat.shape
    quarter = text_embed.shape[0]
    ny, nx, nzh, nzl, nc = (lax.axis_size(a) for a in ("y", "x", "zh", "zl", "c"))
    nrep = nzl * nc
    plane = nx * ny
    cols = width // nrep
    images = nzh * rows
    tiles = width // LANES
    y_at, x_at, zl_at, c_at = (lax.axis_index(a) for a in ("y", "x", "zl", "c"))
    rep_at = zl_at * nc + c_at
    piece = -(-(tiles * cols) // (plane * 8)) * 8
    at_loss = -(-(tiles * cols) // piece) * piece
    assert at_loss < plane * piece
    at = jnp.stack(
        [
            rep_at,
            0 * rep_at,
            y_at * quarter,
            rep_at * quarter,
            quarter + 0 * rep_at,
            c_at,
            zl_at,
            (y_at * nx + x_at == at_loss // piece).astype(jnp.int32),
        ]
        + [rep_at ^ d for d in range(nrep)]
    ).astype(jnp.int32)
    par = jnp.stack([jnp.exp(log_temp[0]), logit_bias[0]])

    copies = call(text_kernel, shape((ny * quarter, width), BF16), text_embed)
    part = rows // nc
    def place(z, low, core):
        return (z % nzh * nzl + low) * nc + core

    near = []
    cross = []
    for z in range(nzh):
        near += [(place(z, 1, k), place(z + 1, k, 0)) for k in range(nc)]
        near += [(place(z, 0, k), place(z - 1, k, 1)) for k in range(nc)]
        cross += [(place(z, 1, k), place(z + 2, 0, k)) for k in range(nc)]
        cross += [(place(z, 0, k), place(z - 2, 1, k)) for k in range(nc)]
    half_rows = lax.dynamic_slice_in_dim(img_feat, c_at * part, part, 0)
    line = ("zh", "zl", "c")
    across = lax.ppermute(half_rows, line, cross)
    beside = lax.ppermute(img_feat, line, near)
    fetched = jnp.concatenate([beside, across], axis=0)
    own = to_all(copies, "y")
    far = shift_by(own, "x", 2)
    left = shift_by(own, "x", 1)
    right = shift_by(own, "x", -1)
    swapped = lax.ppermute(fetched, "c", [(0, 1), (1, 0)])

    unit, low, inv, own_unit, col_unit, feats = call(
        image_kernel,
        [
            shape((width, images), F32),
            shape((width, images), BF16),
            shape((1, images), F32),
            shape((cols, rows), F32),
            shape((cols, images), F32),
            shape((images, width), BF16),
        ],
        at,
        head_weight.T,
        img_feat,
        fetched,
        swapped,
        smem=1,
        flops=2 * width,
    )
    acc, loss_row = call(
        first_kernel,
        [shape((width, images), F32), shape((1, images), F32)],
        at,
        par,
        own,
        left,
        low,
        smem=2,
        flops=2 * 4 * width * images * own.shape[0],
    )
    acc, loss_row = call(
        next_kernel,
        [shape((width, images), F32), shape((1, images), F32)],
        par,
        right,
        low,
        acc,
        loss_row,
        smem=1,
        flops=width,
    )
    keep, send = call(
        last_kernel,
        [shape((2 * cols + EXTRA, images), F32), shape((2 * cols + EXTRA, images), BF16)],
        at,
        par,
        far,
        low,
        unit,
        acc,
        loss_row,
        smem=2,
        flops=4 * width * images * own.shape[0],
        scratch_shapes=[pltpu.VMEM((width, images), F32)],
    )
    got = lax.ppermute(send, "c", [(0, 1), (1, 0)])
    keep2, send2 = call(
        middle_kernel,
        [shape((cols + EXTRA, images), F32), shape((cols + EXTRA, images), BF16)],
        at,
        keep,
        got,
        smem=1,
    )
    got2 = lax.ppermute(send2, "zl", [(0, 1), (1, 0)])
    flat, *dirs = call(
        functools.partial(head_kernel, at_loss),
        [shape((plane * piece, LANES), BF16)] + [shape((cols + EXTRA, rows), BF16)] * nzh,
        keep2,
        got2,
        col_unit,
        inv,
        feats,
        flops=2 * cols * images * width,
    )

    dirs = [dirs[0]] + [shift_by(dirs[s], "zh", -s) for s in range(1, nzh)]
    back = call(back_kernel, shape((cols, rows), BF16), own_unit, inv, *dirs)

    parts = to_all(flat, ("y", "x")).reshape(plane, piece, LANES)
    part = pl.pallas_call(
        sum_kernel,
        out_shape=shape((nzh, piece, LANES), BF16),
        in_specs=[SMEM, VMEM, pl.BlockSpec(memory_space=pl.ANY)],
        out_specs=VMEM,
    )(at, parts, back)
    part = to_all(part, "zh")
    low_part = pl.pallas_call(
        sum_kernel,
        out_shape=shape((plane, piece, LANES), BF16),
        in_specs=[SMEM, VMEM, pl.BlockSpec(memory_space=pl.ANY)],
        out_specs=VMEM,
    )(at, part, back)
    full = to_all(low_part.reshape(plane * piece, LANES), ("y", "x"))
    group = rows * plane * nzh
    head_grad, loss = call(
        functools.partial(final_kernel, at_loss, float(group) * float(group)),
        [shape((cols, width), BF16), shape((1, 1), F32)],
        full,
    )

    backs = [back]
    for d in range(1, nrep):
        backs.append(lax.ppermute(back, ("zl", "c"), [(k, k ^ d) for k in range(nrep)]))
    feat_grad = call(
        feat_kernel,
        shape((rows, width), BF16),
        at,
        head_weight,
        *backs,
        smem=1,
        flops=2 * rows * width * width,
        scratch_shapes=[pltpu.VMEM((width, rows), BF16)],
    )
    return (loss.reshape(1), feat_grad, head_grad.T)


def solution(mesh):
    devices = mesh.devices.reshape(8, 4, 4, 2, 2)
    fine = Mesh(devices, ("y", "x", "zh", "zl", "c"))
    batch, rep = (("y", "x", "zh"), ("zl", "c"))
    in_specs = (P(batch, None), P(), P(batch + rep, None), P(), P())
    out_specs = (P(), P(batch, None), P(None, rep))
    return jax.shard_map(local, mesh=fine, in_specs=in_specs, out_specs=out_specs, check_vma=False)
```

```python
import functools

import jax
import jax.numpy as jnp
from jax import lax
from jax.experimental import pallas as pl
from jax.experimental.pallas import tpu as pltpu
from jax.sharding import Mesh
from jax.sharding import PartitionSpec as P

EPS = 1e-06
BF16 = jnp.bfloat16
F32 = jnp.float32
LANES = 128
EXTRA = 16
VMEM = pl.BlockSpec(memory_space=pltpu.VMEM)
SMEM = pl.BlockSpec(memory_space=pltpu.SMEM)


def call(body, outs, *args, smem=0, flops=0, limit=16, **kwargs):
    many = isinstance(outs, (tuple, list))
    specs = [SMEM] * smem + [VMEM] * (len(args) - smem)
    size = sum(a.size * a.dtype.itemsize for a in args)
    return pl.pallas_call(
        body,
        out_shape=outs,
        in_specs=specs,
        out_specs=[VMEM] * len(outs) if many else VMEM,
        cost_estimate=pl.CostEstimate(flops=flops, bytes_accessed=size, transcendentals=0),
        compiler_params=pltpu.CompilerParams(vmem_limit_bytes=limit * 2**20),
        **kwargs,
    )(*args)


def shape(dims, dtype):
    return jax.ShapeDtypeStruct(dims, dtype)


def split3(value):
    hi = value.astype(BF16)
    rest = value - hi.astype(F32)
    mid = rest.astype(BF16)
    low = (rest - mid.astype(F32)).astype(BF16)
    return [hi, mid, low]


def to_all(copies, axes):
    return lax.all_to_all(copies, axes, 0, 0, tiled=True)


def text_kernel(text_ref, out_ref):
    values = text_ref[...].astype(F32)
    inverse = lax.rsqrt(jnp.sum(values * values, axis=-1, keepdims=True) + EPS)
    low = (values * inverse).astype(BF16)
    n = text_ref.shape[0]
    for k in range(out_ref.shape[0] // n):
        out_ref[k * n : (k + 1) * n] = low


def image_kernel(at_ref, wt_ref, own_ref, fetched_ref, swapped_ref, *refs):
    unit_ref, low_ref, inv_ref, own_unit_ref, cols_ref, feats_ref = refs
    rows = own_ref.shape[0]
    part = rows // 2
    c = at_ref[5]
    feats_ref[:rows] = own_ref[...]
    for k, ref in ((c, fetched_ref), (1 - c, swapped_ref)):
        feats_ref[pl.ds(pl.multiple_of((1 + 2 * k) * rows, 16), rows), :] = ref[:rows]
        feats_ref[pl.ds(pl.multiple_of(2 * rows + k * part, 16), part), :] = ref[rows:]
    head = lax.dot_general(
        wt_ref[...], feats_ref[...], (((1,), (1,)), ((), ())), preferred_element_type=F32
    )
    inv = lax.rsqrt(jnp.sum(head * head, axis=0, keepdims=True) + EPS)
    unit = head * inv
    unit_ref[...] = unit
    low_ref[...] = unit.astype(BF16)
    inv_ref[...] = inv
    cols = cols_ref.shape[0]
    start = pl.multiple_of(at_ref[0] * cols, 16)
    cols_ref[...] = unit_ref[pl.ds(start, cols), :]
    own_unit_ref[...] = unit_ref[pl.ds(start, cols), :rows]


def pairs(par_ref, texts, low_ref, own=None):
    z = par_ref[0] * jnp.dot(texts, low_ref[...], preferred_element_type=F32) + par_ref[1]
    v = z if own is None else jnp.where(own, -z, z)
    e = jnp.exp(-jnp.abs(v))
    one = 1.0 + e
    series = e * (1.0 - e * (0.5 - e * (1.0 / 3.0 - e * (0.25 - e * 0.2))))
    log1p = jnp.where(e < 0.03, series, jnp.log(one))
    soft = jnp.maximum(v, 0.0) + log1p
    s = jnp.where(v >= 0.0, 1.0, e) / one
    slope = (s if own is None else jnp.where(own, -s, s)).astype(BF16)
    return slope, jnp.sum(soft, axis=0, keepdims=True)


def turn(texts, slope):
    return lax.dot_general(texts, slope, (((0,), (0,)), ((), ())), preferred_element_type=F32)


def first_kernel(at_ref, par_ref, own_ref, left_ref, low_ref, acc_ref, loss_ref):
    size = (own_ref.shape[0], low_ref.shape[1])
    col = lax.broadcasted_iota(jnp.int32, size, 0) - at_ref[2]
    row = lax.broadcasted_iota(jnp.int32, size, 1) - at_ref[3]
    own = (row == col) & (col >= 0) & (col < at_ref[4])
    slope, loss = pairs(par_ref, own_ref[...], low_ref, own)
    more_slope, more = pairs(par_ref, left_ref[...], low_ref)
    acc_ref[...] = turn(own_ref[...], slope) + turn(left_ref[...], more_slope)
    loss_ref[...] = loss + more


def next_kernel(par_ref, texts_ref, low_ref, acc_in_ref, loss_in_ref, acc_ref, loss_ref):
    slope, loss = pairs(par_ref, texts_ref[...], low_ref)
    acc_ref[...] = acc_in_ref[...] + turn(texts_ref[...], slope)
    loss_ref[...] = loss_in_ref[...] + loss


def last_kernel(at_ref, par_ref, texts_ref, low_ref, unit_ref, acc_ref, loss_ref, keep_ref, send_ref, sum_ref):
    scale = par_ref[0]
    slope, loss = pairs(par_ref, texts_ref[...], low_ref)
    loss = loss_ref[...] + loss
    total = scale * (acc_ref[...] + turn(texts_ref[...], slope))
    sum_ref[...] = total
    dots = jnp.sum(unit_ref[...] * total, axis=0, keepdims=True)
    cols = (keep_ref.shape[0] - EXTRA) // 2
    c = at_ref[5]
    for k in range(2):
        mine = pl.multiple_of((2 * k + c) * cols, 16)
        other = pl.multiple_of((2 * k + 1 - c) * cols, 16)
        keep_ref[k * cols : (k + 1) * cols] = sum_ref[pl.ds(mine, cols), :]
        send_ref[k * cols : (k + 1) * cols] = sum_ref[pl.ds(other, cols), :].astype(BF16)
    pack(keep_ref, send_ref, 2 * cols, dots, loss)


def pack(keep_ref, send_ref, at, dots, loss):
    zeros = jnp.zeros((EXTRA - 2, dots.shape[1]), F32)
    keep_ref[at : at + EXTRA] = jnp.concatenate([dots, loss, zeros], axis=0)
    terms = [t.astype(F32) for t in split3(dots) + split3(loss)]
    zeros = jnp.zeros((EXTRA - 6, dots.shape[1]), F32)
    send_ref[at : at + EXTRA] = jnp.concatenate(terms + [zeros], axis=0).astype(BF16)


def unpack(keep_ref, got_ref, at):
    kept = keep_ref[at : at + EXTRA]
    got = got_ref[at : at + EXTRA].astype(F32)
    dots = kept[0:1] + (got[0:1] + got[1:2] + got[2:3])
    loss = kept[1:2] + (got[3:4] + got[4:5] + got[5:6])
    return dots, loss


def middle_kernel(at_ref, keep_ref, got_ref, keep2_ref, send2_ref):
    cols = keep2_ref.shape[0] - EXTRA
    dots, loss = unpack(keep_ref, got_ref, 2 * cols)
    zl = at_ref[6]
    mine = pl.multiple_of(zl * cols, 16)
    other = pl.multiple_of((1 - zl) * cols, 16)
    keep2_ref[:cols] = keep_ref[pl.ds(mine, cols), :] + got_ref[pl.ds(mine, cols), :].astype(F32)
    send2_ref[:cols] = (
        keep_ref[pl.ds(other, cols), :] + got_ref[pl.ds(other, cols), :].astype(F32)
    ).astype(BF16)
    pack(keep2_ref, send2_ref, cols, dots, loss)


def head_kernel(at_loss, keep_ref, got_ref, unit_ref, inv_ref, feats_ref, flat_ref, *dir_refs):
    cols = keep_ref.shape[0] - EXTRA
    dots, loss = unpack(keep_ref, got_ref, cols)
    total = keep_ref[:cols] + got_ref[:cols].astype(F32)
    back = ((total - unit_ref[...] * dots) * inv_ref[...]).astype(BF16)
    head = jnp.dot(back, feats_ref[...], preferred_element_type=F32).astype(BF16)
    tiles = feats_ref.shape[1] // LANES
    for k in range(tiles):
        flat_ref[k * cols : (k + 1) * cols] = head[:, k * LANES : (k + 1) * LANES]
    part = loss[:, :LANES]
    for k in range(1, loss.shape[1] // LANES):
        part = part + loss[:, k * LANES : (k + 1) * LANES]
    terms = [t.astype(F32) for t in split3(part)]
    tail = jnp.concatenate(terms + [jnp.zeros((EXTRA - 3, LANES), F32)], axis=0)
    end = tiles * cols
    flat_ref[end:at_loss] = jnp.zeros((at_loss - end, LANES), BF16)
    flat_ref[at_loss : at_loss + EXTRA] = tail.astype(BF16)
    flat_ref[at_loss + EXTRA :] = jnp.zeros((flat_ref.shape[0] - at_loss - EXTRA, LANES), BF16)
    low = total.astype(BF16)
    terms = [t.astype(F32) for t in split3(dots)]
    lines = jnp.concatenate(terms + [jnp.zeros((EXTRA - 3, dots.shape[1]), F32)], axis=0).astype(BF16)
    rows = dir_refs[0].shape[1]
    for k, ref in enumerate(dir_refs):
        ref[:cols] = low[:, k * rows : (k + 1) * rows]
        ref[cols:] = lines[:, k * rows : (k + 1) * rows]


def back_kernel(unit_ref, inv_ref, *refs):
    out_ref = refs[-1]
    cols, rows = unit_ref.shape
    total = refs[0][...].astype(F32)
    for ref in refs[1:-1]:
        total = total + ref[...].astype(F32)
    dots = total[cols : cols + 1] + total[cols + 1 : cols + 2] + total[cols + 2 : cols + 3]
    out_ref[...] = ((total[:cols] - unit_ref[...] * dots) * inv_ref[:, :rows]).astype(BF16)


def to_low(at_ref, total):
    first = total[:EXTRA]
    terms = [t.astype(F32) for t in split3(first[0:1] + first[1:2] + first[2:3])]
    row = jnp.concatenate(terms + [jnp.zeros((EXTRA - 3, LANES), F32)], axis=0)
    return jnp.where(at_ref[7] > 0, row, first).astype(BF16), total[EXTRA:].astype(BF16)


def sum_kernel(at_ref, parts_ref, *refs):
    out_ref = refs[-1]
    first, rest = to_low(at_ref, jnp.sum(parts_ref[...].astype(F32), axis=0))
    for k in range(out_ref.shape[0]):
        out_ref[k, :EXTRA] = first
        out_ref[k, EXTRA:] = rest


def feat_kernel(at_ref, weight_ref, *refs):
    out_ref, back_ref = refs[-2:]
    cols = refs[0].shape[0]
    for d, ref in enumerate(refs[:-2]):
        back_ref[pl.ds(pl.multiple_of(at_ref[8 + d] * cols, 16), cols), :] = ref[...]
    out_ref[...] = lax.dot_general(
        back_ref[...], weight_ref[...], (((0,), (1,)), ((), ())), preferred_element_type=F32
    ).astype(BF16)


def final_kernel(at_loss, pairs, full_ref, head_ref, loss_ref):
    cols, width = head_ref.shape
    tiles = width // LANES
    for k in range(tiles):
        head_ref[:, k * LANES : (k + 1) * LANES] = full_ref[k * cols : (k + 1) * cols]
    total = jnp.sum(full_ref[at_loss : at_loss + EXTRA].astype(F32), axis=0, keepdims=True)
    loss_ref[...] = jnp.sum(total, axis=1, keepdims=True) / pairs


def shift_by(x, axis, step):
    n = lax.axis_size(axis)
    return lax.ppermute(x, axis, [(k, (k + step) % n) for k in range(n)])


def local(img_feat, head_weight, text_embed, log_temp, logit_bias):
    rows, width = img_feat.shape
    quarter = text_embed.shape[0]
    ny, nx, nzh, nzl, nc = (lax.axis_size(a) for a in ("y", "x", "zh", "zl", "c"))
    nrep = nzl * nc
    plane = nx * ny
    cols = width // nrep
    images = nzh * rows
    tiles = width // LANES
    y_at, x_at, zl_at, c_at = (lax.axis_index(a) for a in ("y", "x", "zl", "c"))
    rep_at = zl_at * nc + c_at
    piece = -(-(tiles * cols) // (plane * 8)) * 8
    at_loss = -(-(tiles * cols) // piece) * piece
    assert at_loss < plane * piece
    at = jnp.stack(
        [
            rep_at,
            0 * rep_at,
            y_at * quarter,
            rep_at * quarter,
            quarter + 0 * rep_at,
            c_at,
            zl_at,
            (y_at * nx + x_at == at_loss // piece).astype(jnp.int32),
        ]
        + [rep_at ^ d for d in range(nrep)]
    ).astype(jnp.int32)
    par = jnp.stack([jnp.exp(log_temp[0]), logit_bias[0]])

    copies = call(text_kernel, shape((ny * quarter, width), BF16), text_embed)
    part = rows // nc
    def place(z, low, core):
        return (z % nzh * nzl + low) * nc + core

    near = []
    cross = []
    for z in range(nzh):
        near += [(place(z, 1, k), place(z + 1, k, 0)) for k in range(nc)]
        near += [(place(z, 0, k), place(z - 1, k, 1)) for k in range(nc)]
        cross += [(place(z, 1, k), place(z + 2, 0, k)) for k in range(nc)]
        cross += [(place(z, 0, k), place(z - 2, 1, k)) for k in range(nc)]
    half_rows = lax.dynamic_slice_in_dim(img_feat, c_at * part, part, 0)
    line = ("zh", "zl", "c")
    across = lax.ppermute(half_rows, line, cross)
    beside = lax.ppermute(img_feat, line, near)
    fetched = jnp.concatenate([beside, across], axis=0)
    own = to_all(copies, "y")
    far = shift_by(own, "x", 2)
    left = shift_by(own, "x", 1)
    right = shift_by(own, "x", -1)
    swapped = lax.ppermute(fetched, "c", [(0, 1), (1, 0)])

    unit, low, inv, own_unit, col_unit, feats = call(
        image_kernel,
        [
            shape((width, images), F32),
            shape((width, images), BF16),
            shape((1, images), F32),
            shape((cols, rows), F32),
            shape((cols, images), F32),
            shape((images, width), BF16),
        ],
        at,
        head_weight.T,
        img_feat,
        fetched,
        swapped,
        smem=1,
        flops=2 * width,
    )
    acc, loss_row = call(
        first_kernel,
        [shape((width, images), F32), shape((1, images), F32)],
        at,
        par,
        own,
        left,
        low,
        smem=2,
        flops=2 * 4 * width * images * own.shape[0],
    )
    acc, loss_row = call(
        next_kernel,
        [shape((width, images), F32), shape((1, images), F32)],
        par,
        right,
        low,
        acc,
        loss_row,
        smem=1,
        flops=width,
    )
    keep, send = call(
        last_kernel,
        [shape((2 * cols + EXTRA, images), F32), shape((2 * cols + EXTRA, images), BF16)],
        at,
        par,
        far,
        low,
        unit,
        acc,
        loss_row,
        smem=2,
        flops=4 * width * images * own.shape[0],
        scratch_shapes=[pltpu.VMEM((width, images), F32)],
    )
    got = lax.ppermute(send, "c", [(0, 1), (1, 0)])
    keep2, send2 = call(
        middle_kernel,
        [shape((cols + EXTRA, images), F32), shape((cols + EXTRA, images), BF16)],
        at,
        keep,
        got,
        smem=1,
    )
    got2 = lax.ppermute(send2, "zl", [(0, 1), (1, 0)])
    flat, *dirs = call(
        functools.partial(head_kernel, at_loss),
        [shape((plane * piece, LANES), BF16)] + [shape((cols + EXTRA, rows), BF16)] * nzh,
        keep2,
        got2,
        col_unit,
        inv,
        feats,
        flops=2 * cols * images * width,
    )

    dirs = [dirs[0]] + [shift_by(dirs[s], "zh", -s) for s in range(1, nzh)]
    back = call(back_kernel, shape((cols, rows), BF16), own_unit, inv, *dirs, flops=2 * 10**10)

    parts = to_all(flat, ("y", "x")).reshape(plane, piece, LANES)
    part = call(sum_kernel, shape((nzh, piece, LANES), BF16), at, parts, smem=1)
    part = to_all(part, "zh")
    low_part = call(sum_kernel, shape((plane, piece, LANES), BF16), at, part, smem=1)
    full = to_all(low_part.reshape(plane * piece, LANES), ("y", "x"))
    group = rows * plane * nzh
    head_grad, loss = call(
        functools.partial(final_kernel, at_loss, float(group) * float(group)),
        [shape((cols, width), BF16), shape((1, 1), F32)],
        full,
    )

    backs = [back]
    for d in range(1, nrep):
        backs.append(lax.ppermute(back, ("zl", "c"), [(k, k ^ d) for k in range(nrep)]))
    feat_grad = call(
        feat_kernel,
        shape((rows, width), BF16),
        at,
        head_weight,
        *backs,
        smem=1,
        flops=2 * rows * width * width,
        scratch_shapes=[pltpu.VMEM((width, rows), BF16)],
    )
    return (loss.reshape(1), feat_grad, head_grad.T)


def solution(mesh):
    devices = mesh.devices.reshape(8, 4, 4, 2, 2)
    fine = Mesh(devices, ("y", "x", "zh", "zl", "c"))
    batch, rep = (("y", "x", "zh"), ("zl", "c"))
    in_specs = (P(batch, None), P(), P(batch + rep, None), P(), P())
    out_specs = (P(), P(batch, None), P(None, rep))
    return jax.shard_map(local, mesh=fine, in_specs=in_specs, out_specs=out_specs, check_vma=False)
```

```python
import functools

import jax
import jax.numpy as jnp
from jax import lax
from jax.experimental import pallas as pl
from jax.experimental.pallas import tpu as pltpu
from jax.sharding import Mesh
from jax.sharding import PartitionSpec as P

EPS = 1e-06
BF16 = jnp.bfloat16
F32 = jnp.float32
LANES = 128
EXTRA = 16
VMEM = pl.BlockSpec(memory_space=pltpu.VMEM)
SMEM = pl.BlockSpec(memory_space=pltpu.SMEM)


def call(body, outs, *args, smem=0, flops=0, limit=16, **kwargs):
    many = isinstance(outs, (tuple, list))
    specs = [SMEM] * smem + [VMEM] * (len(args) - smem)
    size = sum(a.size * a.dtype.itemsize for a in args)
    return pl.pallas_call(
        body,
        out_shape=outs,
        in_specs=specs,
        out_specs=[VMEM] * len(outs) if many else VMEM,
        cost_estimate=pl.CostEstimate(flops=flops, bytes_accessed=size, transcendentals=0),
        compiler_params=pltpu.CompilerParams(vmem_limit_bytes=limit * 2**20),
        **kwargs,
    )(*args)


def shape(dims, dtype):
    return jax.ShapeDtypeStruct(dims, dtype)


def split3(value):
    hi = value.astype(BF16)
    rest = value - hi.astype(F32)
    mid = rest.astype(BF16)
    low = (rest - mid.astype(F32)).astype(BF16)
    return [hi, mid, low]


def to_all(copies, axes):
    return lax.all_to_all(copies, axes, 0, 0, tiled=True)


def text_kernel(text_ref, out_ref):
    values = text_ref[...].astype(F32)
    inverse = lax.rsqrt(jnp.sum(values * values, axis=-1, keepdims=True) + EPS)
    low = (values * inverse).astype(BF16)
    n = text_ref.shape[0]
    for k in range(out_ref.shape[0] // n):
        out_ref[k * n : (k + 1) * n] = low


def image_kernel(at_ref, wt_ref, own_ref, fetched_ref, swapped_ref, *refs):
    unit_ref, low_ref, inv_ref, own_unit_ref, cols_ref, feats_ref = refs
    rows = own_ref.shape[0]
    part = rows // 2
    c = at_ref[5]
    feats_ref[:rows] = own_ref[...]
    for k, ref in ((c, fetched_ref), (1 - c, swapped_ref)):
        feats_ref[pl.ds(pl.multiple_of((1 + 2 * k) * rows, 16), rows), :] = ref[:rows]
        feats_ref[pl.ds(pl.multiple_of(2 * rows + k * part, 16), part), :] = ref[rows:]
    head = lax.dot_general(
        wt_ref[...], feats_ref[...], (((0,), (1,)), ((), ())), preferred_element_type=F32
    )
    inv = lax.rsqrt(jnp.sum(head * head, axis=0, keepdims=True) + EPS)
    unit = head * inv
    unit_ref[...] = unit
    low_ref[...] = unit.astype(BF16)
    inv_ref[...] = inv
    cols = cols_ref.shape[0]
    start = pl.multiple_of(at_ref[0] * cols, 16)
    cols_ref[...] = unit_ref[pl.ds(start, cols), :]
    own_unit_ref[...] = unit_ref[pl.ds(start, cols), :rows]


def pairs(par_ref, texts, low_ref, own=None):
    z = par_ref[0] * jnp.dot(texts, low_ref[...], preferred_element_type=F32) + par_ref[1]
    v = z if own is None else jnp.where(own, -z, z)
    e = jnp.exp(-jnp.abs(v))
    one = 1.0 + e
    series = e * (1.0 - e * (0.5 - e * (1.0 / 3.0 - e * (0.25 - e * 0.2))))
    log1p = jnp.where(e < 0.03, series, jnp.log(one))
    soft = jnp.maximum(v, 0.0) + log1p
    s = jnp.where(v >= 0.0, 1.0, e) / one
    slope = (s if own is None else jnp.where(own, -s, s)).astype(BF16)
    return slope, jnp.sum(soft, axis=0, keepdims=True)


def turn(texts, slope):
    return lax.dot_general(texts, slope, (((0,), (0,)), ((), ())), preferred_element_type=F32)


def first_kernel(at_ref, par_ref, own_ref, left_ref, low_ref, acc_ref, loss_ref):
    size = (own_ref.shape[0], low_ref.shape[1])
    col = lax.broadcasted_iota(jnp.int32, size, 0) - at_ref[2]
    row = lax.broadcasted_iota(jnp.int32, size, 1) - at_ref[3]
    own = (row == col) & (col >= 0) & (col < at_ref[4])
    slope, loss = pairs(par_ref, own_ref[...], low_ref, own)
    more_slope, more = pairs(par_ref, left_ref[...], low_ref)
    acc_ref[...] = turn(own_ref[...], slope) + turn(left_ref[...], more_slope)
    loss_ref[...] = loss + more


def second_kernel(at_ref, par_ref, right_ref, far_ref, low_ref, unit_ref, acc_ref, loss_ref, keep_ref, send_ref, sum_ref):
    scale = par_ref[0]
    slope, loss = pairs(par_ref, right_ref[...], low_ref)
    more_slope, more = pairs(par_ref, far_ref[...], low_ref)
    loss = loss_ref[...] + loss + more
    total = scale * (acc_ref[...] + turn(right_ref[...], slope) + turn(far_ref[...], more_slope))
    sum_ref[...] = total
    dots = jnp.sum(unit_ref[...] * total, axis=0, keepdims=True)
    cols = (keep_ref.shape[0] - EXTRA) // 2
    c = at_ref[5]
    for k in range(2):
        mine = pl.multiple_of((2 * k + c) * cols, 16)
        other = pl.multiple_of((2 * k + 1 - c) * cols, 16)
        keep_ref[k * cols : (k + 1) * cols] = sum_ref[pl.ds(mine, cols), :]
        send_ref[k * cols : (k + 1) * cols] = sum_ref[pl.ds(other, cols), :].astype(BF16)
    pack(keep_ref, send_ref, 2 * cols, dots, loss)


def pack(keep_ref, send_ref, at, dots, loss):
    zeros = jnp.zeros((EXTRA - 2, dots.shape[1]), F32)
    keep_ref[at : at + EXTRA] = jnp.concatenate([dots, loss, zeros], axis=0)
    terms = [t.astype(F32) for t in split3(dots) + split3(loss)]
    zeros = jnp.zeros((EXTRA - 6, dots.shape[1]), F32)
    send_ref[at : at + EXTRA] = jnp.concatenate(terms + [zeros], axis=0).astype(BF16)


def unpack(keep_ref, got_ref, at):
    kept = keep_ref[at : at + EXTRA]
    got = got_ref[at : at + EXTRA].astype(F32)
    dots = kept[0:1] + (got[0:1] + got[1:2] + got[2:3])
    loss = kept[1:2] + (got[3:4] + got[4:5] + got[5:6])
    return dots, loss


def middle_kernel(at_ref, keep_ref, got_ref, keep2_ref, send2_ref):
    cols = keep2_ref.shape[0] - EXTRA
    dots, loss = unpack(keep_ref, got_ref, 2 * cols)
    zl = at_ref[6]
    mine = pl.multiple_of(zl * cols, 16)
    other = pl.multiple_of((1 - zl) * cols, 16)
    keep2_ref[:cols] = keep_ref[pl.ds(mine, cols), :] + got_ref[pl.ds(mine, cols), :].astype(F32)
    send2_ref[:cols] = (
        keep_ref[pl.ds(other, cols), :] + got_ref[pl.ds(other, cols), :].astype(F32)
    ).astype(BF16)
    pack(keep2_ref, send2_ref, cols, dots, loss)


def head_kernel(at_loss, keep_ref, got_ref, unit_ref, inv_ref, feats_ref, flat_ref, *dir_refs):
    cols = keep_ref.shape[0] - EXTRA
    dots, loss = unpack(keep_ref, got_ref, cols)
    total = keep_ref[:cols] + got_ref[:cols].astype(F32)
    back = ((total - unit_ref[...] * dots) * inv_ref[...]).astype(BF16)
    head = jnp.dot(back, feats_ref[...], preferred_element_type=F32).astype(BF16)
    tiles = feats_ref.shape[1] // LANES
    for k in range(tiles):
        flat_ref[k * cols : (k + 1) * cols] = head[:, k * LANES : (k + 1) * LANES]
    part = loss[:, :LANES]
    for k in range(1, loss.shape[1] // LANES):
        part = part + loss[:, k * LANES : (k + 1) * LANES]
    terms = [t.astype(F32) for t in split3(part)]
    tail = jnp.concatenate(terms + [jnp.zeros((EXTRA - 3, LANES), F32)], axis=0)
    end = tiles * cols
    flat_ref[end:at_loss] = jnp.zeros((at_loss - end, LANES), BF16)
    flat_ref[at_loss : at_loss + EXTRA] = tail.astype(BF16)
    flat_ref[at_loss + EXTRA :] = jnp.zeros((flat_ref.shape[0] - at_loss - EXTRA, LANES), BF16)
    low = total.astype(BF16)
    terms = [t.astype(F32) for t in split3(dots)]
    lines = jnp.concatenate(terms + [jnp.zeros((EXTRA - 3, dots.shape[1]), F32)], axis=0).astype(BF16)
    rows = dir_refs[0].shape[1]
    for k, ref in enumerate(dir_refs):
        ref[:cols] = low[:, k * rows : (k + 1) * rows]
        ref[cols:] = lines[:, k * rows : (k + 1) * rows]


def back_kernel(unit_ref, inv_ref, *refs):
    out_ref = refs[-1]
    cols, rows = unit_ref.shape
    total = refs[0][...].astype(F32)
    for ref in refs[1:-1]:
        total = total + ref[...].astype(F32)
    dots = total[cols : cols + 1] + total[cols + 1 : cols + 2] + total[cols + 2 : cols + 3]
    out_ref[...] = ((total[:cols] - unit_ref[...] * dots) * inv_ref[:, :rows]).astype(BF16)


def to_low(at_ref, total):
    first = total[:EXTRA]
    terms = [t.astype(F32) for t in split3(first[0:1] + first[1:2] + first[2:3])]
    row = jnp.concatenate(terms + [jnp.zeros((EXTRA - 3, LANES), F32)], axis=0)
    return jnp.where(at_ref[7] > 0, row, first).astype(BF16), total[EXTRA:].astype(BF16)


def sum_kernel(at_ref, parts_ref, *refs):
    out_ref = refs[-1]
    first, rest = to_low(at_ref, jnp.sum(parts_ref[...].astype(F32), axis=0))
    for k in range(out_ref.shape[0]):
        out_ref[k, :EXTRA] = first
        out_ref[k, EXTRA:] = rest


def feat_kernel(at_ref, weight_ref, *refs):
    out_ref, back_ref = refs[-2:]
    cols = refs[0].shape[0]
    for d, ref in enumerate(refs[:-2]):
        back_ref[pl.ds(pl.multiple_of(at_ref[8 + d] * cols, 16), cols), :] = ref[...]
    out_ref[...] = lax.dot_general(
        back_ref[...], weight_ref[...], (((0,), (1,)), ((), ())), preferred_element_type=F32
    ).astype(BF16)


def final_kernel(at_loss, pairs, full_ref, head_ref, loss_ref):
    cols, width = head_ref.shape
    tiles = width // LANES
    for k in range(tiles):
        head_ref[:, k * LANES : (k + 1) * LANES] = full_ref[k * cols : (k + 1) * cols]
    total = jnp.sum(full_ref[at_loss : at_loss + EXTRA].astype(F32), axis=0, keepdims=True)
    loss_ref[...] = jnp.sum(total, axis=1, keepdims=True) / pairs


def shift_by(x, axis, step):
    n = lax.axis_size(axis)
    return lax.ppermute(x, axis, [(k, (k + step) % n) for k in range(n)])


def local(img_feat, head_weight, text_embed, log_temp, logit_bias):
    rows, width = img_feat.shape
    quarter = text_embed.shape[0]
    ny, nx, nzh, nzl, nc = (lax.axis_size(a) for a in ("y", "x", "zh", "zl", "c"))
    nrep = nzl * nc
    plane = nx * ny
    cols = width // nrep
    images = nzh * rows
    tiles = width // LANES
    y_at, x_at, zl_at, c_at = (lax.axis_index(a) for a in ("y", "x", "zl", "c"))
    rep_at = zl_at * nc + c_at
    piece = -(-(tiles * cols) // (plane * 8)) * 8
    at_loss = -(-(tiles * cols) // piece) * piece
    assert at_loss < plane * piece
    at = jnp.stack(
        [
            rep_at,
            0 * rep_at,
            y_at * quarter,
            rep_at * quarter,
            quarter + 0 * rep_at,
            c_at,
            zl_at,
            (y_at * nx + x_at == at_loss // piece).astype(jnp.int32),
        ]
        + [rep_at ^ d for d in range(nrep)]
    ).astype(jnp.int32)
    par = jnp.stack([jnp.exp(log_temp[0]), logit_bias[0]])

    copies = call(text_kernel, shape((ny * quarter, width), BF16), text_embed)
    part = rows // nc
    def place(z, low, core):
        return (z % nzh * nzl + low) * nc + core

    near = []
    cross = []
    for z in range(nzh):
        near += [(place(z, 1, k), place(z + 1, k, 0)) for k in range(nc)]
        near += [(place(z, 0, k), place(z - 1, k, 1)) for k in range(nc)]
        cross += [(place(z, 1, k), place(z + 2, 0, k)) for k in range(nc)]
        cross += [(place(z, 0, k), place(z - 2, 1, k)) for k in range(nc)]
    half_rows = lax.dynamic_slice_in_dim(img_feat, c_at * part, part, 0)
    line = ("zh", "zl", "c")
    across = lax.ppermute(half_rows, line, cross)
    beside = lax.ppermute(img_feat, line, near)
    fetched = jnp.concatenate([beside, across], axis=0)
    own = to_all(copies, "y")
    far = shift_by(own, "x", 2)
    left = shift_by(own, "x", 1)
    right = shift_by(own, "x", -1)
    swapped = lax.ppermute(fetched, "c", [(0, 1), (1, 0)])

    unit, low, inv, own_unit, col_unit, feats = call(
        image_kernel,
        [
            shape((width, images), F32),
            shape((width, images), BF16),
            shape((1, images), F32),
            shape((cols, rows), F32),
            shape((cols, images), F32),
            shape((images, width), BF16),
        ],
        at,
        head_weight,
        img_feat,
        fetched,
        swapped,
        smem=1,
        flops=2 * width,
    )
    acc, loss_row = call(
        first_kernel,
        [shape((width, images), F32), shape((1, images), F32)],
        at,
        par,
        own,
        left,
        low,
        smem=2,
        flops=8 * width * images * own.shape[0],
    )
    keep, send = call(
        second_kernel,
        [shape((2 * cols + EXTRA, images), F32), shape((2 * cols + EXTRA, images), BF16)],
        at,
        par,
        right,
        far,
        low,
        unit,
        acc,
        loss_row,
        smem=2,
        flops=8 * width * images * own.shape[0],
        scratch_shapes=[pltpu.VMEM((width, images), F32)],
    )
    got = lax.ppermute(send, "c", [(0, 1), (1, 0)])
    keep2, send2 = call(
        middle_kernel,
        [shape((cols + EXTRA, images), F32), shape((cols + EXTRA, images), BF16)],
        at,
        keep,
        got,
        smem=1,
    )
    got2 = lax.ppermute(send2, "zl", [(0, 1), (1, 0)])
    flat, *dirs = call(
        functools.partial(head_kernel, at_loss),
        [shape((plane * piece, LANES), BF16)] + [shape((cols + EXTRA, rows), BF16)] * nzh,
        keep2,
        got2,
        col_unit,
        inv,
        feats,
        flops=2 * cols * images * width,
    )

    dirs = [dirs[0]] + [shift_by(dirs[s], "zh", -s) for s in range(1, nzh)]
    back = call(back_kernel, shape((cols, rows), BF16), own_unit, inv, *dirs)

    parts = to_all(flat, ("y", "x")).reshape(plane, piece, LANES)
    part = pl.pallas_call(
        sum_kernel,
        out_shape=shape((nzh, piece, LANES), BF16),
        in_specs=[SMEM, VMEM, pl.BlockSpec(memory_space=pl.ANY)],
        out_specs=VMEM,
    )(at, parts, back)
    part = to_all(part, "zh")
    low_part = call(sum_kernel, shape((plane, piece, LANES), BF16), at, part, smem=1)
    full = to_all(low_part.reshape(plane * piece, LANES), ("y", "x"))
    group = rows * plane * nzh
    head_grad, loss = call(
        functools.partial(final_kernel, at_loss, float(group) * float(group)),
        [shape((cols, width), BF16), shape((1, 1), F32)],
        full,
    )

    backs = [back]
    for d in range(1, nrep):
        backs.append(lax.ppermute(back, ("zl", "c"), [(k, k ^ d) for k in range(nrep)]))
    feat_grad = call(
        feat_kernel,
        shape((rows, width), BF16),
        at,
        head_weight,
        *backs,
        smem=1,
        flops=2 * rows * width * width,
        scratch_shapes=[pltpu.VMEM((width, rows), BF16)],
    )
    return (loss.reshape(1), feat_grad, head_grad.T)


def solution(mesh):
    devices = mesh.devices.reshape(8, 4, 4, 2, 2)
    fine = Mesh(devices, ("y", "x", "zh", "zl", "c"))
    batch, rep = (("y", "x", "zh"), ("zl", "c"))
    in_specs = (P(batch, None), P(), P(batch + rep, None), P(), P())
    out_specs = (P(), P(batch, None), P(None, rep))
    return jax.shard_map(local, mesh=fine, in_specs=in_specs, out_specs=out_specs, check_vma=False)
```

```python
import functools

import jax
import jax.numpy as jnp
from jax import lax
from jax.experimental import pallas as pl
from jax.experimental.pallas import tpu as pltpu
from jax.sharding import Mesh
from jax.sharding import PartitionSpec as P

EPS = 1e-06
BF16 = jnp.bfloat16
F32 = jnp.float32
LANES = 128
EXTRA = 16
VMEM = pl.BlockSpec(memory_space=pltpu.VMEM)
SMEM = pl.BlockSpec(memory_space=pltpu.SMEM)


def call(body, outs, *args, smem=0, flops=0, limit=16, **kwargs):
    many = isinstance(outs, (tuple, list))
    specs = [SMEM] * smem + [VMEM] * (len(args) - smem)
    size = sum(a.size * a.dtype.itemsize for a in args)
    return pl.pallas_call(
        body,
        out_shape=outs,
        in_specs=specs,
        out_specs=[VMEM] * len(outs) if many else VMEM,
        cost_estimate=pl.CostEstimate(flops=flops, bytes_accessed=size, transcendentals=0),
        compiler_params=pltpu.CompilerParams(vmem_limit_bytes=limit * 2**20),
        **kwargs,
    )(*args)


def shape(dims, dtype):
    return jax.ShapeDtypeStruct(dims, dtype)


def split3(value):
    hi = value.astype(BF16)
    rest = value - hi.astype(F32)
    mid = rest.astype(BF16)
    low = (rest - mid.astype(F32)).astype(BF16)
    return [hi, mid, low]


def to_all(copies, axes):
    return lax.all_to_all(copies, axes, 0, 0, tiled=True)


def text_kernel(text_ref, out_ref):
    values = text_ref[...].astype(F32)
    inverse = lax.rsqrt(jnp.sum(values * values, axis=-1, keepdims=True) + EPS)
    low = (values * inverse).astype(BF16)
    n = text_ref.shape[0]
    for k in range(out_ref.shape[0] // n):
        out_ref[k * n : (k + 1) * n] = low


def join_kernel(a_ref, b_ref, out_ref):
    out_ref[: a_ref.shape[0]] = a_ref[...]
    out_ref[a_ref.shape[0] :] = b_ref[...]


def image_kernel(at_ref, wt_ref, own_ref, fetched_ref, swapped_ref, *refs):
    unit_ref, low_ref, inv_ref, own_unit_ref, cols_ref, feats_ref = refs
    rows = own_ref.shape[0]
    part = rows // 2
    c = at_ref[5]
    feats_ref[:rows] = own_ref[...]
    for k, ref in ((c, fetched_ref), (1 - c, swapped_ref)):
        feats_ref[pl.ds(pl.multiple_of((1 + 2 * k) * rows, 16), rows), :] = ref[:rows]
        feats_ref[pl.ds(pl.multiple_of(2 * rows + k * part, 16), part), :] = ref[rows:]
    head = lax.dot_general(
        wt_ref[...], feats_ref[...], (((0,), (1,)), ((), ())), preferred_element_type=F32
    )
    inv = lax.rsqrt(jnp.sum(head * head, axis=0, keepdims=True) + EPS)
    unit = head * inv
    unit_ref[...] = unit
    low_ref[...] = unit.astype(BF16)
    inv_ref[...] = inv
    cols = cols_ref.shape[0]
    start = pl.multiple_of(at_ref[0] * cols, 16)
    cols_ref[...] = unit_ref[pl.ds(start, cols), :]
    own_unit_ref[...] = unit_ref[pl.ds(start, cols), :rows]


def pairs(par_ref, texts, low_ref, own=None):
    z = par_ref[0] * jnp.dot(texts, low_ref[...], preferred_element_type=F32) + par_ref[1]
    v = z if own is None else jnp.where(own, -z, z)
    e = jnp.exp(-jnp.abs(v))
    one = 1.0 + e
    series = e * (1.0 - e * (0.5 - e * (1.0 / 3.0 - e * (0.25 - e * 0.2))))
    log1p = jnp.where(e < 0.03, series, jnp.log(one))
    soft = jnp.maximum(v, 0.0) + log1p
    s = jnp.where(v >= 0.0, 1.0, e) / one
    slope = (s if own is None else jnp.where(own, -s, s)).astype(BF16)
    return slope, jnp.sum(soft, axis=0, keepdims=True)


def turn(texts, slope):
    return lax.dot_general(texts, slope, (((0,), (0,)), ((), ())), preferred_element_type=F32)


def first_kernel(at_ref, par_ref, own_ref, left_ref, low_ref, acc_ref, loss_ref):
    size = (own_ref.shape[0], low_ref.shape[1])
    col = lax.broadcasted_iota(jnp.int32, size, 0) - at_ref[2]
    row = lax.broadcasted_iota(jnp.int32, size, 1) - at_ref[3]
    own = (row == col) & (col >= 0) & (col < at_ref[4])
    slope, loss = pairs(par_ref, own_ref[...], low_ref, own)
    more_slope, more = pairs(par_ref, left_ref[...], low_ref)
    acc_ref[...] = turn(own_ref[...], slope) + turn(left_ref[...], more_slope)
    loss_ref[...] = loss + more


def next_kernel(par_ref, texts_ref, low_ref, acc_in_ref, loss_in_ref, acc_ref, loss_ref):
    slope, loss = pairs(par_ref, texts_ref[...], low_ref)
    acc_ref[...] = acc_in_ref[...] + turn(texts_ref[...], slope)
    loss_ref[...] = loss_in_ref[...] + loss


def last_kernel(at_ref, par_ref, texts_ref, low_ref, unit_ref, acc_ref, loss_ref, keep_ref, send_ref, sum_ref):
    scale = par_ref[0]
    slope, loss = pairs(par_ref, texts_ref[...], low_ref)
    loss = loss_ref[...] + loss
    total = scale * (acc_ref[...] + turn(texts_ref[...], slope))
    sum_ref[...] = total
    dots = jnp.sum(unit_ref[...] * total, axis=0, keepdims=True)
    cols = (keep_ref.shape[0] - EXTRA) // 2
    c = at_ref[5]
    for k in range(2):
        mine = pl.multiple_of((2 * k + c) * cols, 16)
        other = pl.multiple_of((2 * k + 1 - c) * cols, 16)
        keep_ref[k * cols : (k + 1) * cols] = sum_ref[pl.ds(mine, cols), :]
        send_ref[k * cols : (k + 1) * cols] = sum_ref[pl.ds(other, cols), :].astype(BF16)
    pack(keep_ref, send_ref, 2 * cols, dots, loss)


def pack(keep_ref, send_ref, at, dots, loss):
    zeros = jnp.zeros((EXTRA - 2, dots.shape[1]), F32)
    keep_ref[at : at + EXTRA] = jnp.concatenate([dots, loss, zeros], axis=0)
    terms = [t.astype(F32) for t in split3(dots) + split3(loss)]
    zeros = jnp.zeros((EXTRA - 6, dots.shape[1]), F32)
    send_ref[at : at + EXTRA] = jnp.concatenate(terms + [zeros], axis=0).astype(BF16)


def unpack(keep_ref, got_ref, at):
    kept = keep_ref[at : at + EXTRA]
    got = got_ref[at : at + EXTRA].astype(F32)
    dots = kept[0:1] + (got[0:1] + got[1:2] + got[2:3])
    loss = kept[1:2] + (got[3:4] + got[4:5] + got[5:6])
    return dots, loss


def middle_kernel(at_ref, keep_ref, got_ref, keep2_ref, send2_ref):
    cols = keep2_ref.shape[0] - EXTRA
    dots, loss = unpack(keep_ref, got_ref, 2 * cols)
    zl = at_ref[6]
    mine = pl.multiple_of(zl * cols, 16)
    other = pl.multiple_of((1 - zl) * cols, 16)
    keep2_ref[:cols] = keep_ref[pl.ds(mine, cols), :] + got_ref[pl.ds(mine, cols), :].astype(F32)
    send2_ref[:cols] = (
        keep_ref[pl.ds(other, cols), :] + got_ref[pl.ds(other, cols), :].astype(F32)
    ).astype(BF16)
    pack(keep2_ref, send2_ref, cols, dots, loss)


def head_kernel(at_loss, keep_ref, got_ref, unit_ref, inv_ref, feats_ref, flat_ref, *dir_refs):
    cols = keep_ref.shape[0] - EXTRA
    dots, loss = unpack(keep_ref, got_ref, cols)
    total = keep_ref[:cols] + got_ref[:cols].astype(F32)
    back = ((total - unit_ref[...] * dots) * inv_ref[...]).astype(BF16)
    head = jnp.dot(back, feats_ref[...], preferred_element_type=F32).astype(BF16)
    tiles = feats_ref.shape[1] // LANES
    for k in range(tiles):
        flat_ref[k * cols : (k + 1) * cols] = head[:, k * LANES : (k + 1) * LANES]
    part = loss[:, :LANES]
    for k in range(1, loss.shape[1] // LANES):
        part = part + loss[:, k * LANES : (k + 1) * LANES]
    terms = [t.astype(F32) for t in split3(part)]
    tail = jnp.concatenate(terms + [jnp.zeros((EXTRA - 3, LANES), F32)], axis=0)
    end = tiles * cols
    flat_ref[end:at_loss] = jnp.zeros((at_loss - end, LANES), BF16)
    flat_ref[at_loss : at_loss + EXTRA] = tail.astype(BF16)
    flat_ref[at_loss + EXTRA :] = jnp.zeros((flat_ref.shape[0] - at_loss - EXTRA, LANES), BF16)
    low = total.astype(BF16)
    terms = [t.astype(F32) for t in split3(dots)]
    lines = jnp.concatenate(terms + [jnp.zeros((EXTRA - 3, dots.shape[1]), F32)], axis=0).astype(BF16)
    rows = dir_refs[0].shape[1]
    for k, ref in enumerate(dir_refs):
        ref[:cols] = low[:, k * rows : (k + 1) * rows]
        ref[cols:] = lines[:, k * rows : (k + 1) * rows]


def back_kernel(unit_ref, inv_ref, *refs):
    out_ref = refs[-1]
    cols, rows = unit_ref.shape
    total = refs[0][...].astype(F32)
    for ref in refs[1:-1]:
        total = total + ref[...].astype(F32)
    dots = total[cols : cols + 1] + total[cols + 1 : cols + 2] + total[cols + 2 : cols + 3]
    out_ref[...] = ((total[:cols] - unit_ref[...] * dots) * inv_ref[:, :rows]).astype(BF16)


def to_low(at_ref, total):
    first = total[:EXTRA]
    terms = [t.astype(F32) for t in split3(first[0:1] + first[1:2] + first[2:3])]
    row = jnp.concatenate(terms + [jnp.zeros((EXTRA - 3, LANES), F32)], axis=0)
    return jnp.where(at_ref[7] > 0, row, first).astype(BF16), total[EXTRA:].astype(BF16)


def sum_kernel(at_ref, parts_ref, *refs):
    out_ref = refs[-1]
    first, rest = to_low(at_ref, jnp.sum(parts_ref[...].astype(F32), axis=0))
    for k in range(out_ref.shape[0]):
        out_ref[k, :EXTRA] = first
        out_ref[k, EXTRA:] = rest


def feat_kernel(at_ref, weight_ref, *refs):
    out_ref, back_ref = refs[-2:]
    cols = refs[0].shape[0]
    for d, ref in enumerate(refs[:-2]):
        back_ref[pl.ds(pl.multiple_of(at_ref[8 + d] * cols, 16), cols), :] = ref[...]
    out_ref[...] = lax.dot_general(
        back_ref[...], weight_ref[...], (((0,), (1,)), ((), ())), preferred_element_type=F32
    ).astype(BF16)


def final_kernel(at_loss, pairs, full_ref, head_ref, loss_ref):
    cols, width = head_ref.shape
    tiles = width // LANES
    for k in range(tiles):
        head_ref[:, k * LANES : (k + 1) * LANES] = full_ref[k * cols : (k + 1) * cols]
    total = jnp.sum(full_ref[at_loss : at_loss + EXTRA].astype(F32), axis=0, keepdims=True)
    loss_ref[...] = jnp.sum(total, axis=1, keepdims=True) / pairs


def shift_by(x, axis, step):
    n = lax.axis_size(axis)
    return lax.ppermute(x, axis, [(k, (k + step) % n) for k in range(n)])


def local(img_feat, head_weight, text_embed, log_temp, logit_bias):
    rows, width = img_feat.shape
    quarter = text_embed.shape[0]
    ny, nx, nzh, nzl, nc = (lax.axis_size(a) for a in ("y", "x", "zh", "zl", "c"))
    nrep = nzl * nc
    plane = nx * ny
    cols = width // nrep
    images = nzh * rows
    tiles = width // LANES
    y_at, x_at, zl_at, c_at = (lax.axis_index(a) for a in ("y", "x", "zl", "c"))
    rep_at = zl_at * nc + c_at
    piece = -(-(tiles * cols) // (plane * 8)) * 8
    at_loss = -(-(tiles * cols) // piece) * piece
    assert at_loss < plane * piece
    at = jnp.stack(
        [
            rep_at,
            0 * rep_at,
            y_at * quarter,
            rep_at * quarter,
            quarter + 0 * rep_at,
            c_at,
            zl_at,
            (y_at * nx + x_at == at_loss // piece).astype(jnp.int32),
        ]
        + [rep_at ^ d for d in range(nrep)]
    ).astype(jnp.int32)
    par = jnp.stack([jnp.exp(log_temp[0]), logit_bias[0]])

    copies = call(text_kernel, shape((ny * quarter, width), BF16), text_embed)
    part = rows // nc
    def place(z, low, core):
        return (z % nzh * nzl + low) * nc + core

    near = []
    cross = []
    for z in range(nzh):
        near += [(place(z, 1, k), place(z + 1, k, 0)) for k in range(nc)]
        near += [(place(z, 0, k), place(z - 1, k, 1)) for k in range(nc)]
        cross += [(place(z, 1, k), place(z + 2, 0, k)) for k in range(nc)]
        cross += [(place(z, 0, k), place(z - 2, 1, k)) for k in range(nc)]
    half_rows = lax.dynamic_slice_in_dim(img_feat, c_at * part, part, 0)
    line = ("zh", "zl", "c")
    across = lax.ppermute(half_rows, line, cross)
    beside = lax.ppermute(img_feat, line, near)
    fetched = call(
        join_kernel, shape((beside.shape[0] + across.shape[0], width), BF16), beside, across
    )
    own = to_all(copies, "y")
    far = shift_by(own, "x", 2)
    left = shift_by(own, "x", 1)
    right = shift_by(own, "x", -1)
    swapped = lax.ppermute(fetched, "c", [(0, 1), (1, 0)])

    unit, low, inv, own_unit, col_unit, feats = call(
        image_kernel,
        [
            shape((width, images), F32),
            shape((width, images), BF16),
            shape((1, images), F32),
            shape((cols, rows), F32),
            shape((cols, images), F32),
            shape((images, width), BF16),
        ],
        at,
        head_weight,
        img_feat,
        fetched,
        swapped,
        smem=1,
        flops=2 * width,
    )
    acc, loss_row = call(
        first_kernel,
        [shape((width, images), F32), shape((1, images), F32)],
        at,
        par,
        own,
        left,
        low,
        smem=2,
        flops=width,
    )
    acc, loss_row = call(
        next_kernel,
        [shape((width, images), F32), shape((1, images), F32)],
        par,
        right,
        low,
        acc,
        loss_row,
        smem=1,
        flops=width,
    )
    keep, send = call(
        last_kernel,
        [shape((2 * cols + EXTRA, images), F32), shape((2 * cols + EXTRA, images), BF16)],
        at,
        par,
        far,
        low,
        unit,
        acc,
        loss_row,
        smem=2,
        flops=4 * width * images * own.shape[0],
        scratch_shapes=[pltpu.VMEM((width, images), F32)],
    )
    got = lax.ppermute(send, "c", [(0, 1), (1, 0)])
    keep2, send2 = call(
        middle_kernel,
        [shape((cols + EXTRA, images), F32), shape((cols + EXTRA, images), BF16)],
        at,
        keep,
        got,
        smem=1,
    )
    got2 = lax.ppermute(send2, "zl", [(0, 1), (1, 0)])
    flat, *dirs = call(
        functools.partial(head_kernel, at_loss),
        [shape((plane * piece, LANES), BF16)] + [shape((cols + EXTRA, rows), BF16)] * nzh,
        keep2,
        got2,
        col_unit,
        inv,
        feats,
        flops=2 * cols * images * width,
    )

    dirs = [dirs[0]] + [shift_by(dirs[s], "zh", -s) for s in range(1, nzh)]
    back = call(back_kernel, shape((cols, rows), BF16), own_unit, inv, *dirs)

    parts = to_all(flat, ("y", "x")).reshape(plane, piece, LANES)
    part = pl.pallas_call(
        sum_kernel,
        out_shape=shape((nzh, piece, LANES), BF16),
        in_specs=[SMEM, VMEM, pl.BlockSpec(memory_space=pl.ANY)],
        out_specs=VMEM,
    )(at, parts, back)
    part = to_all(part, "zh")
    low_part = call(sum_kernel, shape((plane, piece, LANES), BF16), at, part, smem=1)
    full = to_all(low_part.reshape(plane * piece, LANES), ("y", "x"))
    group = rows * plane * nzh
    head_grad, loss = call(
        functools.partial(final_kernel, at_loss, float(group) * float(group)),
        [shape((cols, width), BF16), shape((1, 1), F32)],
        full,
    )

    backs = [back]
    for d in range(1, nrep):
        backs.append(lax.ppermute(back, ("zl", "c"), [(k, k ^ d) for k in range(nrep)]))
    feat_grad = call(
        feat_kernel,
        shape((rows, width), BF16),
        at,
        head_weight,
        *backs,
        smem=1,
        flops=2 * rows * width * width,
        scratch_shapes=[pltpu.VMEM((width, rows), BF16)],
    )
    return (loss.reshape(1), feat_grad, head_grad.T)


def solution(mesh):
    devices = mesh.devices.reshape(8, 4, 4, 2, 2)
    fine = Mesh(devices, ("y", "x", "zh", "zl", "c"))
    batch, rep = (("y", "x", "zh"), ("zl", "c"))
    in_specs = (P(batch, None), P(), P(batch + rep, None), P(), P())
    out_specs = (P(), P(batch, None), P(None, rep))
    return jax.shard_map(local, mesh=fine, in_specs=in_specs, out_specs=out_specs, check_vma=False)
```

```python
import functools

import jax
import jax.numpy as jnp
from jax import lax
from jax.experimental import pallas as pl
from jax.experimental.pallas import tpu as pltpu
from jax.sharding import Mesh
from jax.sharding import PartitionSpec as P

EPS = 1e-06
BF16 = jnp.bfloat16
F32 = jnp.float32
LANES = 128
EXTRA = 16
VMEM = pl.BlockSpec(memory_space=pltpu.VMEM)
SMEM = pl.BlockSpec(memory_space=pltpu.SMEM)


def call(body, outs, *args, smem=0, flops=0, limit=16, **kwargs):
    many = isinstance(outs, (tuple, list))
    specs = [SMEM] * smem + [VMEM] * (len(args) - smem)
    size = sum(a.size * a.dtype.itemsize for a in args)
    return pl.pallas_call(
        body,
        out_shape=outs,
        in_specs=specs,
        out_specs=[VMEM] * len(outs) if many else VMEM,
        cost_estimate=pl.CostEstimate(flops=flops, bytes_accessed=size, transcendentals=0),
        compiler_params=pltpu.CompilerParams(vmem_limit_bytes=limit * 2**20),
        **kwargs,
    )(*args)


def shape(dims, dtype):
    return jax.ShapeDtypeStruct(dims, dtype)


def split3(value):
    hi = value.astype(BF16)
    rest = value - hi.astype(F32)
    mid = rest.astype(BF16)
    low = (rest - mid.astype(F32)).astype(BF16)
    return [hi, mid, low]


def to_all(copies, axes):
    return lax.all_to_all(copies, axes, 0, 0, tiled=True)


def text_kernel(text_ref, out_ref):
    values = text_ref[...].astype(F32)
    inverse = lax.rsqrt(jnp.sum(values * values, axis=-1, keepdims=True) + EPS)
    low = (values * inverse).astype(BF16)
    n = text_ref.shape[0]
    for k in range(out_ref.shape[0] // n):
        out_ref[k * n : (k + 1) * n] = low


def join_kernel(a_ref, b_ref, out_ref):
    out_ref[: a_ref.shape[0]] = a_ref[...]
    out_ref[a_ref.shape[0] :] = b_ref[...]


def image_kernel(at_ref, weight_ref, own_ref, fetched_ref, swapped_ref, *refs):
    unit_ref, low_ref, inv_ref, own_unit_ref, cols_ref, feats_ref = refs
    rows = own_ref.shape[0]
    part = rows // 2
    c = at_ref[5]
    feats_ref[:rows] = own_ref[...]
    for k, ref in ((c, fetched_ref), (1 - c, swapped_ref)):
        feats_ref[pl.ds(pl.multiple_of((1 + 2 * k) * rows, 16), rows), :] = ref[:rows]
        feats_ref[pl.ds(pl.multiple_of(2 * rows + k * part, 16), part), :] = ref[rows:]
    head = lax.dot_general(
        weight_ref[...], feats_ref[...], (((0,), (1,)), ((), ())), preferred_element_type=F32
    )
    inv = lax.rsqrt(jnp.sum(head * head, axis=0, keepdims=True) + EPS)
    unit = head * inv
    unit_ref[...] = unit
    low_ref[...] = unit.astype(BF16)
    inv_ref[...] = inv
    cols = cols_ref.shape[0]
    start = pl.multiple_of(at_ref[0] * cols, 16)
    cols_ref[...] = unit_ref[pl.ds(start, cols), :]
    own_unit_ref[...] = unit_ref[pl.ds(start, cols), :rows]


def pairs(par_ref, texts, low_ref, own=None):
    z = par_ref[0] * jnp.dot(texts, low_ref[...], preferred_element_type=F32) + par_ref[1]
    v = z if own is None else jnp.where(own, -z, z)
    e = jnp.exp(-jnp.abs(v))
    one = 1.0 + e
    series = e * (1.0 - e * (0.5 - e * (1.0 / 3.0 - e * (0.25 - e * 0.2))))
    log1p = jnp.where(e < 0.03, series, jnp.log(one))
    soft = jnp.maximum(v, 0.0) + log1p
    s = jnp.where(v >= 0.0, 1.0, e) / one
    slope = (s if own is None else jnp.where(own, -s, s)).astype(BF16)
    return slope, jnp.sum(soft, axis=0, keepdims=True)


def turn(texts, slope):
    return lax.dot_general(texts, slope, (((0,), (0,)), ((), ())), preferred_element_type=F32)


def first_kernel(at_ref, par_ref, own_ref, left_ref, low_ref, acc_ref, loss_ref):
    size = (own_ref.shape[0], low_ref.shape[1])
    col = lax.broadcasted_iota(jnp.int32, size, 0) - at_ref[2]
    row = lax.broadcasted_iota(jnp.int32, size, 1) - at_ref[3]
    own = (row == col) & (col >= 0) & (col < at_ref[4])
    slope, loss = pairs(par_ref, own_ref[...], low_ref, own)
    more_slope, more = pairs(par_ref, left_ref[...], low_ref)
    acc_ref[...] = turn(own_ref[...], slope) + turn(left_ref[...], more_slope)
    loss_ref[...] = loss + more


def second_kernel(at_ref, par_ref, right_ref, far_ref, low_ref, unit_ref, acc_ref, loss_ref, keep_ref, send_ref, sum_ref):
    scale = par_ref[0]
    slope, loss = pairs(par_ref, right_ref[...], low_ref)
    more_slope, more = pairs(par_ref, far_ref[...], low_ref)
    loss = loss_ref[...] + loss + more
    total = scale * (acc_ref[...] + turn(right_ref[...], slope) + turn(far_ref[...], more_slope))
    sum_ref[...] = total
    dots = jnp.sum(unit_ref[...] * total, axis=0, keepdims=True)
    cols = (keep_ref.shape[0] - EXTRA) // 2
    c = at_ref[5]
    for k in range(2):
        mine = pl.multiple_of((2 * k + c) * cols, 16)
        other = pl.multiple_of((2 * k + 1 - c) * cols, 16)
        keep_ref[k * cols : (k + 1) * cols] = sum_ref[pl.ds(mine, cols), :]
        send_ref[k * cols : (k + 1) * cols] = sum_ref[pl.ds(other, cols), :].astype(BF16)
    pack(keep_ref, send_ref, 2 * cols, dots, loss)


def pack(keep_ref, send_ref, at, dots, loss):
    zeros = jnp.zeros((EXTRA - 2, dots.shape[1]), F32)
    keep_ref[at : at + EXTRA] = jnp.concatenate([dots, loss, zeros], axis=0)
    terms = [t.astype(F32) for t in split3(dots) + split3(loss)]
    zeros = jnp.zeros((EXTRA - 6, dots.shape[1]), F32)
    send_ref[at : at + EXTRA] = jnp.concatenate(terms + [zeros], axis=0).astype(BF16)


def unpack(keep_ref, got_ref, at):
    kept = keep_ref[at : at + EXTRA]
    got = got_ref[at : at + EXTRA].astype(F32)
    dots = kept[0:1] + (got[0:1] + got[1:2] + got[2:3])
    loss = kept[1:2] + (got[3:4] + got[4:5] + got[5:6])
    return dots, loss


def middle_kernel(at_ref, keep_ref, got_ref, keep2_ref, send2_ref):
    cols = keep2_ref.shape[0] - EXTRA
    dots, loss = unpack(keep_ref, got_ref, 2 * cols)
    zl = at_ref[6]
    mine = pl.multiple_of(zl * cols, 16)
    other = pl.multiple_of((1 - zl) * cols, 16)
    keep2_ref[:cols] = keep_ref[pl.ds(mine, cols), :] + got_ref[pl.ds(mine, cols), :].astype(F32)
    send2_ref[:cols] = (
        keep_ref[pl.ds(other, cols), :] + got_ref[pl.ds(other, cols), :].astype(F32)
    ).astype(BF16)
    pack(keep2_ref, send2_ref, cols, dots, loss)


def head_kernel(at_loss, keep_ref, got_ref, unit_ref, inv_ref, feats_ref, flat_ref, *dir_refs):
    cols = keep_ref.shape[0] - EXTRA
    dots, loss = unpack(keep_ref, got_ref, cols)
    total = keep_ref[:cols] + got_ref[:cols].astype(F32)
    back = ((total - unit_ref[...] * dots) * inv_ref[...]).astype(BF16)
    head = jnp.dot(back, feats_ref[...], preferred_element_type=F32).astype(BF16)
    tiles = feats_ref.shape[1] // LANES
    for k in range(tiles):
        flat_ref[k * cols : (k + 1) * cols] = head[:, k * LANES : (k + 1) * LANES]
    part = loss[:, :LANES]
    for k in range(1, loss.shape[1] // LANES):
        part = part + loss[:, k * LANES : (k + 1) * LANES]
    terms = [t.astype(F32) for t in split3(part)]
    tail = jnp.concatenate(terms + [jnp.zeros((EXTRA - 3, LANES), F32)], axis=0)
    end = tiles * cols
    flat_ref[end:at_loss] = jnp.zeros((at_loss - end, LANES), BF16)
    flat_ref[at_loss : at_loss + EXTRA] = tail.astype(BF16)
    flat_ref[at_loss + EXTRA :] = jnp.zeros((flat_ref.shape[0] - at_loss - EXTRA, LANES), BF16)
    low = total.astype(BF16)
    terms = [t.astype(F32) for t in split3(dots)]
    lines = jnp.concatenate(terms + [jnp.zeros((EXTRA - 3, dots.shape[1]), F32)], axis=0).astype(BF16)
    rows = dir_refs[0].shape[1]
    for k, ref in enumerate(dir_refs):
        ref[:cols] = low[:, k * rows : (k + 1) * rows]
        ref[cols:] = lines[:, k * rows : (k + 1) * rows]


def back_kernel(unit_ref, inv_ref, *refs):
    out_ref = refs[-1]
    cols, rows = unit_ref.shape
    total = refs[0][...].astype(F32)
    for ref in refs[1:-1]:
        total = total + ref[...].astype(F32)
    dots = total[cols : cols + 1] + total[cols + 1 : cols + 2] + total[cols + 2 : cols + 3]
    out_ref[...] = ((total[:cols] - unit_ref[...] * dots) * inv_ref[:, :rows]).astype(BF16)


def sum_kernel(parts_ref, after_ref, out_ref):
    total = jnp.sum(parts_ref[...].astype(F32), axis=0)
    for k in range(out_ref.shape[0]):
        out_ref[k] = total


def feat_kernel(at_ref, weight_ref, *refs):
    out_ref, back_ref = refs[-2:]
    cols = refs[0].shape[0]
    for d, ref in enumerate(refs[:-2]):
        back_ref[pl.ds(pl.multiple_of(at_ref[8 + d] * cols, 16), cols), :] = ref[...]
    out_ref[...] = lax.dot_general(
        back_ref[...], weight_ref[...], (((0,), (1,)), ((), ())), preferred_element_type=F32
    ).astype(BF16)


def last_sum_kernel(at_ref, parts_ref, out_ref):
    total = jnp.sum(parts_ref[...], axis=0)
    low = total.astype(BF16)
    first = total[:EXTRA]
    terms = [t.astype(F32) for t in split3(first[0:1] + first[1:2] + first[2:3])]
    row = jnp.concatenate(terms + [jnp.zeros((EXTRA - 3, LANES), F32)], axis=0).astype(BF16)
    first = jnp.where(at_ref[7] > 0, row.astype(F32), first).astype(BF16)
    for k in range(out_ref.shape[0]):
        out_ref[k, :EXTRA] = first
        out_ref[k, EXTRA:] = low[EXTRA:]


def final_kernel(at_loss, pairs, full_ref, head_ref, loss_ref):
    cols, width = head_ref.shape
    tiles = width // LANES
    for k in range(tiles):
        head_ref[:, k * LANES : (k + 1) * LANES] = full_ref[k * cols : (k + 1) * cols]
    total = jnp.sum(full_ref[at_loss : at_loss + EXTRA].astype(F32), axis=0, keepdims=True)
    loss_ref[...] = jnp.sum(total, axis=1, keepdims=True) / pairs


def shift_by(x, axis, step):
    n = lax.axis_size(axis)
    return lax.ppermute(x, axis, [(k, (k + step) % n) for k in range(n)])


def local(img_feat, head_weight, text_embed, log_temp, logit_bias):
    rows, width = img_feat.shape
    quarter = text_embed.shape[0]
    ny, nx, nzh, nzl, nc = (lax.axis_size(a) for a in ("y", "x", "zh", "zl", "c"))
    nrep = nzl * nc
    plane = nx * ny
    cols = width // nrep
    images = nzh * rows
    tiles = width // LANES
    y_at, x_at, zl_at, c_at = (lax.axis_index(a) for a in ("y", "x", "zl", "c"))
    rep_at = zl_at * nc + c_at
    piece = -(-(tiles * cols) // (plane * 8)) * 8
    at_loss = -(-(tiles * cols) // piece) * piece
    assert at_loss < plane * piece
    at = jnp.stack(
        [
            rep_at,
            0 * rep_at,
            y_at * quarter,
            rep_at * quarter,
            quarter + 0 * rep_at,
            c_at,
            zl_at,
            (y_at * nx + x_at == at_loss // piece).astype(jnp.int32),
        ]
        + [rep_at ^ d for d in range(nrep)]
    ).astype(jnp.int32)
    par = jnp.stack([jnp.exp(log_temp[0]), logit_bias[0]])

    copies = call(text_kernel, shape((ny * quarter, width), BF16), text_embed)
    part = rows // nc
    def place(z, low, core):
        return (z % nzh * nzl + low) * nc + core

    near = []
    cross = []
    for z in range(nzh):
        near += [(place(z, 1, k), place(z + 1, k, 0)) for k in range(nc)]
        near += [(place(z, 0, k), place(z - 1, k, 1)) for k in range(nc)]
        cross += [(place(z, 1, k), place(z + 2, 0, k)) for k in range(nc)]
        cross += [(place(z, 0, k), place(z - 2, 1, k)) for k in range(nc)]
    half_rows = lax.dynamic_slice_in_dim(img_feat, c_at * part, part, 0)
    line = ("zh", "zl", "c")
    across = lax.ppermute(half_rows, line, cross)
    beside = lax.ppermute(img_feat, line, near)
    fetched = call(
        join_kernel, shape((beside.shape[0] + across.shape[0], width), BF16), beside, across
    )
    own = to_all(copies, "y")
    far = shift_by(own, "x", 2)
    left = shift_by(own, "x", 1)
    right = shift_by(own, "x", -1)
    swapped = lax.ppermute(fetched, "c", [(0, 1), (1, 0)])

    unit, low, inv, own_unit, col_unit, feats = call(
        image_kernel,
        [
            shape((width, images), F32),
            shape((width, images), BF16),
            shape((1, images), F32),
            shape((cols, rows), F32),
            shape((cols, images), F32),
            shape((images, width), BF16),
        ],
        at,
        head_weight,
        img_feat,
        fetched,
        swapped,
        smem=1,
        flops=2 * width,
    )
    acc, loss_row = call(
        first_kernel,
        [shape((width, images), F32), shape((1, images), F32)],
        at,
        par,
        own,
        left,
        low,
        smem=2,
        flops=width,
    )
    keep, send = call(
        second_kernel,
        [shape((2 * cols + EXTRA, images), F32), shape((2 * cols + EXTRA, images), BF16)],
        at,
        par,
        right,
        far,
        low,
        unit,
        acc,
        loss_row,
        smem=2,
        flops=width,
        scratch_shapes=[pltpu.VMEM((width, images), F32)],
    )
    got = lax.ppermute(send, "c", [(0, 1), (1, 0)])
    keep2, send2 = call(
        middle_kernel,
        [shape((cols + EXTRA, images), F32), shape((cols + EXTRA, images), BF16)],
        at,
        keep,
        got,
        smem=1,
    )
    got2 = lax.ppermute(send2, "zl", [(0, 1), (1, 0)])
    flat, *dirs = call(
        functools.partial(head_kernel, at_loss),
        [shape((plane * piece, LANES), BF16)] + [shape((cols + EXTRA, rows), BF16)] * nzh,
        keep2,
        got2,
        col_unit,
        inv,
        feats,
        flops=2 * cols * images * width,
    )

    dirs = [dirs[0]] + [shift_by(dirs[s], "zh", -s) for s in range(1, nzh)]
    back = call(back_kernel, shape((cols, rows), BF16), own_unit, inv, *dirs)

    parts = to_all(flat, ("y", "x")).reshape(plane, piece, LANES)
    part = pl.pallas_call(
        sum_kernel,
        out_shape=shape((nzh, piece, LANES), F32),
        in_specs=[VMEM, pl.BlockSpec(memory_space=pl.ANY)],
        out_specs=VMEM,
    )(parts, back)
    part = to_all(part, "zh")
    low_part = call(last_sum_kernel, shape((plane, piece, LANES), BF16), at, part, smem=1)
    full = to_all(low_part.reshape(plane * piece, LANES), ("y", "x"))
    group = rows * plane * nzh
    head_grad, loss = call(
        functools.partial(final_kernel, at_loss, float(group) * float(group)),
        [shape((cols, width), BF16), shape((1, 1), F32)],
        full,
    )

    backs = [back]
    for d in range(1, nrep):
        backs.append(lax.ppermute(back, ("zl", "c"), [(k, k ^ d) for k in range(nrep)]))
    feat_grad = call(
        feat_kernel,
        shape((rows, width), BF16),
        at,
        head_weight,
        *backs,
        smem=1,
        flops=2 * rows * width * width,
        scratch_shapes=[pltpu.VMEM((width, rows), BF16)],
    )
    return (loss.reshape(1), feat_grad, head_grad.T)


def solution(mesh):
    devices = mesh.devices.reshape(8, 4, 4, 2, 2)
    fine = Mesh(devices, ("y", "x", "zh", "zl", "c"))
    batch, rep = (("y", "x", "zh"), ("zl", "c"))
    in_specs = (P(batch, None), P(), P(batch + rep, None), P(), P())
    out_specs = (P(), P(batch, None), P(None, rep))
    return jax.shard_map(local, mesh=fine, in_specs=in_specs, out_specs=out_specs, check_vma=False)
```

```python
import functools

import jax
import jax.numpy as jnp
from jax import lax
from jax.experimental import pallas as pl
from jax.experimental.pallas import tpu as pltpu
from jax.sharding import Mesh
from jax.sharding import PartitionSpec as P

EPS = 1e-06
BF16 = jnp.bfloat16
F32 = jnp.float32
LANES = 128
EXTRA = 16
VMEM = pl.BlockSpec(memory_space=pltpu.VMEM)
SMEM = pl.BlockSpec(memory_space=pltpu.SMEM)


def call(body, outs, *args, smem=0, flops=0, limit=16, **kwargs):
    many = isinstance(outs, (tuple, list))
    specs = [SMEM] * smem + [VMEM] * (len(args) - smem)
    size = sum(a.size * a.dtype.itemsize for a in args)
    return pl.pallas_call(
        body,
        out_shape=outs,
        in_specs=specs,
        out_specs=[VMEM] * len(outs) if many else VMEM,
        cost_estimate=pl.CostEstimate(flops=flops, bytes_accessed=size, transcendentals=0),
        compiler_params=pltpu.CompilerParams(vmem_limit_bytes=limit * 2**20),
        **kwargs,
    )(*args)


def shape(dims, dtype):
    return jax.ShapeDtypeStruct(dims, dtype)


def split3(value):
    hi = value.astype(BF16)
    rest = value - hi.astype(F32)
    mid = rest.astype(BF16)
    low = (rest - mid.astype(F32)).astype(BF16)
    return [hi, mid, low]


def to_all(copies, axes):
    return lax.all_to_all(copies, axes, 0, 0, tiled=True)


def text_kernel(text_ref, out_ref):
    values = text_ref[...].astype(F32)
    inverse = lax.rsqrt(jnp.sum(values * values, axis=-1, keepdims=True) + EPS)
    low = (values * inverse).astype(BF16)
    n = text_ref.shape[0]
    for k in range(out_ref.shape[0] // n):
        out_ref[k * n : (k + 1) * n] = low


def image_kernel(at_ref, wt_ref, own_ref, fetched_ref, swapped_ref, *refs):
    unit_ref, low_ref, inv_ref, own_unit_ref, cols_ref, feats_ref = refs
    rows = own_ref.shape[0]
    part = rows // 2
    c = at_ref[5]
    feats_ref[:rows] = own_ref[...]
    for k, ref in ((c, fetched_ref), (1 - c, swapped_ref)):
        feats_ref[pl.ds(pl.multiple_of((1 + 2 * k) * rows, 16), rows), :] = ref[:rows]
        feats_ref[pl.ds(pl.multiple_of(2 * rows + k * part, 16), part), :] = ref[rows:]
    head = lax.dot_general(
        wt_ref[...], feats_ref[...], (((1,), (1,)), ((), ())), preferred_element_type=F32
    )
    inv = lax.rsqrt(jnp.sum(head * head, axis=0, keepdims=True) + EPS)
    unit = head * inv
    unit_ref[...] = unit
    low_ref[...] = unit.astype(BF16)
    inv_ref[...] = inv
    cols = cols_ref.shape[0]
    start = pl.multiple_of(at_ref[0] * cols, 16)
    cols_ref[...] = unit_ref[pl.ds(start, cols), :]
    own_unit_ref[...] = unit_ref[pl.ds(start, cols), :rows]


def pairs(par_ref, texts, low_ref, own=None):
    z = par_ref[0] * jnp.dot(texts, low_ref[...], preferred_element_type=F32) + par_ref[1]
    v = z if own is None else jnp.where(own, -z, z)
    e = jnp.exp(-jnp.abs(v))
    one = 1.0 + e
    series = e * (1.0 - e * (0.5 - e * (1.0 / 3.0 - e * (0.25 - e * 0.2))))
    log1p = jnp.where(e < 0.03, series, jnp.log(one))
    soft = jnp.maximum(v, 0.0) + log1p
    s = jnp.where(v >= 0.0, 1.0, e) / one
    slope = (s if own is None else jnp.where(own, -s, s)).astype(BF16)
    return slope, jnp.sum(soft, axis=0, keepdims=True)


def turn(texts, slope):
    return lax.dot_general(texts, slope, (((0,), (0,)), ((), ())), preferred_element_type=F32)


def first_kernel(at_ref, par_ref, own_ref, left_ref, low_ref, acc_ref, loss_ref):
    size = (own_ref.shape[0], low_ref.shape[1])
    col = lax.broadcasted_iota(jnp.int32, size, 0) - at_ref[2]
    row = lax.broadcasted_iota(jnp.int32, size, 1) - at_ref[3]
    own = (row == col) & (col >= 0) & (col < at_ref[4])
    slope, loss = pairs(par_ref, own_ref[...], low_ref, own)
    more_slope, more = pairs(par_ref, left_ref[...], low_ref)
    acc_ref[...] = turn(own_ref[...], slope) + turn(left_ref[...], more_slope)
    loss_ref[...] = loss + more


def second_kernel(at_ref, par_ref, right_ref, far_ref, low_ref, unit_ref, acc_ref, loss_ref, keep_ref, send_ref, sum_ref):
    scale = par_ref[0]
    slope, loss = pairs(par_ref, right_ref[...], low_ref)
    more_slope, more = pairs(par_ref, far_ref[...], low_ref)
    loss = loss_ref[...] + loss + more
    total = scale * (acc_ref[...] + turn(right_ref[...], slope) + turn(far_ref[...], more_slope))
    sum_ref[...] = total
    dots = jnp.sum(unit_ref[...] * total, axis=0, keepdims=True)
    cols = (keep_ref.shape[0] - EXTRA) // 2
    c = at_ref[5]
    for k in range(2):
        mine = pl.multiple_of((2 * k + c) * cols, 16)
        other = pl.multiple_of((2 * k + 1 - c) * cols, 16)
        keep_ref[k * cols : (k + 1) * cols] = sum_ref[pl.ds(mine, cols), :]
        send_ref[k * cols : (k + 1) * cols] = sum_ref[pl.ds(other, cols), :].astype(BF16)
    pack(keep_ref, send_ref, 2 * cols, dots, loss)


def pack(keep_ref, send_ref, at, dots, loss):
    zeros = jnp.zeros((EXTRA - 2, dots.shape[1]), F32)
    keep_ref[at : at + EXTRA] = jnp.concatenate([dots, loss, zeros], axis=0)
    terms = [t.astype(F32) for t in split3(dots) + split3(loss)]
    zeros = jnp.zeros((EXTRA - 6, dots.shape[1]), F32)
    send_ref[at : at + EXTRA] = jnp.concatenate(terms + [zeros], axis=0).astype(BF16)


def unpack(keep_ref, got_ref, at):
    kept = keep_ref[at : at + EXTRA]
    got = got_ref[at : at + EXTRA].astype(F32)
    dots = kept[0:1] + (got[0:1] + got[1:2] + got[2:3])
    loss = kept[1:2] + (got[3:4] + got[4:5] + got[5:6])
    return dots, loss


def middle_kernel(at_ref, keep_ref, got_ref, keep2_ref, send2_ref):
    cols = keep2_ref.shape[0] - EXTRA
    dots, loss = unpack(keep_ref, got_ref, 2 * cols)
    zl = at_ref[6]
    mine = pl.multiple_of(zl * cols, 16)
    other = pl.multiple_of((1 - zl) * cols, 16)
    keep2_ref[:cols] = keep_ref[pl.ds(mine, cols), :] + got_ref[pl.ds(mine, cols), :].astype(F32)
    send2_ref[:cols] = (
        keep_ref[pl.ds(other, cols), :] + got_ref[pl.ds(other, cols), :].astype(F32)
    ).astype(BF16)
    pack(keep2_ref, send2_ref, cols, dots, loss)


def head_kernel(at_loss, keep_ref, got_ref, unit_ref, inv_ref, feats_ref, flat_ref, *dir_refs):
    cols = keep_ref.shape[0] - EXTRA
    dots, loss = unpack(keep_ref, got_ref, cols)
    total = keep_ref[:cols] + got_ref[:cols].astype(F32)
    back = ((total - unit_ref[...] * dots) * inv_ref[...]).astype(BF16)
    head = jnp.dot(back, feats_ref[...], preferred_element_type=F32).astype(BF16)
    tiles = feats_ref.shape[1] // LANES
    for k in range(tiles):
        flat_ref[k * cols : (k + 1) * cols] = head[:, k * LANES : (k + 1) * LANES]
    part = loss[:, :LANES]
    for k in range(1, loss.shape[1] // LANES):
        part = part + loss[:, k * LANES : (k + 1) * LANES]
    terms = [t.astype(F32) for t in split3(part)]
    tail = jnp.concatenate(terms + [jnp.zeros((EXTRA - 3, LANES), F32)], axis=0)
    end = tiles * cols
    flat_ref[end:at_loss] = jnp.zeros((at_loss - end, LANES), BF16)
    flat_ref[at_loss : at_loss + EXTRA] = tail.astype(BF16)
    flat_ref[at_loss + EXTRA :] = jnp.zeros((flat_ref.shape[0] - at_loss - EXTRA, LANES), BF16)
    low = total.astype(BF16)
    terms = [t.astype(F32) for t in split3(dots)]
    lines = jnp.concatenate(terms + [jnp.zeros((EXTRA - 3, dots.shape[1]), F32)], axis=0).astype(BF16)
    rows = dir_refs[0].shape[1]
    for k, ref in enumerate(dir_refs):
        ref[:cols] = low[:, k * rows : (k + 1) * rows]
        ref[cols:] = lines[:, k * rows : (k + 1) * rows]


def back_kernel(unit_ref, inv_ref, *refs):
    out_ref = refs[-1]
    cols, rows = unit_ref.shape
    total = refs[0][...].astype(F32)
    for ref in refs[1:-1]:
        total = total + ref[...].astype(F32)
    dots = total[cols : cols + 1] + total[cols + 1 : cols + 2] + total[cols + 2 : cols + 3]
    out_ref[...] = ((total[:cols] - unit_ref[...] * dots) * inv_ref[:, :rows]).astype(BF16)


def to_low(at_ref, total):
    first = total[:EXTRA]
    terms = [t.astype(F32) for t in split3(first[0:1] + first[1:2] + first[2:3])]
    row = jnp.concatenate(terms + [jnp.zeros((EXTRA - 3, LANES), F32)], axis=0)
    return jnp.where(at_ref[7] > 0, row, first).astype(BF16), total[EXTRA:].astype(BF16)


def sum_kernel(at_ref, parts_ref, *refs):
    out_ref = refs[-1]
    first, rest = to_low(at_ref, jnp.sum(parts_ref[...].astype(F32), axis=0))
    for k in range(out_ref.shape[0]):
        out_ref[k, :EXTRA] = first
        out_ref[k, EXTRA:] = rest


def feat_kernel(at_ref, weight_ref, *refs):
    out_ref, back_ref = refs[-2:]
    cols = refs[0].shape[0]
    for d, ref in enumerate(refs[:-2]):
        back_ref[pl.ds(pl.multiple_of(at_ref[8 + d] * cols, 16), cols), :] = ref[...]
    out_ref[...] = lax.dot_general(
        back_ref[...], weight_ref[...], (((0,), (1,)), ((), ())), preferred_element_type=F32
    ).astype(BF16)


def final_kernel(at_loss, pairs, full_ref, head_ref, loss_ref):
    cols, width = head_ref.shape
    tiles = width // LANES
    for k in range(tiles):
        head_ref[:, k * LANES : (k + 1) * LANES] = full_ref[k * cols : (k + 1) * cols]
    total = jnp.sum(full_ref[at_loss : at_loss + EXTRA].astype(F32), axis=0, keepdims=True)
    loss_ref[...] = jnp.sum(total, axis=1, keepdims=True) / pairs


def shift_by(x, axis, step):
    n = lax.axis_size(axis)
    return lax.ppermute(x, axis, [(k, (k + step) % n) for k in range(n)])


def local(img_feat, head_weight, text_embed, log_temp, logit_bias):
    rows, width = img_feat.shape
    quarter = text_embed.shape[0]
    ny, nx, nzh, nzl, nc = (lax.axis_size(a) for a in ("y", "x", "zh", "zl", "c"))
    nrep = nzl * nc
    plane = nx * ny
    cols = width // nrep
    images = nzh * rows
    tiles = width // LANES
    y_at, x_at, zl_at, c_at = (lax.axis_index(a) for a in ("y", "x", "zl", "c"))
    rep_at = zl_at * nc + c_at
    piece = -(-(tiles * cols) // (plane * 8)) * 8
    at_loss = -(-(tiles * cols) // piece) * piece
    assert at_loss < plane * piece
    at = jnp.stack(
        [
            rep_at,
            0 * rep_at,
            y_at * quarter,
            rep_at * quarter,
            quarter + 0 * rep_at,
            c_at,
            zl_at,
            (y_at * nx + x_at == at_loss // piece).astype(jnp.int32),
        ]
        + [rep_at ^ d for d in range(nrep)]
    ).astype(jnp.int32)
    par = jnp.stack([jnp.exp(log_temp[0]), logit_bias[0]])

    copies = call(text_kernel, shape((ny * quarter, width), BF16), text_embed)
    part = rows // nc
    def place(z, low, core):
        return (z % nzh * nzl + low) * nc + core

    near = []
    cross = []
    for z in range(nzh):
        near += [(place(z, 1, k), place(z + 1, k, 0)) for k in range(nc)]
        near += [(place(z, 0, k), place(z - 1, k, 1)) for k in range(nc)]
        cross += [(place(z, 1, k), place(z + 2, 0, k)) for k in range(nc)]
        cross += [(place(z, 0, k), place(z - 2, 1, k)) for k in range(nc)]
    half_rows = lax.dynamic_slice_in_dim(img_feat, c_at * part, part, 0)
    line = ("zh", "zl", "c")
    across = lax.ppermute(half_rows, line, cross)
    beside = lax.ppermute(img_feat, line, near)
    fetched = jnp.concatenate([beside, across], axis=0)
    own = to_all(copies, "y")
    far = shift_by(own, "x", 2)
    left = shift_by(own, "x", 1)
    right = shift_by(own, "x", -1)
    swapped = lax.ppermute(fetched, "c", [(0, 1), (1, 0)])

    unit, low, inv, own_unit, col_unit, feats = call(
        image_kernel,
        [
            shape((width, images), F32),
            shape((width, images), BF16),
            shape((1, images), F32),
            shape((cols, rows), F32),
            shape((cols, images), F32),
            shape((images, width), BF16),
        ],
        at,
        head_weight.T,
        img_feat,
        fetched,
        swapped,
        smem=1,
        flops=2 * width,
    )
    acc, loss_row = call(
        first_kernel,
        [shape((width, images), F32), shape((1, images), F32)],
        at,
        par,
        own,
        left,
        low,
        smem=2,
        flops=8 * width * images * own.shape[0],
    )
    keep, send = call(
        second_kernel,
        [shape((2 * cols + EXTRA, images), F32), shape((2 * cols + EXTRA, images), BF16)],
        at,
        par,
        right,
        far,
        low,
        unit,
        acc,
        loss_row,
        smem=2,
        flops=8 * width * images * own.shape[0],
        scratch_shapes=[pltpu.VMEM((width, images), F32)],
    )
    got = lax.ppermute(send, "c", [(0, 1), (1, 0)])
    keep2, send2 = call(
        middle_kernel,
        [shape((cols + EXTRA, images), F32), shape((cols + EXTRA, images), BF16)],
        at,
        keep,
        got,
        smem=1,
    )
    got2 = lax.ppermute(send2, "zl", [(0, 1), (1, 0)])
    flat, *dirs = call(
        functools.partial(head_kernel, at_loss),
        [shape((plane * piece, LANES), BF16)] + [shape((cols + EXTRA, rows), BF16)] * nzh,
        keep2,
        got2,
        col_unit,
        inv,
        feats,
        flops=2 * cols * images * width,
    )

    dirs = [dirs[0]] + [shift_by(dirs[s], "zh", -s) for s in range(1, nzh)]
    back = call(back_kernel, shape((cols, rows), BF16), own_unit, inv, *dirs)

    parts = to_all(flat, ("y", "x")).reshape(plane, piece, LANES)
    part = pl.pallas_call(
        sum_kernel,
        out_shape=shape((nzh, piece, LANES), BF16),
        in_specs=[SMEM, VMEM, pl.BlockSpec(memory_space=pl.ANY)],
        out_specs=VMEM,
    )(at, parts, back)
    part = to_all(part, "zh")
    low_part = call(sum_kernel, shape((plane, piece, LANES), BF16), at, part, smem=1)
    full = to_all(low_part.reshape(plane * piece, LANES), ("y", "x"))
    group = rows * plane * nzh
    head_grad, loss = call(
        functools.partial(final_kernel, at_loss, float(group) * float(group)),
        [shape((cols, width), BF16), shape((1, 1), F32)],
        full,
    )

    backs = [back]
    for d in range(1, nrep):
        backs.append(lax.ppermute(back, ("zl", "c"), [(k, k ^ d) for k in range(nrep)]))
    feat_grad = call(
        feat_kernel,
        shape((rows, width), BF16),
        at,
        head_weight,
        *backs,
        smem=1,
        flops=2 * rows * width * width,
        scratch_shapes=[pltpu.VMEM((width, rows), BF16)],
    )
    return (loss.reshape(1), feat_grad, head_grad.T)


def solution(mesh):
    devices = mesh.devices.reshape(8, 4, 4, 2, 2)
    fine = Mesh(devices, ("y", "x", "zh", "zl", "c"))
    batch, rep = (("y", "x", "zh"), ("zl", "c"))
    in_specs = (P(batch, None), P(), P(batch + rep, None), P(), P())
    out_specs = (P(), P(batch, None), P(None, rep))
    return jax.shard_map(local, mesh=fine, in_specs=in_specs, out_specs=out_specs, check_vma=False)
```
